256 devices in a mesh: seq: 32 (over z_lo, x, core), ch: 8 (over z_hi, y).
Axes of the slice: x: 4, y: 4, z: 8 (z_hi: 2, z_lo: 4; z = z_hi * 4 + z_lo), core: 2. Of those that a mesh axis runs over, the one named last changes fastest.
Arguments:
- queries: bfloat16 [16384, 4096], P('seq', 'ch'), may hold values from -6 to 6
- keys: bfloat16 [16384, 4096], P('seq', 'ch'), may hold values from -6 to 6
- values: bfloat16 [16384, 4096], P('seq', 'ch'), may hold values from -6 to 6
- filters: bfloat16 [16384, 4096], P('seq', 'ch'), may hold values from -2 to 2
- short_weights: float32 [3, 3, 4096], P(None, None, 'ch'), may hold values from -3 to 3
- skip_gain: float32 [4096], P('ch'), may hold values from -4 to 4
- stream: bfloat16 [16384, 4096], P('seq', 'ch'), may hold values from -25 to 25
- norm_gain: float32 [4096], P('ch'), may hold values from 0.25 to 1.75
Outputs:
- stream_out: bfloat16 [16384, 4096], P('seq', 'ch')
- normed: bfloat16 [16384, 4096], P('seq', 'ch')
The draws below stay inside these ranges and needn't reach their ends.
All inputs are finite; a program needn't handle non-finite values.
Results may differ from the reference program's by a relative error of at most 0.014.
Values may be sent and summed in bfloat16 or wider, within the bound.
No kernel may reach another device: no remote copies, remote signals or barrier semaphores. Data moves between devices by JAX's collectives and lax.ppermute only.
A program may use at most 64 MiB of HBM per device.

```python
import math
import jax
import jax.numpy as jnp
from jax import lax

D = 4096
TOKENS = 16384


def draw_filters(key, part):
    key = jax.random.fold_in(key, 11)
    key_life, key_rough = jax.random.split(key, 2)
    position = jnp.arange(TOKENS, dtype=jnp.float32)[:, None]
    life = jnp.exp(jax.random.uniform(key_life, (D,), jnp.float32, math.log(16.0), math.log(2.0 * TOKENS)))
    rough = jax.random.truncated_normal(key_rough, -5.0, 5.0, (TOKENS, D), jnp.float32)
    rate = 1.0 / life
    shaped = rough * jnp.sqrt(2.0 * rate)[None, :] * jnp.exp(-rate[None, :] * position)
    return shaped.astype(jnp.bfloat16)


def draw_stream(key, part):
    key = jax.random.fold_in(key, 23)
    key_rows, key_base = jax.random.split(key, 2)
    channel = jnp.arange(D, dtype=jnp.float32) / D
    rows = jnp.exp(jax.random.uniform(key_rows, (TOKENS, 1), jnp.float32, math.log(0.4), math.log(4.0)))
    column = 0.5 * jnp.exp(math.log(3.0) * channel)
    base = jax.random.truncated_normal(key_base, -4.0, 4.0, (TOKENS, D), jnp.float32)
    return (base * rows * column[None, :]).astype(jnp.bfloat16)


def block_scale(key, shape, cuts, least, high):
    def one(axis_at, parts):
        heights = jax.random.uniform(jax.random.fold_in(jax.random.fold_in(key, 6), axis_at), (parts,), jnp.float32, least / len(cuts), high / len(cuts))
        return jnp.repeat(jnp.exp(heights), shape[axis_at] // parts).reshape((-1,) + (1,) * (len(shape) - axis_at - 1))

    factor_of = one(*cuts[0])
    for cut in cuts[1:]:
        factor_of = factor_of * one(*cut)
    return factor_of


def scatter_about(own_key, shape, deviation, most, cuts=(), kind=jnp.bfloat16):
    entries = jax.random.normal(own_key, shape, jnp.float32) * deviation
    if len(cuts) > 0:
        entries = block_scale(own_key, shape, cuts, -0.22, 0.18) * entries
    return jnp.clip(entries, min=-most, max=most).astype(kind)


def setup_inputs(seed: int = 0) -> dict:
    key_list = jax.random.split(jax.random.key(seed), 9)
    return {
        "queries": scatter_about(key_list[0], (TOKENS, D), 1.0, 6.0, ((0, 32), (1, 8))),
        "keys": scatter_about(key_list[1], (TOKENS, D), 1.0, 6.0, ((0, 32), (1, 8))),
        "values": scatter_about(key_list[2], (TOKENS, D), 1.0, 6.0, ((0, 32), (1, 8))),
        "filters": draw_filters(jax.random.fold_in(key_list[8], 71), 0),
        "short_weights": scatter_about(key_list[4], (3, 3, D), 0.6, 3.0, ((2, 8),), jnp.float32),
        "skip_gain": scatter_about(key_list[5], (D,), 1.0, 4.0, ((0, 8),), jnp.float32),
        "stream": draw_stream(jax.random.fold_in(key_list[8], 71), 0),
        "norm_gain": jnp.clip(1.0 + 0.15 * jax.random.normal(key_list[7], (D,), jnp.float32), 0.25, 1.75),
    }


def short_filter(branch, taps):
    first = jnp.pad(branch, ((1, 0), (0, 0)))[:-1]
    second = jnp.pad(branch, ((2, 0), (0, 0)))[:-2]
    return taps[0] * branch + taps[1] * first + taps[2] * second

def long_conv(product, filters):
    length = product.shape[0]
    groups = D // 256
    left = product.reshape(length, groups, 256).transpose(1, 0, 2)
    right = filters.reshape(length, groups, 256).transpose(1, 0, 2)

    def one_group(pair):
        signal_block, filter_block = pair
        spec_a = jnp.fft.rfft(signal_block, n=2 * length, axis=0)
        spec_b = jnp.fft.rfft(filter_block, n=2 * length, axis=0)
        return jnp.fft.irfft(spec_a * spec_b, n=2 * length, axis=0)[:length]
    result = lax.map(one_group, (left, right))
    return result.transpose(1, 0, 2).reshape(length, D)

def reference(queries, keys, values, filters, short_weights, skip_gain, stream, norm_gain):
    qf = short_filter(queries.astype(jnp.float32), short_weights[0]).astype(jnp.bfloat16)
    kf = short_filter(keys.astype(jnp.float32), short_weights[1])
    vf = short_filter(values.astype(jnp.float32), short_weights[2])
    u_low = lax.optimization_barrier((kf * vf).astype(jnp.bfloat16))
    u_wide = u_low.astype(jnp.float32)
    conv = long_conv(u_wide, filters.astype(jnp.float32))
    y_low = lax.optimization_barrier((conv + skip_gain[None, :] * u_wide).astype(jnp.bfloat16))
    q_wide = lax.optimization_barrier(qf).astype(jnp.float32)
    gated = lax.optimization_barrier((q_wide * y_low.astype(jnp.float32)).astype(jnp.bfloat16))
    summed = stream.astype(jnp.float32) + gated.astype(jnp.float32)
    stream_out = summed.astype(jnp.bfloat16)
    rms = jnp.sqrt(lax.optimization_barrier(jnp.mean(summed * summed, axis=1)) + 1e-05)
    normed = (summed / rms[:, None] * norm_gain[None, :]).astype(jnp.bfloat16)
    return (stream_out, normed)
```

```python
import jax
import jax.numpy as jnp
import numpy as np
from jax import lax
from jax.experimental import pallas as pl
from jax.experimental.pallas import tpu as pltpu
from jax.sharding import PartitionSpec as P

LANE = 128
EDGE = 16
GROUP = 4
VMEM_LIMIT = 48 * 1024 * 1024


def params():
    return pltpu.CompilerParams(vmem_limit_bytes=VMEM_LIMIT)


def tables():
    n = LANE * LANE
    a = np.arange(LANE, dtype=np.float64)
    first = -2.0 * np.pi * np.outer(a + 0.25, a) / LANE
    twist = -2.0 * np.pi * np.outer(a + 0.25, a) / n
    second = -2.0 * np.pi * np.outer(a, a) / LANE
    t1 = np.concatenate([np.cos(first), np.sin(first)], 0)
    cos2, sin2 = np.cos(second), np.sin(second)
    t2 = np.block([[cos2, sin2], [-sin2, cos2]])
    t2_inv = np.block([[cos2, -sin2], [sin2, cos2]])
    t1_inv = np.concatenate([np.cos(first).T, np.sin(first).T], 1) / n
    low = [jnp.asarray(t, jnp.bfloat16) for t in (t1, t2, t2_inv, t1_inv)]
    return (*low, jnp.asarray(np.cos(twist), jnp.float32), jnp.asarray(np.sin(twist), jnp.float32))


def edges_kernel(q_ref, k_ref, v_ref, out_ref):
    out_ref[0] = q_ref[...]
    out_ref[1] = k_ref[...]
    out_ref[2] = v_ref[...]


def last_rows(q, k, v):
    rows, width = q.shape
    spec = pl.BlockSpec((EDGE, width), lambda i: (rows // EDGE - 1, 0))
    return pl.pallas_call(
        edges_kernel,
        grid=(1,),
        in_specs=[spec] * 3,
        out_specs=pl.BlockSpec((3, EDGE, width), lambda i: (0, 0, 0)),
        out_shape=jax.ShapeDtypeStruct((3, EDGE, width), q.dtype),
        compiler_params=params(),
    )(q, k, v)


def put_turned(out_ref, j, block):
    depth = out_ref.shape[2]
    per = LANE // depth
    for g in range(block.shape[1] // LANE):
        turned = block[:, g * LANE : (g + 1) * LANE].T
        out_ref[g * per : (g + 1) * per, j] = turned.reshape(per, depth, LANE).astype(out_ref.dtype)


def turn_kernel(x_ref, out_ref):
    for j in range(out_ref.shape[1]):
        put_turned(out_ref, j, x_ref[j * LANE : (j + 1) * LANE, :].astype(jnp.float32))


def split_shape(x, groups):
    rows, width = x.shape
    return jax.ShapeDtypeStruct((groups, rows // LANE, width // groups, LANE), x.dtype)


def turn(x, groups):
    return pl.pallas_call(
        turn_kernel, out_shape=split_shape(x, groups), compiler_params=params()
    )(x)


def extend(ext_ref, x_ref, edge):
    rows = x_ref.shape[0]
    ext_ref[0:8, :] = edge[EDGE - 8 :, :].astype(jnp.float32)
    ext_ref[8 : 8 + rows, :] = x_ref[...].astype(jnp.float32)


def taps_of(ext_ref, taps, start, size):
    return (
        taps[0:1, :] * ext_ref[start + 8 : start + 8 + size, :]
        + taps[1:2, :] * ext_ref[start + 7 : start + 7 + size, :]
        + taps[2:3, :] * ext_ref[start + 6 : start + 6 + size, :]
    )


def product_kernel(k_ref, v_ref, edge_ref, taps_ref, out_ref, k_ext, v_ext):
    extend(k_ext, k_ref, edge_ref[1])
    extend(v_ext, v_ref, edge_ref[2])
    for j in range(out_ref.shape[1]):
        kf = taps_of(k_ext, taps_ref[1], j * LANE, LANE)
        vf = taps_of(v_ext, taps_ref[2], j * LANE, LANE)
        put_turned(out_ref, j, kf * vf)


def product(k, v, edge, taps, groups):
    rows, width = k.shape
    ext = pltpu.VMEM((rows + 8, width), jnp.float32)
    return pl.pallas_call(
        product_kernel,
        out_shape=split_shape(k, groups),
        scratch_shapes=[ext, ext],
        compiler_params=params(),
    )(k, v, edge, taps)


def gate_kernel(q_ref, edge_ref, taps_ref, out_ref, q_ext):
    extend(q_ext, q_ref, edge_ref[0])
    for j in range(out_ref.shape[0] // LANE):
        qf = taps_of(q_ext, taps_ref[0], j * LANE, LANE)
        out_ref[j * LANE : (j + 1) * LANE, :] = qf.astype(out_ref.dtype)


def gate(q, edge, taps):
    rows, width = q.shape
    return pl.pallas_call(
        gate_kernel,
        out_shape=jax.ShapeDtypeStruct(q.shape, q.dtype),
        scratch_shapes=[pltpu.VMEM((rows + 8, width), jnp.float32)],
        compiler_params=params(),
    )(q, edge, taps)


def mix(table, data):
    return jnp.dot(table, data, preferred_element_type=jnp.float32)


def conv_kernel(u_ref, f_ref, skip_ref, t1, t2, t2_inv, t1_inv, tw_c, tw_s, y_ref, u_wide, f_wide, y_wide):
    depth = skip_ref.shape[0]
    u_wide[...] = u_ref[...].astype(jnp.float32)
    f_wide[...] = f_ref[...].astype(jnp.float32)
    low = jnp.bfloat16

    def part(x, i):
        return x[:, i * LANE : (i + 1) * LANE]

    for start in range(0, depth, GROUP):
        chans = range(start, start + GROUP)
        rows = [pl.ds(c, LANE, stride=depth) for c in chans]
        data = [u_wide[r, :].astype(low) for r in rows] + [f_wide[r, :].astype(low) for r in rows]
        first = mix(t1[...], jnp.concatenate(data, 1))
        turned = []
        for i in range(2 * GROUP):
            re, im = part(first[:LANE], i), part(first[LANE:], i)
            c, s = tw_c[...], tw_s[...]
            turned.append(jnp.concatenate([re * c - im * s, re * s + im * c], 1).astype(low))
        spec = mix(jnp.concatenate(turned, 0), t2[...])
        prod = []
        for i in range(GROUP):
            a = spec[i * LANE : (i + 1) * LANE]
            b = spec[(GROUP + i) * LANE : (GROUP + i + 1) * LANE]
            ar, ai, br, bi = a[:, :LANE], a[:, LANE:], b[:, :LANE], b[:, LANE:]
            prod.append(jnp.concatenate([ar * br - ai * bi, ar * bi + ai * br], 1).astype(low))
        back = mix(jnp.concatenate(prod, 0), t2_inv[...])
        cols = []
        for i in range(GROUP):
            v = back[i * LANE : (i + 1) * LANE]
            re, im = v[:, :LANE], v[:, LANE:]
            c, s = tw_c[...], tw_s[...]
            cols.append(jnp.concatenate([re * c + im * s, im * c - re * s], 0).astype(low))
        conv = mix(t1_inv[...], jnp.concatenate(cols, 1))
        for i, r in enumerate(rows):
            y_wide[r, :] = part(conv, i)
    shape = (LANE, depth, LANE)
    y = y_wide[...].reshape(shape) + skip_ref[...][None] * u_wide[...].reshape(shape)
    y_ref[...] = y.reshape(y_ref.shape).astype(y_ref.dtype)


def long_conv(u, f, skip):
    wide = pltpu.VMEM(u.shape, jnp.float32)
    return pl.pallas_call(
        conv_kernel,
        out_shape=jax.ShapeDtypeStruct(u.shape, u.dtype),
        scratch_shapes=[wide] * 3,
        compiler_params=params(),
    )(u, f, skip, *tables())


def join_kernel(y_ref, qf_ref, stream_ref, out_ref, sum_ref, sq_ref):
    groups, slabs, depth, _ = y_ref.shape
    per = LANE // depth
    sq_ref[...] = jnp.zeros_like(sq_ref)
    for j in range(slabs):
        rows = slice(j * LANE, (j + 1) * LANE)
        squares = jnp.zeros((LANE, LANE), jnp.float32)
        for g in range(groups // per):
            cols = slice(g * LANE, (g + 1) * LANE)
            y = y_ref[g * per : (g + 1) * per, j].reshape(LANE, LANE).astype(jnp.float32).T
            gated = (qf_ref[rows, cols].astype(jnp.float32) * y).astype(jnp.bfloat16)
            summed = stream_ref[rows, cols].astype(jnp.float32) + gated.astype(jnp.float32)
            out_ref[rows, cols] = summed.astype(out_ref.dtype)
            sum_ref[rows, cols] = summed
            squares = squares + summed * summed
        total = jnp.sum(squares.T, axis=0, keepdims=True)
        for d in range(sq_ref.shape[0]):
            sq_ref[d, j : j + 1, :] = total


def join(y, qf, stream, fan):
    return pl.pallas_call(
        join_kernel,
        out_shape=(
            jax.ShapeDtypeStruct(stream.shape, stream.dtype),
            jax.ShapeDtypeStruct(stream.shape, jnp.float32),
            jax.ShapeDtypeStruct((fan, 8, LANE), jnp.float32),
        ),
        compiler_params=params(),
    )(y, qf, stream)


def norm_kernel(channels, sum_ref, sq_ref, gain_ref, out_ref):
    squares = jnp.sum(sq_ref[...], axis=0)
    scale = 1.0 / jnp.sqrt(squares / channels + 1e-05)
    for j in range(out_ref.shape[0] // LANE):
        rows = slice(j * LANE, (j + 1) * LANE)
        column = jnp.broadcast_to(scale[j : j + 1, :], (LANE, LANE)).T
        for g in range(out_ref.shape[1] // LANE):
            cols = slice(g * LANE, (g + 1) * LANE)
            out_ref[rows, cols] = (sum_ref[rows, cols] * column * gain_ref[:, cols]).astype(out_ref.dtype)


def norm(summed, squares, gain):
    channels = summed.shape[1] * squares.shape[0]

    def kernel(*refs):
        norm_kernel(channels, *refs)

    return pl.pallas_call(
        kernel,
        out_shape=jax.ShapeDtypeStruct(summed.shape, jnp.bfloat16),
        compiler_params=params(),
    )(summed, squares, gain[None, :])


def exchange(x, axis):
    return lax.all_to_all(x, axis, split_axis=0, concat_axis=0, tiled=True)


def shards(queries, keys, values, filters, short_weights, skip_gain, stream, norm_gain):
    groups = lax.axis_size("seq")
    fan = lax.axis_size("ch")
    rows, width = queries.shape
    slab = width // groups
    edge = last_rows(queries, keys, values)
    edge = lax.ppermute(edge, "seq", [(i, i + 1) for i in range(groups - 1)])
    f_all = exchange(turn(filters, groups), "seq")
    u_all = exchange(product(keys, values, edge, short_weights, groups), "seq")
    qf = gate(queries, edge, short_weights)
    skip = lax.dynamic_slice_in_dim(skip_gain, lax.axis_index("seq") * slab, slab, 0)
    skip = jnp.broadcast_to(skip[:, None], (slab, LANE))
    flat = (groups * rows // LANE * slab, LANE)
    y = long_conv(u_all.reshape(flat), f_all.reshape(flat), skip)
    y_home = exchange(y.reshape(u_all.shape), "seq")
    stream_out, summed, squares = join(y_home, qf, stream, fan)
    normed = norm(summed, exchange(squares, "ch"), norm_gain)
    return (stream_out, normed)


def solution(mesh):
    wide = P("seq", "ch")
    in_specs = (wide, wide, wide, wide, P(None, None, "ch"), P("ch"), wide, P("ch"))
    return jax.shard_map(shards, mesh=mesh, in_specs=in_specs, out_specs=(wide, wide), check_vma=False)
```

```python
import jax
import jax.numpy as jnp
import numpy as np
from jax import lax
from jax.experimental import pallas as pl
from jax.experimental.pallas import tpu as pltpu
from jax.sharding import PartitionSpec as P

LANE = 128
EDGE = 16
GROUP = 4
Z_SIZE = 4
X_SIZE = 4
VMEM_LIMIT = 48 * 1024 * 1024


def params(limit=VMEM_LIMIT):
    return pltpu.CompilerParams(vmem_limit_bytes=limit)


def cost(micros):
    return pl.CostEstimate(flops=int(micros * 1e9), bytes_accessed=0, transcendentals=0)


def tables():
    n = LANE * LANE
    a = np.arange(LANE, dtype=np.float64)
    first = -2.0 * np.pi * np.outer(a + 0.25, a) / LANE
    twist = -2.0 * np.pi * np.outer(a + 0.25, a) / n
    second = -2.0 * np.pi * np.outer(a, a) / LANE
    t1 = np.concatenate([np.cos(first), np.sin(first)], 0)
    cos2, sin2 = np.cos(second), np.sin(second)
    t2 = np.block([[cos2, sin2], [-sin2, cos2]])
    t2_inv = np.block([[cos2, -sin2], [sin2, cos2]])
    t1_inv = np.concatenate([np.cos(first).T, np.sin(first).T], 1) / n
    low = [jnp.asarray(t, jnp.bfloat16) for t in (t1, t2, t2_inv, t1_inv)]
    return (*low, jnp.asarray(np.cos(twist), jnp.float32), jnp.asarray(np.sin(twist), jnp.float32))


def edges_kernel(q_ref, k_ref, v_ref, out_ref, sems):
    rows = q_ref.shape[0]
    copies = [
        pltpu.make_async_copy(ref.at[pl.ds(rows - EDGE, EDGE), :], out_ref.at[i], sems.at[i])
        for i, ref in enumerate((q_ref, k_ref, v_ref))
    ]
    for copy in copies:
        copy.start()
    for copy in copies:
        copy.wait()


def last_rows(q, k, v):
    return pl.pallas_call(
        edges_kernel,
        in_specs=[pl.BlockSpec(memory_space=pl.ANY)] * 3,
        out_shape=jax.ShapeDtypeStruct((3, EDGE, q.shape[1]), q.dtype),
        scratch_shapes=[pltpu.SemaphoreType.DMA((3,))],
        compiler_params=params(60 * 1024 * 1024),
    )(q, k, v)


def put_turned(out_ref, j, block):
    depth = out_ref.shape[2]
    per = LANE // depth
    for g in range(block.shape[1] // LANE):
        turned = block[:, g * LANE : (g + 1) * LANE].T
        out_ref[g * per : (g + 1) * per, j] = turned.reshape(per, depth, LANE).astype(out_ref.dtype)


def place():
    me = lax.axis_index("seq")
    return me // (X_SIZE * 2), me // 2 % X_SIZE, me % 2


def turn_kernel(x_ref, after_ref, *outs):
    z, x, c = place()
    depth = outs[0].shape[3]
    for kz, out_ref in enumerate(outs):
        g = (z + kz) % Z_SIZE
        for j in range(out_ref.shape[2]):
            block = x_ref[j * LANE : (j + 1) * LANE, pl.ds(pl.multiple_of(g * LANE, LANE), LANE)]
            turned = block.astype(jnp.float32).T.astype(out_ref.dtype)
            for d in range(X_SIZE * 2):
                tile = turned[d * depth : (d + 1) * depth]
                out_ref[(d // 2 - x + X_SIZE) % X_SIZE, (d % 2 - c + 2) % 2, j] = tile


def split_shape(x, groups):
    rows, width = x.shape
    return jax.ShapeDtypeStruct((groups, rows // LANE, width // groups, LANE), x.dtype)


def turn(x, after, groups):
    rows, width = x.shape
    shape = jax.ShapeDtypeStruct((X_SIZE, 2, rows // LANE, width // groups, LANE), x.dtype)
    return pl.pallas_call(
        turn_kernel,
        in_specs=[pl.BlockSpec(memory_space=pltpu.VMEM), pl.BlockSpec(memory_space=pl.ANY)],
        out_shape=(shape,) * Z_SIZE,
        cost_estimate=cost(10),
        compiler_params=params(),
    )(x, after)


def pack_kernel(*refs):
    ins, outs = refs[:Z_SIZE], refs[Z_SIZE:]
    for d, out_ref in enumerate(outs):
        for kz, in_ref in enumerate(ins):
            out_ref[kz] = in_ref[d // 2, d % 2]


def pack(parts):
    shape = jax.ShapeDtypeStruct((Z_SIZE, *parts[0].shape[2:]), parts[0].dtype)
    return pl.pallas_call(
        pack_kernel, out_shape=(shape,) * (X_SIZE * 2), cost_estimate=cost(20), compiler_params=params()
    )(*parts)


def shift(block, dz, dx, dc):
    route = []
    for z in range(Z_SIZE):
        for x in range(X_SIZE):
            for c in range(2):
                to = ((z + dz) % Z_SIZE * X_SIZE + (x + dx) % X_SIZE) * 2 + (c + dc) % 2
                route.append(((z * X_SIZE + x) * 2 + c, to))
    return lax.ppermute(block, "seq", route)


def spread(x, after, groups):
    parts = turn(x, after, groups)
    parts = [parts[0]] + [shift(parts[k], k, 0, 0) for k in range(1, Z_SIZE)]
    parts = pack(parts)
    return [parts[0]] + [shift(parts[d], 0, d // 2, d % 2) for d in range(1, X_SIZE * 2)]


def extend(ext_ref, x_ref, edge):
    rows = x_ref.shape[0]
    ext_ref[0:8, :] = edge[EDGE - 8 :, :].astype(jnp.float32)
    ext_ref[8 : 8 + rows, :] = x_ref[...].astype(jnp.float32)


def taps_of(ext_ref, taps, start, size):
    return (
        taps[0:1, :] * ext_ref[start + 8 : start + 8 + size, :]
        + taps[1:2, :] * ext_ref[start + 7 : start + 7 + size, :]
        + taps[2:3, :] * ext_ref[start + 6 : start + 6 + size, :]
    )


def product_kernel(k_ref, v_ref, edge_ref, taps_ref, out_ref, k_ext, v_ext):
    extend(k_ext, k_ref, edge_ref[1])
    extend(v_ext, v_ref, edge_ref[2])
    for j in range(out_ref.shape[1]):
        kf = taps_of(k_ext, taps_ref[1], j * LANE, LANE)
        vf = taps_of(v_ext, taps_ref[2], j * LANE, LANE)
        put_turned(out_ref, j, kf * vf)


def product(k, v, edge, taps, groups):
    rows, width = k.shape
    ext = pltpu.VMEM((rows + 8, width), jnp.float32)
    return pl.pallas_call(
        product_kernel,
        out_shape=split_shape(k, groups),
        scratch_shapes=[ext, ext],
        cost_estimate=cost(20),
        compiler_params=params(),
    )(k, v, edge, taps)


def gate_kernel(q_ref, edge_ref, taps_ref, out_ref, q_ext):
    extend(q_ext, q_ref, edge_ref[0])
    for j in range(out_ref.shape[0] // LANE):
        qf = taps_of(q_ext, taps_ref[0], j * LANE, LANE)
        out_ref[j * LANE : (j + 1) * LANE, :] = qf.astype(out_ref.dtype)


def gate(q, edge, taps):
    rows, width = q.shape
    return pl.pallas_call(
        gate_kernel,
        out_shape=jax.ShapeDtypeStruct(q.shape, q.dtype),
        scratch_shapes=[pltpu.VMEM((rows + 8, width), jnp.float32)],
        compiler_params=params(),
    )(q, edge, taps)


def mix(table, data):
    return jnp.dot(table, data, preferred_element_type=jnp.float32)


def conv_kernel(u_ref, skip_ref, t1, t2, t2_inv, t1_inv, tw_c, tw_s, *rest):
    f_refs, (y_ref, u_wide, f_wide, y_wide) = rest[:-4], rest[-4:]
    depth = skip_ref.shape[0]
    u_wide[...] = u_ref[...].astype(jnp.float32)
    z, x, c = place()
    size = u_ref.shape[0] // (Z_SIZE * len(f_refs))
    for d, f_ref in enumerate(f_refs):
        for kz in range(Z_SIZE):
            src = ((z - kz + Z_SIZE) % Z_SIZE * X_SIZE + (x - d // 2 + X_SIZE) % X_SIZE) * 2 + (c + d) % 2
            row = pl.multiple_of(src * size, size)
            f_wide[pl.ds(row, size), :] = f_ref[kz].reshape(size, LANE).astype(jnp.float32)
    low = jnp.bfloat16

    def part(x, i):
        return x[:, i * LANE : (i + 1) * LANE]

    for start in range(0, depth, GROUP):
        chans = range(start, start + GROUP)
        rows = [pl.ds(c, LANE, stride=depth) for c in chans]
        data = [u_wide[r, :].astype(low) for r in rows] + [f_wide[r, :].astype(low) for r in rows]
        first = mix(t1[...], jnp.concatenate(data, 1))
        turned = []
        for i in range(2 * GROUP):
            re, im = part(first[:LANE], i), part(first[LANE:], i)
            c, s = tw_c[...], tw_s[...]
            turned.append(jnp.concatenate([re * c - im * s, re * s + im * c], 1).astype(low))
        spec = mix(jnp.concatenate(turned, 0), t2[...])
        prod = []
        for i in range(GROUP):
            a = spec[i * LANE : (i + 1) * LANE]
            b = spec[(GROUP + i) * LANE : (GROUP + i + 1) * LANE]
            ar, ai, br, bi = a[:, :LANE], a[:, LANE:], b[:, :LANE], b[:, LANE:]
            prod.append(jnp.concatenate([ar * br - ai * bi, ar * bi + ai * br], 1).astype(low))
        back = mix(jnp.concatenate(prod, 0), t2_inv[...])
        cols = []
        for i in range(GROUP):
            v = back[i * LANE : (i + 1) * LANE]
            re, im = v[:, :LANE], v[:, LANE:]
            c, s = tw_c[...], tw_s[...]
            cols.append(jnp.concatenate([re * c + im * s, im * c - re * s], 0).astype(low))
        conv = mix(t1_inv[...], jnp.concatenate(cols, 1))
        for i, r in enumerate(rows):
            y_wide[r, :] = part(conv, i)
    shape = (LANE, depth, LANE)
    y = y_wide[...].reshape(shape) + skip_ref[...][None] * u_wide[...].reshape(shape)
    y_ref[...] = y.reshape(y_ref.shape).astype(y_ref.dtype)


def long_conv(u, f, skip):
    wide = pltpu.VMEM(u.shape, jnp.float32)
    return pl.pallas_call(
        conv_kernel,
        out_shape=jax.ShapeDtypeStruct(u.shape, u.dtype),
        scratch_shapes=[wide] * 3,
        compiler_params=params(),
    )(u, skip, *tables(), *f)


def join_kernel(y_ref, qf_ref, stream_ref, gain_ref, out_ref, sum_ref, sq_ref):
    groups, slabs, depth, _ = y_ref.shape
    per = LANE // depth
    sq_ref[...] = jnp.zeros_like(sq_ref)
    for j in range(slabs):
        rows = slice(j * LANE, (j + 1) * LANE)
        squares = jnp.zeros((LANE, LANE), jnp.float32)
        for g in range(groups // per):
            cols = slice(g * LANE, (g + 1) * LANE)
            y = y_ref[g * per : (g + 1) * per, j].reshape(LANE, LANE).astype(jnp.float32).T
            gated = (qf_ref[rows, cols].astype(jnp.float32) * y).astype(jnp.bfloat16)
            summed = stream_ref[rows, cols].astype(jnp.float32) + gated.astype(jnp.float32)
            out_ref[rows, cols] = summed.astype(out_ref.dtype)
            sum_ref[rows, cols] = summed * gain_ref[:, cols]
            squares = squares + summed * summed
        total = jnp.sum(squares.T, axis=0, keepdims=True)
        for d in range(sq_ref.shape[0]):
            sq_ref[d, j : j + 1, :] = total


def join(y, qf, stream, gain, fan):
    return pl.pallas_call(
        join_kernel,
        out_shape=(
            jax.ShapeDtypeStruct(stream.shape, stream.dtype),
            jax.ShapeDtypeStruct(stream.shape, jnp.float32),
            jax.ShapeDtypeStruct((fan, 8, LANE), jnp.float32),
        ),
        compiler_params=params(),
    )(y, qf, stream, gain[None, :])


def norm_kernel(channels, sum_ref, sq_ref, out_ref):
    squares = jnp.sum(sq_ref[...], axis=0)
    scale = 1.0 / jnp.sqrt(squares / channels + 1e-05)
    for j in range(out_ref.shape[0] // LANE):
        rows = slice(j * LANE, (j + 1) * LANE)
        column = jnp.broadcast_to(scale[j : j + 1, :], (LANE, LANE)).T
        for g in range(out_ref.shape[1] // LANE):
            cols = slice(g * LANE, (g + 1) * LANE)
            out_ref[rows, cols] = (sum_ref[rows, cols] * column).astype(out_ref.dtype)


def norm(summed, squares):
    channels = summed.shape[1] * squares.shape[0]

    def kernel(*refs):
        norm_kernel(channels, *refs)

    return pl.pallas_call(
        kernel,
        out_shape=jax.ShapeDtypeStruct(summed.shape, jnp.bfloat16),
        compiler_params=params(),
    )(summed, squares)


def exchange(x, axis):
    return lax.all_to_all(x, axis, split_axis=0, concat_axis=0, tiled=True)


def shards(queries, keys, values, filters, short_weights, skip_gain, stream, norm_gain):
    groups = lax.axis_size("seq")
    fan = lax.axis_size("ch")
    rows, width = queries.shape
    slab = width // groups
    own_edge = last_rows(queries, keys, values)
    edge = lax.ppermute(own_edge, "seq", [(i, i + 1) for i in range(groups - 1)])
    f_all = spread(filters, own_edge, groups)
    u_all = exchange(product(keys, values, edge, short_weights, groups), "seq")
    qf = gate(queries, edge, short_weights)
    skip = lax.dynamic_slice_in_dim(skip_gain, lax.axis_index("seq") * slab, slab, 0)
    skip = jnp.broadcast_to(skip[:, None], (slab, LANE))
    flat = (groups * rows // LANE * slab, LANE)
    y = long_conv(u_all.reshape(flat), f_all, skip)
    y_home = exchange(y.reshape(u_all.shape), "seq")
    stream_out, summed, squares = join(y_home, qf, stream, norm_gain, fan)
    normed = norm(summed, exchange(squares, "ch"))
    return (stream_out, normed)


def solution(mesh):
    wide = P("seq", "ch")
    in_specs = (wide, wide, wide, wide, P(None, None, "ch"), P("ch"), wide, P("ch"))
    return jax.shard_map(shards, mesh=mesh, in_specs=in_specs, out_specs=(wide, wide), check_vma=False)
```

```python
import jax
import jax.numpy as jnp
import numpy as np
from jax import lax
from jax.experimental import pallas as pl
from jax.experimental.pallas import tpu as pltpu
from jax.sharding import PartitionSpec as P

LANE = 128
EDGE = 16
GROUP = 8
Z_SIZE = 4
X_SIZE = 4
AHEAD = 3
MIB = 1024 * 1024


def params(mebibytes):
    return pltpu.CompilerParams(vmem_limit_bytes=mebibytes * MIB)


def cost(micros):
    return pl.CostEstimate(flops=int(micros * 1e9), bytes_accessed=0, transcendentals=0)


def tables():
    n = LANE * LANE
    a = np.arange(LANE, dtype=np.float64)
    first = -2.0 * np.pi * np.outer(a + 0.25, a) / LANE
    twist = -2.0 * np.pi * np.outer(a + 0.25, a) / n
    second = -2.0 * np.pi * np.outer(a, a) / LANE
    t1 = np.concatenate([np.cos(first), np.sin(first)], 0)
    cos2, sin2 = np.cos(second), np.sin(second)
    t2 = np.block([[cos2, sin2], [-sin2, cos2]])
    t2_inv = np.block([[cos2, -sin2], [sin2, cos2]])
    t1_inv = np.concatenate([np.cos(first).T, np.sin(first).T], 1) / n
    low = [jnp.asarray(t, jnp.bfloat16) for t in (t1, t2, t2_inv, t1_inv)]
    return (*low, jnp.asarray(np.cos(twist), jnp.float32), jnp.asarray(np.sin(twist), jnp.float32))


def place():
    me = lax.axis_index("seq")
    return me // (X_SIZE * 2), me // 2 % X_SIZE, me % 2


HBM = pl.BlockSpec(memory_space=pl.ANY)
VMEM = pl.BlockSpec(memory_space=pltpu.VMEM)


def send(source, target, sem):
    copy = pltpu.make_async_copy(source, target, sem)
    copy.start()
    return copy


def wait_all(copies):
    for copy in copies:
        copy.wait()


def edge_rows(first, last):
    zero = jnp.zeros_like(first[:1])
    own = [first[0:1], first[1:2], zero, first[0:1]]
    passed = [last[EDGE - 1 :], zero, last[EDGE - 2 : EDGE - 1], last[EDGE - 1 :]]
    return own, passed


def lead_kernel(k_ref, v_ref, f_ref, *rest):
    outs, (f_buf, e_buf, out_buf, f_sem, e_sem, out_sem) = rest[:Z_SIZE], rest[Z_SIZE:]
    rows = f_ref.shape[0]
    slabs = outs[0].shape[2] - 1
    head, tail = pl.ds(0, EDGE), pl.ds(rows - EDGE, EDGE)
    pieces = [pl.ds(j * LANE, LANE) for j in range(slabs)]
    f_copies = [send(f_ref.at[p, :], f_buf.at[p, :], f_sem.at[j]) for j, p in enumerate(pieces)]
    sources = [k_ref.at[head, :], k_ref.at[tail, :], v_ref.at[head, :], v_ref.at[tail, :]]
    e_copies = [send(x, e_buf.at[i], e_sem.at[i]) for i, x in enumerate(sources)]
    z, x, c = place()
    depth = outs[0].shape[3]
    out_copies = []

    def put(j, block_of):
        for kz in range(Z_SIZE):
            g = (z + kz) % Z_SIZE
            block = block_of(pl.ds(pl.multiple_of(g * LANE, LANE), LANE))
            turned = block.T.astype(out_buf.dtype)
            for d in range(X_SIZE * 2):
                tile = turned[d * depth : (d + 1) * depth]
                out_buf[kz, (d // 2 - x + X_SIZE) % X_SIZE, (d % 2 - c + 2) % 2, j] = tile
        for kz, out_ref in enumerate(outs):
            out_copies.append(send(out_buf.at[kz, :, :, j], out_ref.at[:, :, j], out_sem.at[kz, j]))

    for j, p in enumerate(pieces):
        f_copies[j].wait()
        put(j, lambda cols, p=p: f_buf[p, cols].astype(jnp.float32))
    wait_all(e_copies)

    def edge_block(cols):
        k0, k1, v0, v1 = [e_buf[i, :, cols].astype(jnp.float32) for i in range(len(sources))]
        own_k, next_k = edge_rows(k0, k1)
        own_v, next_v = edge_rows(v0, v1)
        listed = own_k + own_v + next_k + next_v
        return jnp.concatenate(listed + [jnp.zeros((LANE - len(listed), LANE), jnp.float32)], 0)

    put(slabs, edge_block)
    wait_all(out_copies)


def lead(k, v, f, groups):
    rows, width = f.shape
    slabs = AHEAD
    shape = jax.ShapeDtypeStruct((X_SIZE, 2, slabs + 1, width // groups, LANE), f.dtype)
    return pl.pallas_call(
        lead_kernel,
        in_specs=[HBM] * 3,
        out_specs=(HBM,) * Z_SIZE,
        out_shape=(shape,) * Z_SIZE,
        scratch_shapes=[
            pltpu.VMEM((slabs * LANE, width), f.dtype),
            pltpu.VMEM((4, EDGE, width), f.dtype),
            pltpu.VMEM((Z_SIZE, *shape.shape), f.dtype),
            pltpu.SemaphoreType.DMA((slabs,)),
            pltpu.SemaphoreType.DMA((4,)),
            pltpu.SemaphoreType.DMA((Z_SIZE, slabs + 1)),
        ],
        cost_estimate=cost(10),
        compiler_params=params(60),
    )(k, v, f)


def coef_kernel(taps_ref, skip_ref, taps_out, skip_out, turned):
    depth = skip_out.shape[0]
    me = lax.axis_index("seq")
    per = LANE // depth
    cols = pl.ds(pl.multiple_of(me // per * LANE, LANE), LANE)
    k, v = taps_ref[1, :, cols], taps_ref[2, :, cols]

    def pairs(w, order):
        return [w[i : i + 1] for i in order for _ in range(2)]

    rows = pairs(k, (0, 1)) + pairs(v, (0, 1)) + pairs(k, (1, 2)) + pairs(v, (1, 2))
    zeros = jnp.zeros((LANE - len(rows), LANE), jnp.float32)
    mine = pl.ds(pl.multiple_of(me % per * depth, depth), depth)
    turned[...] = jnp.concatenate(rows + [zeros], 0).T
    taps_out[...] = turned[mine, :]
    turned[...] = jnp.broadcast_to(skip_ref[:, cols], (LANE, LANE)).T
    skip_out[...] = turned[mine, :]


def coefficients(taps, skip, depth):
    shape = jax.ShapeDtypeStruct((depth, LANE), jnp.float32)
    return pl.pallas_call(
        coef_kernel,
        out_shape=(shape, shape),
        scratch_shapes=[pltpu.VMEM((LANE, LANE), jnp.float32)],
        compiler_params=params(4),
    )(taps, skip[None, :])


def put_turned(out_ref, j, block):
    depth = out_ref.shape[2]
    per = LANE // depth
    for g in range(block.shape[1] // LANE):
        turned = block[:, g * LANE : (g + 1) * LANE].T
        out_ref[g * per : (g + 1) * per, j] = turned.reshape(per, depth, LANE).astype(out_ref.dtype)


def pack_kernel(*refs):
    ins, outs = refs[:Z_SIZE], refs[Z_SIZE:]
    for d, out_ref in enumerate(outs):
        for kz, in_ref in enumerate(ins):
            out_ref[kz] = in_ref[d // 2, d % 2]


def pack(parts):
    shape = jax.ShapeDtypeStruct((Z_SIZE, *parts[0].shape[2:]), parts[0].dtype)
    return pl.pallas_call(
        pack_kernel,
        out_shape=(shape,) * (X_SIZE * 2),
        cost_estimate=cost(20),
        compiler_params=params(6),
    )(*parts)


def shift(block, dz, dx, dc):
    route = []
    for z in range(Z_SIZE):
        for x in range(X_SIZE):
            for c in range(2):
                to = ((z + dz) % Z_SIZE * X_SIZE + (x + dx) % X_SIZE) * 2 + (c + dc) % 2
                route.append(((z * X_SIZE + x) * 2 + c, to))
    return lax.ppermute(block, "seq", route)


def spread(parts):
    parts = [parts[0]] + [shift(parts[k], k, 0, 0) for k in range(1, Z_SIZE)]
    parts = pack(parts)
    return [parts[0]] + [shift(parts[d], 0, d // 2, d % 2) for d in range(1, X_SIZE * 2)]


def extend(ext_ref, x_ref, edge):
    rows = x_ref.shape[0]
    ext_ref[0:8, :] = edge
    ext_ref[8 : 8 + rows, :] = x_ref[...].astype(jnp.float32)


def taps_of(ext_ref, taps, start, size):
    return (
        taps[0:1, :] * ext_ref[start + 8 : start + 8 + size, :]
        + taps[1:2, :] * ext_ref[start + 7 : start + 7 + size, :]
        + taps[2:3, :] * ext_ref[start + 6 : start + 6 + size, :]
    )


def product_kernel(k_ref, v_ref, f_ref, taps_ref, out_ref, k_ext, v_ext, out_buf, sem):
    slabs = k_ref.shape[0] // LANE
    copies = []

    def put(j, block):
        put_turned(out_buf, j, block)
        copies.append(send(out_buf.at[:, j], out_ref.at[:, j], sem.at[j]))

    for j in range(AHEAD, slabs):
        put(slabs + j - AHEAD, f_ref[j * LANE : (j + 1) * LANE, :].astype(jnp.float32))
    zero = jnp.zeros((8, k_ref.shape[1]), jnp.float32)
    k_ext[0:8, :] = zero
    v_ext[0:8, :] = zero
    for j in range(slabs):
        rows, ext = slice(j * LANE, (j + 1) * LANE), slice(8 + j * LANE, 8 + (j + 1) * LANE)
        k_ext[ext, :] = k_ref[rows, :].astype(jnp.float32)
        v_ext[ext, :] = v_ref[rows, :].astype(jnp.float32)
        kf = taps_of(k_ext, taps_ref[1], j * LANE, LANE)
        vf = taps_of(v_ext, taps_ref[2], j * LANE, LANE)
        put(j, kf * vf)
    wait_all(copies)


def product(k, v, f, taps, groups):
    rows, width = k.shape
    ext = pltpu.VMEM((rows + 8, width), jnp.float32)
    slabs = rows // LANE * 2 - AHEAD
    shape = jax.ShapeDtypeStruct((groups, slabs, width // groups, LANE), k.dtype)
    return pl.pallas_call(
        product_kernel,
        in_specs=[VMEM] * 4,
        out_specs=HBM,
        out_shape=shape,
        scratch_shapes=[ext, ext, pltpu.VMEM(shape.shape, shape.dtype), pltpu.SemaphoreType.DMA((slabs,))],
        cost_estimate=cost(20),
        compiler_params=params(12),
    )(k, v, f, taps)


def gate_kernel(q_ref, edge_ref, taps_ref, out_ref, q_ext):
    extend(q_ext, q_ref, edge_ref[EDGE - 8 :, :].astype(jnp.float32))
    for j in range(out_ref.shape[0] // LANE):
        qf = taps_of(q_ext, taps_ref[0], j * LANE, LANE)
        out_ref[j * LANE : (j + 1) * LANE, :] = qf.astype(out_ref.dtype)


def gate(q, edge, taps):
    rows, width = q.shape
    return pl.pallas_call(
        gate_kernel,
        out_shape=jax.ShapeDtypeStruct(q.shape, q.dtype),
        scratch_shapes=[pltpu.VMEM((rows + 8, width), jnp.float32)],
        compiler_params=params(8),
    )(q, edge, taps)


def mix(table, data):
    return jnp.dot(table, data, preferred_element_type=jnp.float32)


def mend(u_wide, edges, taps):
    depth = taps.shape[0]
    rows = edges.shape[0] - depth
    lane = lax.broadcasted_iota(jnp.int32, (rows, LANE), 1)
    sources = rows // depth
    weights = jnp.broadcast_to(taps[...][None], (sources, depth, LANE)).reshape(rows, LANE)
    terms = jnp.where(lane < 8, edges[depth:, :], edges[:rows, :]) * weights

    def after(x, steps):
        return pltpu.roll(x, LANE - steps, 1)

    terms = terms + after(terms, 2)
    terms = terms + after(terms, 8)
    fixed = (terms * after(terms, 4)).astype(jnp.bfloat16).astype(jnp.float32)
    size = u_wide.shape[0] // sources
    for i in range(sources):
        part, at = slice(i * depth, (i + 1) * depth), slice(i * size, i * size + depth)
        u_wide[at, :] = jnp.where(lane[part] < 2, fixed[part], u_wide[at, :])


def conv_kernel(u_ref, q_ref, taps_ref, skip_ref, t1, t2, t2_inv, t1_inv, tw_c, tw_s, *rest):
    f_refs, (y_ref, q_edge, u_wide, f_wide, y_wide, edges, y_buf, q_sem, y_sem) = rest[:-9], rest[-9:]
    q_copy = send(q_ref.at[pl.ds(q_ref.shape[0] - EDGE, EDGE), :], q_edge, q_sem)
    depth = skip_ref.shape[0]
    edges[:depth, :] = jnp.zeros((depth, LANE), jnp.float32)
    z, x, c = place()
    sources = u_ref.shape[0]
    size = u_wide.shape[0] // sources
    ahead = AHEAD * depth
    for i in range(sources):
        both = u_ref[i].astype(jnp.float32).reshape(-1, LANE)
        u_wide[i * size : (i + 1) * size, :] = both[:size]
        f_wide[i * size + ahead : (i + 1) * size, :] = both[size:]
    for d, f_ref in enumerate(f_refs):
        for kz in range(Z_SIZE):
            src = ((z - kz + Z_SIZE) % Z_SIZE * X_SIZE + (x - d // 2 + X_SIZE) % X_SIZE) * 2 + (c + d) % 2
            row = pl.multiple_of(src * size, size)
            f_wide[pl.ds(row, ahead), :] = f_ref[kz, :AHEAD].reshape(ahead, LANE).astype(jnp.float32)
            row = pl.multiple_of((src + 1) * depth, depth)
            edges[pl.ds(row, depth), :] = f_ref[kz, AHEAD].astype(jnp.float32)
    mend(u_wide, edges, taps_ref)
    low = jnp.bfloat16

    def part(x, i):
        return x[:, i * LANE : (i + 1) * LANE]

    for start in range(0, depth, GROUP):
        chans = range(start, start + GROUP)
        rows = [pl.ds(c, LANE, stride=depth) for c in chans]
        data = [u_wide[r, :].astype(low) for r in rows] + [f_wide[r, :].astype(low) for r in rows]
        first = mix(t1[...], jnp.concatenate(data, 1))
        turned = []
        for i in range(2 * GROUP):
            re, im = part(first[:LANE], i), part(first[LANE:], i)
            c, s = tw_c[...], tw_s[...]
            turned.append(jnp.concatenate([re * c - im * s, re * s + im * c], 1).astype(low))
        spec = mix(jnp.concatenate(turned, 0), t2[...])
        prod = []
        for i in range(GROUP):
            a = spec[i * LANE : (i + 1) * LANE]
            b = spec[(GROUP + i) * LANE : (GROUP + i + 1) * LANE]
            ar, ai, br, bi = a[:, :LANE], a[:, LANE:], b[:, :LANE], b[:, LANE:]
            prod.append(jnp.concatenate([ar * br - ai * bi, ar * bi + ai * br], 1).astype(low))
        back = mix(jnp.concatenate(prod, 0), t2_inv[...])
        cols = []
        for i in range(GROUP):
            v = back[i * LANE : (i + 1) * LANE]
            re, im = v[:, :LANE], v[:, LANE:]
            c, s = tw_c[...], tw_s[...]
            cols.append(jnp.concatenate([re * c + im * s, im * c - re * s], 0).astype(low))
        conv = mix(t1_inv[...], jnp.concatenate(cols, 1))
        for i, r in enumerate(rows):
            y_wide[r, :] = part(conv, i)
    copies = []
    parts = y_sem.shape[0]
    rows = y_ref.shape[0] // parts
    shape = (rows // depth, depth, LANE)
    for i in range(parts):
        at = slice(i * rows, (i + 1) * rows)
        y = y_wide[at, :].reshape(shape) + skip_ref[...][None] * u_wide[at, :].reshape(shape)
        y_buf[at, :] = y.reshape(rows, LANE).astype(y_buf.dtype)
        copies.append(send(y_buf.at[at, :], y_ref.at[at, :], y_sem.at[i]))
    wait_all(copies + [q_copy])


def long_conv(u, f, q, taps, skip):
    sources, slabs, depth, _ = u.shape
    slabs = (slabs + AHEAD) // 2
    flat = (sources * slabs * depth, LANE)
    wide = pltpu.VMEM(flat, jnp.float32)
    edges = pltpu.VMEM(((sources + 1) * depth, LANE), jnp.float32)
    operands = (u, q, taps, skip, *tables(), *f)
    y, q_edge = pl.pallas_call(
        conv_kernel,
        in_specs=[HBM if x is q else VMEM for x in operands],
        out_specs=(HBM, VMEM),
        out_shape=(jax.ShapeDtypeStruct(flat, u.dtype), jax.ShapeDtypeStruct((EDGE, q.shape[1]), q.dtype)),
        scratch_shapes=[wide] * 3
        + [edges, pltpu.VMEM(flat, u.dtype), pltpu.SemaphoreType.DMA, pltpu.SemaphoreType.DMA((4,))],
        compiler_params=params(40),
    )(*operands)
    return y.reshape(sources, slabs, depth, LANE), q_edge


def join_kernel(y_ref, qf_ref, stream_ref, gain_ref, out_ref, sum_ref, sq_ref, out_buf, sem):
    groups, slabs, depth, _ = y_ref.shape
    per = LANE // depth
    sq_ref[...] = jnp.zeros_like(sq_ref)
    copies = []
    for j in range(slabs):
        rows = slice(j * LANE, (j + 1) * LANE)
        squares = jnp.zeros((LANE, LANE), jnp.float32)
        for g in range(groups // per):
            cols = slice(g * LANE, (g + 1) * LANE)
            y = y_ref[g * per : (g + 1) * per, j].reshape(LANE, LANE).astype(jnp.float32).T
            gated = (qf_ref[rows, cols].astype(jnp.float32) * y).astype(jnp.bfloat16)
            summed = stream_ref[rows, cols].astype(jnp.float32) + gated.astype(jnp.float32)
            out_buf[rows, cols] = summed.astype(out_buf.dtype)
            sum_ref[rows, cols] = summed * gain_ref[:, cols]
            squares = squares + summed * summed
        copies.append(send(out_buf.at[rows, :], out_ref.at[rows, :], sem.at[j]))
        total = jnp.sum(squares.T, axis=0, keepdims=True)
        for d in range(sq_ref.shape[0]):
            sq_ref[d, j : j + 1, :] = total
    wait_all(copies)


def join(y, qf, stream, gain, fan):
    rows, _ = stream.shape
    return pl.pallas_call(
        join_kernel,
        in_specs=[VMEM] * 4,
        out_specs=(HBM, VMEM, VMEM),
        out_shape=(
            jax.ShapeDtypeStruct(stream.shape, stream.dtype),
            jax.ShapeDtypeStruct(stream.shape, jnp.float32),
            jax.ShapeDtypeStruct((fan, 8, LANE), jnp.float32),
        ),
        scratch_shapes=[
            pltpu.VMEM(stream.shape, stream.dtype),
            pltpu.SemaphoreType.DMA((rows // LANE,)),
        ],
        compiler_params=params(12),
    )(y, qf, stream, gain[None, :])


def norm_kernel(channels, sum_ref, sq_ref, out_ref, out_buf, sem):
    squares = jnp.sum(sq_ref[...], axis=0)
    scale = 1.0 / jnp.sqrt(squares / channels + 1e-05)
    copies = []
    for j in range(out_ref.shape[0] // LANE):
        rows = slice(j * LANE, (j + 1) * LANE)
        column = jnp.broadcast_to(scale[j : j + 1, :], (LANE, LANE)).T
        for g in range(out_ref.shape[1] // LANE):
            cols = slice(g * LANE, (g + 1) * LANE)
            out_buf[rows, cols] = (sum_ref[rows, cols] * column).astype(out_buf.dtype)
        copies.append(send(out_buf.at[rows, :], out_ref.at[rows, :], sem.at[j]))
    wait_all(copies)


def norm(summed, squares):
    channels = summed.shape[1] * squares.shape[0]

    def kernel(*refs):
        norm_kernel(channels, *refs)

    return pl.pallas_call(
        kernel,
        in_specs=[VMEM] * 2,
        out_specs=HBM,
        out_shape=jax.ShapeDtypeStruct(summed.shape, jnp.bfloat16),
        scratch_shapes=[
            pltpu.VMEM(summed.shape, jnp.bfloat16),
            pltpu.SemaphoreType.DMA((summed.shape[0] // LANE,)),
        ],
        compiler_params=params(8),
    )(summed, squares)


def exchange(x, axis):
    return lax.all_to_all(x, axis, split_axis=0, concat_axis=0, tiled=True)


def shards(queries, keys, values, filters, short_weights, skip_gain, stream, norm_gain):
    groups = lax.axis_size("seq")
    fan = lax.axis_size("ch")
    rows, width = queries.shape
    slab = width // groups
    parts = lead(keys, values, filters, groups)
    u_all = exchange(product(keys, values, filters, short_weights, groups), "seq")
    f_all = spread(parts)
    taps, skip = coefficients(short_weights, skip_gain, slab)
    y, q_edge = long_conv(u_all, f_all, queries, taps, skip)
    y_home = exchange(y, "seq")
    q_edge = lax.ppermute(q_edge, "seq", [(i, i + 1) for i in range(groups - 1)])
    qf = gate(queries, q_edge, short_weights)
    stream_out, summed, squares = join(y_home, qf, stream, norm_gain, fan)
    normed = norm(summed, exchange(squares, "ch"))
    return (stream_out, normed)


def solution(mesh):
    wide = P("seq", "ch")
    in_specs = (wide, wide, wide, wide, P(None, None, "ch"), P("ch"), wide, P("ch"))
    return jax.shard_map(shards, mesh=mesh, in_specs=in_specs, out_specs=(wide, wide), check_vma=False)
```

```python
import jax
import jax.numpy as jnp
import numpy as np
from jax import lax
from jax.experimental import pallas as pl
from jax.experimental.pallas import tpu as pltpu
from jax.sharding import PartitionSpec as P

LANE = 128
EDGE = 16
GROUP = 8
Z_SIZE = 4
X_SIZE = 4
AHEAD = 4
Y_SIZE = 4
MIB = 1024 * 1024


def params(mebibytes):
    return pltpu.CompilerParams(vmem_limit_bytes=mebibytes * MIB)


def cost(micros):
    return pl.CostEstimate(flops=int(micros * 1e9), bytes_accessed=0, transcendentals=0)


def tables():
    n = LANE * LANE
    a = np.arange(LANE, dtype=np.float64)
    first = -2.0 * np.pi * np.outer(a + 0.25, a) / LANE
    twist = -2.0 * np.pi * np.outer(a + 0.25, a) / n
    second = -2.0 * np.pi * np.outer(a, a) / LANE
    t1 = np.concatenate([np.cos(first), np.sin(first)], 0)
    cos2, sin2 = np.cos(second), np.sin(second)
    t2 = np.block([[cos2, sin2], [-sin2, cos2]])
    t2_inv = np.block([[cos2, -sin2], [sin2, cos2]])
    t1_inv = np.concatenate([np.cos(first).T, np.sin(first).T], 1) / n
    low = [jnp.asarray(t, jnp.bfloat16) for t in (t1, t2, t2_inv, t1_inv)]
    return (*low, jnp.asarray(np.cos(twist), jnp.float32), jnp.asarray(np.sin(twist), jnp.float32))


def place():
    me = lax.axis_index("seq")
    return me // (X_SIZE * 2), me // 2 % X_SIZE, me % 2


HBM = pl.BlockSpec(memory_space=pl.ANY)
VMEM = pl.BlockSpec(memory_space=pltpu.VMEM)


def send(source, target, sem):
    copy = pltpu.make_async_copy(source, target, sem)
    copy.start()
    return copy


def wait_all(copies):
    for copy in copies:
        copy.wait()


def edge_rows(first, last):
    zero = jnp.zeros_like(first[:1])
    own = [first[0:1], first[1:2], zero, first[0:1]]
    passed = [last[EDGE - 1 :], zero, last[EDGE - 2 : EDGE - 1], last[EDGE - 1 :]]
    return own, passed


def lead_kernel(k_ref, v_ref, f_ref, *rest):
    outs, (f_buf, e_buf, out_buf, f_sem, e_sem, out_sem) = rest[:Z_SIZE], rest[Z_SIZE:]
    rows = f_ref.shape[0]
    head, tail = pl.ds(0, EDGE), pl.ds(rows - EDGE, EDGE)
    pieces = [pl.ds(j * LANE, LANE) for j in range(AHEAD)]
    f_copies = [send(f_ref.at[p, :], f_buf.at[p, :], f_sem.at[j]) for j, p in enumerate(pieces)]
    sources = [k_ref.at[head, :], k_ref.at[tail, :], v_ref.at[head, :], v_ref.at[tail, :]]
    e_copies = [send(x, e_buf.at[i], e_sem.at[i]) for i, x in enumerate(sources)]
    z, x, c = place()
    depth = out_buf.shape[2]
    cols = [pl.ds(pl.multiple_of((z + kz) % Z_SIZE * LANE, LANE), LANE) for kz in range(Z_SIZE)]
    for j, p in enumerate(pieces):
        f_copies[j].wait()
        for kz in range(Z_SIZE):
            turned = f_buf[p, cols[kz]].astype(jnp.float32).T.astype(out_buf.dtype)
            for d in range(X_SIZE * 2):
                to = (d // 2 - x + X_SIZE) % X_SIZE * 2 + (d % 2 - c + 2) % 2
                out_buf[kz, to * AHEAD + j] = turned[d * depth : (d + 1) * depth]
    wait_all(e_copies)
    copies = []
    for kz, out_ref in enumerate(outs):
        k0, k1, v0, v1 = [e_buf[i, :, cols[kz]].astype(jnp.float32) for i in range(len(sources))]
        own_k, next_k = edge_rows(k0, k1)
        own_v, next_v = edge_rows(v0, v1)
        edge = jnp.concatenate(own_k + own_v + next_k + next_v, 0)
        out_buf[kz, X_SIZE * 2 * AHEAD] = edge.astype(out_buf.dtype)
        copies.append(send(out_buf.at[kz], out_ref, out_sem.at[kz]))
    wait_all(copies)


def lead(k, v, f, groups):
    rows, width = f.shape
    shape = jax.ShapeDtypeStruct((X_SIZE * 2 * AHEAD + 1, width // groups, LANE), f.dtype)
    return pl.pallas_call(
        lead_kernel,
        in_specs=[HBM] * 3,
        out_specs=(HBM,) * Z_SIZE,
        out_shape=(shape,) * Z_SIZE,
        scratch_shapes=[
            pltpu.VMEM((AHEAD * LANE, width), f.dtype),
            pltpu.VMEM((4, EDGE, width), f.dtype),
            pltpu.VMEM((Z_SIZE, *shape.shape), f.dtype),
            pltpu.SemaphoreType.DMA((AHEAD,)),
            pltpu.SemaphoreType.DMA((4,)),
            pltpu.SemaphoreType.DMA((Z_SIZE,)),
        ],
        cost_estimate=cost(10),
        compiler_params=params(60),
    )(k, v, f)


def coef_kernel(taps_ref, skip_ref, taps_out, skip_out, turned):
    depth = skip_out.shape[0]
    me = lax.axis_index("seq")
    per = LANE // depth
    cols = pl.ds(pl.multiple_of(me // per * LANE, LANE), LANE)
    k, v = taps_ref[1, :, cols], taps_ref[2, :, cols]

    def pairs(w, order):
        return [w[i : i + 1] for i in order for _ in range(2)]

    rows = pairs(k, (0, 1)) + pairs(v, (0, 1)) + pairs(k, (1, 2)) + pairs(v, (1, 2))
    zeros = jnp.zeros((LANE - len(rows), LANE), jnp.float32)
    mine = pl.ds(pl.multiple_of(me % per * depth, depth), depth)
    turned[...] = jnp.concatenate(rows + [zeros], 0).T
    taps_out[...] = turned[mine, :]
    turned[...] = jnp.broadcast_to(skip_ref[:, cols], (LANE, LANE)).T
    skip_out[...] = turned[mine, :]


def coefficients(taps, skip, depth):
    shape = jax.ShapeDtypeStruct((depth, LANE), jnp.float32)
    return pl.pallas_call(
        coef_kernel,
        out_shape=(shape, shape),
        scratch_shapes=[pltpu.VMEM((LANE, LANE), jnp.float32)],
        compiler_params=params(4),
    )(taps, skip[None, :])


def put_turned(out_ref, j, block):
    depth = out_ref.shape[2]
    per = LANE // depth
    for g in range(block.shape[1] // LANE):
        turned = block[:, g * LANE : (g + 1) * LANE].T
        out_ref[g * per : (g + 1) * per, j] = turned.reshape(per, depth, LANE).astype(out_ref.dtype)


def pack_kernel(*refs):
    ins, outs, turned = refs[:Z_SIZE], refs[Z_SIZE:-1], refs[-1]
    last = ins[0].shape[0] - 1
    depth = ins[0].shape[1]
    edges = [in_ref[last].astype(jnp.float32) for in_ref in ins]
    zeros = jnp.zeros((LANE - Z_SIZE * depth, LANE), jnp.float32)
    turned[...] = jnp.concatenate(edges + [zeros], 0).T
    _, x, c = place()
    for d, out_ref in enumerate(outs):
        for kz, in_ref in enumerate(ins):
            out_ref[kz * AHEAD : (kz + 1) * AHEAD] = in_ref[d * AHEAD : (d + 1) * AHEAD]
        at = ((x + d // 2) % X_SIZE * 2 + (c + d) % 2) * depth
        out_ref[Z_SIZE * AHEAD] = turned[pl.ds(pl.multiple_of(at, depth), depth), :].astype(out_ref.dtype)


def pack(parts):
    shape = jax.ShapeDtypeStruct((Z_SIZE * AHEAD + 1, *parts[0].shape[1:]), parts[0].dtype)
    return pl.pallas_call(
        pack_kernel,
        out_shape=(shape,) * (X_SIZE * 2),
        scratch_shapes=[pltpu.VMEM((LANE, LANE), jnp.float32)],
        cost_estimate=cost(20),
        compiler_params=params(6),
    )(*parts)


def shift(block, dz, dx, dc):
    route = []
    for z in range(Z_SIZE):
        for x in range(X_SIZE):
            for c in range(2):
                to = ((z + dz) % Z_SIZE * X_SIZE + (x + dx) % X_SIZE) * 2 + (c + dc) % 2
                route.append(((z * X_SIZE + x) * 2 + c, to))
    return lax.ppermute(block, "seq", route)


def spread(parts):
    parts = [parts[0]] + [shift(parts[k], k, 0, 0) for k in range(1, Z_SIZE)]
    parts = pack(parts)
    return [parts[0]] + [shift(parts[d], 0, d // 2, d % 2) for d in range(1, X_SIZE * 2)]


def extend(ext_ref, x_ref, edge):
    rows = x_ref.shape[0]
    ext_ref[0:8, :] = edge
    ext_ref[8 : 8 + rows, :] = x_ref[...].astype(jnp.float32)


def taps_of(ext_ref, taps, start, size):
    return (
        taps[0:1, :] * ext_ref[start + 8 : start + 8 + size, :]
        + taps[1:2, :] * ext_ref[start + 7 : start + 7 + size, :]
        + taps[2:3, :] * ext_ref[start + 6 : start + 6 + size, :]
    )


def product_kernel(k_ref, v_ref, f_ref, taps_ref, out_ref, k_ext, v_ext, out_buf, sem):
    slabs = k_ref.shape[0] // LANE
    copies = []

    def put(j, block):
        put_turned(out_buf, j, block)
        copies.append(send(out_buf.at[:, j], out_ref.at[:, j], sem.at[j]))

    for j in range(AHEAD, slabs):
        put(slabs + j - AHEAD, f_ref[j * LANE : (j + 1) * LANE, :].astype(jnp.float32))
    zero = jnp.zeros((8, k_ref.shape[1]), jnp.float32)
    k_ext[0:8, :] = zero
    v_ext[0:8, :] = zero
    for j in range(slabs):
        rows, ext = slice(j * LANE, (j + 1) * LANE), slice(8 + j * LANE, 8 + (j + 1) * LANE)
        k_ext[ext, :] = k_ref[rows, :].astype(jnp.float32)
        v_ext[ext, :] = v_ref[rows, :].astype(jnp.float32)
        kf = taps_of(k_ext, taps_ref[1], j * LANE, LANE)
        vf = taps_of(v_ext, taps_ref[2], j * LANE, LANE)
        put(j, kf * vf)
    wait_all(copies)


def product(k, v, f, taps, groups):
    rows, width = k.shape
    ext = pltpu.VMEM((rows + 8, width), jnp.float32)
    slabs = rows // LANE * 2 - AHEAD
    shape = jax.ShapeDtypeStruct((groups, slabs, width // groups, LANE), k.dtype)
    return pl.pallas_call(
        product_kernel,
        in_specs=[VMEM] * 4,
        out_specs=HBM,
        out_shape=shape,
        scratch_shapes=[ext, ext, pltpu.VMEM(shape.shape, shape.dtype), pltpu.SemaphoreType.DMA((slabs,))],
        cost_estimate=cost(20),
        compiler_params=params(12),
    )(k, v, f, taps)


def gate_kernel(q_ref, edge_ref, taps_ref, out_ref, q_ext):
    extend(q_ext, q_ref, edge_ref[EDGE - 8 :, :].astype(jnp.float32))
    for j in range(out_ref.shape[0] // LANE):
        qf = taps_of(q_ext, taps_ref[0], j * LANE, LANE)
        out_ref[j * LANE : (j + 1) * LANE, :] = qf.astype(out_ref.dtype)


def gate(q, edge, taps):
    rows, width = q.shape
    return pl.pallas_call(
        gate_kernel,
        out_shape=jax.ShapeDtypeStruct(q.shape, q.dtype),
        scratch_shapes=[pltpu.VMEM((rows + 8, width), jnp.float32)],
        compiler_params=params(8),
    )(q, edge, taps)


def mix(table, data):
    return jnp.dot(table, data, preferred_element_type=jnp.float32)


def mend(u_wide, edges, taps):
    depth = taps.shape[0]
    rows = edges.shape[0] - depth
    lane = lax.broadcasted_iota(jnp.int32, (rows, LANE), 1)
    sources = rows // depth
    weights = jnp.broadcast_to(taps[...][None], (sources, depth, LANE)).reshape(rows, LANE)
    terms = jnp.where(lane < 8, edges[depth:, :], edges[:rows, :]) * weights

    def after(x, steps):
        return pltpu.roll(x, LANE - steps, 1)

    terms = terms + after(terms, 2)
    terms = terms + after(terms, 8)
    fixed = (terms * after(terms, 4)).astype(jnp.bfloat16).astype(jnp.float32)
    size = u_wide.shape[0] // sources
    for i in range(sources):
        part, at = slice(i * depth, (i + 1) * depth), slice(i * size, i * size + depth)
        u_wide[at, :] = jnp.where(lane[part] < 2, fixed[part], u_wide[at, :])


def conv_kernel(u_ref, q_ref, taps_ref, skip_ref, t1, t2, t2_inv, t1_inv, tw_c, tw_s, *rest):
    f_refs, (y_ref, q_edge, u_wide, f_wide, y_wide, edges, y_buf, q_sem, y_sem) = rest[:-9], rest[-9:]
    q_copy = send(q_ref.at[pl.ds(q_ref.shape[0] - EDGE, EDGE), :], q_edge, q_sem)
    depth = skip_ref.shape[0]
    edges[:depth, :] = jnp.zeros((depth, LANE), jnp.float32)
    z, x, c = place()
    sources = u_ref.shape[0]
    size = u_wide.shape[0] // sources
    ahead = AHEAD * depth
    for i in range(sources):
        both = u_ref[i].astype(jnp.float32).reshape(-1, LANE)
        u_wide[i * size : (i + 1) * size, :] = both[:size]
        if ahead < size:
            f_wide[i * size + ahead : (i + 1) * size, :] = both[size:]
    for d, f_ref in enumerate(f_refs):
        edge = f_ref[Z_SIZE * AHEAD].astype(jnp.float32)
        for kz in range(Z_SIZE):
            src = ((z - kz + Z_SIZE) % Z_SIZE * X_SIZE + (x - d // 2 + X_SIZE) % X_SIZE) * 2 + (c + d) % 2
            row = pl.multiple_of(src * size, size)
            tiles = f_ref[kz * AHEAD : (kz + 1) * AHEAD].reshape(ahead, LANE)
            f_wide[pl.ds(row, ahead), :] = tiles.astype(jnp.float32)
            row = pl.multiple_of((src + 1) * depth, depth)
            edges[pl.ds(row, depth), :] = pltpu.roll(edge, LANE - kz * depth, 1) if kz else edge
    low = jnp.bfloat16

    def part(x, i):
        return x[:, i * LANE : (i + 1) * LANE]

    def spectra(wide, rows):
        data = [wide[r, :].astype(low) for r in rows]
        first = mix(t1[...], jnp.concatenate(data, 1))
        turned = []
        for i in range(len(rows)):
            re, im = part(first[:LANE], i), part(first[LANE:], i)
            c, s = tw_c[...], tw_s[...]
            turned.append(jnp.concatenate([re * c - im * s, re * s + im * c], 1).astype(low))
        return mix(jnp.concatenate(turned, 0), t2[...])

    for start in range(0, depth, GROUP):
        rows = [pl.ds(ch, LANE, stride=depth) for ch in range(start, start + GROUP)]
        f_spec = spectra(f_wide, rows)
        if start == 0:
            mend(u_wide, edges, taps_ref)
        u_spec = spectra(u_wide, rows)
        prod = []
        for i in range(GROUP):
            a, b = u_spec[i * LANE : (i + 1) * LANE], f_spec[i * LANE : (i + 1) * LANE]
            ar, ai, br, bi = a[:, :LANE], a[:, LANE:], b[:, :LANE], b[:, LANE:]
            prod.append(jnp.concatenate([ar * br - ai * bi, ar * bi + ai * br], 1).astype(low))
        back = mix(jnp.concatenate(prod, 0), t2_inv[...])
        cols = []
        for i in range(GROUP):
            v = back[i * LANE : (i + 1) * LANE]
            re, im = v[:, :LANE], v[:, LANE:]
            c, s = tw_c[...], tw_s[...]
            cols.append(jnp.concatenate([re * c + im * s, im * c - re * s], 0).astype(low))
        conv = mix(t1_inv[...], jnp.concatenate(cols, 1))
        for i, r in enumerate(rows):
            y_wide[r, :] = part(conv, i)
    copies = []
    parts = y_sem.shape[0]
    rows = y_ref.shape[0] // parts
    shape = (rows // depth, depth, LANE)
    for i in range(parts):
        at = slice(i * rows, (i + 1) * rows)
        y = y_wide[at, :].reshape(shape) + skip_ref[...][None] * u_wide[at, :].reshape(shape)
        y_buf[at, :] = y.reshape(rows, LANE).astype(y_buf.dtype)
        copies.append(send(y_buf.at[at, :], y_ref.at[at, :], y_sem.at[i]))
    wait_all(copies + [q_copy])


def long_conv(u, f, q, taps, skip):
    sources, slabs, depth, _ = u.shape
    slabs = (slabs + AHEAD) // 2
    flat = (sources * slabs * depth, LANE)
    wide = pltpu.VMEM(flat, jnp.float32)
    edges = pltpu.VMEM(((sources + 1) * depth, LANE), jnp.float32)
    operands = (u, q, taps, skip, *tables(), *f)
    y, q_edge = pl.pallas_call(
        conv_kernel,
        in_specs=[HBM if x is q else VMEM for x in operands],
        out_specs=(HBM, VMEM),
        out_shape=(jax.ShapeDtypeStruct(flat, u.dtype), jax.ShapeDtypeStruct((EDGE, q.shape[1]), q.dtype)),
        scratch_shapes=[wide] * 3
        + [edges, pltpu.VMEM(flat, u.dtype), pltpu.SemaphoreType.DMA, pltpu.SemaphoreType.DMA((4,))],
        compiler_params=params(40),
    )(*operands)
    return y.reshape(sources, slabs, depth, LANE), q_edge


def join_kernel(y_ref, qf_ref, stream_ref, gain_ref, out_ref, sum_ref, sq_ref):
    groups, slabs, depth, _ = y_ref.shape
    per = LANE // depth
    sq_ref[...] = jnp.zeros_like(sq_ref)
    for j in range(slabs):
        rows = slice(j * LANE, (j + 1) * LANE)
        squares = jnp.zeros((LANE, LANE), jnp.float32)
        for g in range(groups // per):
            cols = slice(g * LANE, (g + 1) * LANE)
            y = y_ref[g * per : (g + 1) * per, j].reshape(LANE, LANE).astype(jnp.float32).T
            gated = (qf_ref[rows, cols].astype(jnp.float32) * y).astype(jnp.bfloat16)
            summed = stream_ref[rows, cols].astype(jnp.float32) + gated.astype(jnp.float32)
            out_ref[rows, cols] = summed.astype(out_ref.dtype)
            sum_ref[rows, cols] = summed * gain_ref[:, cols]
            squares = squares + summed * summed
        total = jnp.sum(squares.T, axis=0, keepdims=True)
        sq_ref[j : j + 1, :] = total


def join(y, qf, stream, gain):
    return pl.pallas_call(
        join_kernel,
        in_specs=[VMEM] * 4,
        out_shape=(
            jax.ShapeDtypeStruct(stream.shape, stream.dtype),
            jax.ShapeDtypeStruct(stream.shape, jnp.float32),
            jax.ShapeDtypeStruct((8, LANE), jnp.float32),
        ),
        compiler_params=params(12),
    )(y, qf, stream, gain[None, :])


def norm_kernel(channels, low_ref, sum_ref, *rest):
    sq_refs, (low_out, out_ref, out_buf, low_sem, sem) = rest[:-5], rest[-5:]
    copies = [send(low_ref, low_out, low_sem)]
    squares = sum(ref[...] for ref in sq_refs)
    scale = 1.0 / jnp.sqrt(squares / channels + 1e-05)
    for j in range(out_ref.shape[0] // LANE):
        rows = slice(j * LANE, (j + 1) * LANE)
        column = jnp.broadcast_to(scale[j : j + 1, :], (LANE, LANE)).T
        for g in range(out_ref.shape[1] // LANE):
            cols = slice(g * LANE, (g + 1) * LANE)
            out_buf[rows, cols] = (sum_ref[rows, cols] * column).astype(out_buf.dtype)
        copies.append(send(out_buf.at[rows, :], out_ref.at[rows, :], sem.at[j]))
    wait_all(copies)


def norm(low, summed, squares, channels):

    def kernel(*refs):
        norm_kernel(channels, *refs)

    return pl.pallas_call(
        kernel,
        in_specs=[VMEM] * (2 + len(squares)),
        out_specs=(HBM,) * 2,
        out_shape=(jax.ShapeDtypeStruct(summed.shape, low.dtype),) * 2,
        scratch_shapes=[
            pltpu.VMEM(summed.shape, low.dtype),
            pltpu.SemaphoreType.DMA,
            pltpu.SemaphoreType.DMA((summed.shape[0] // LANE,)),
        ],
        compiler_params=params(8),
    )(low, summed, *squares)


def exchange(x, axis):
    return lax.all_to_all(x, axis, split_axis=0, concat_axis=0, tiled=True)


def across(block, fan, dz, dy):
    route = [(i, (i + dz) % fan // Y_SIZE * Y_SIZE + (i + dy) % Y_SIZE) for i in range(fan)]
    return lax.ppermute(block, "ch", route)


def shards(queries, keys, values, filters, short_weights, skip_gain, stream, norm_gain):
    groups = lax.axis_size("seq")
    fan = lax.axis_size("ch")
    rows, width = queries.shape
    slab = width // groups
    parts = lead(keys, values, filters, groups)
    u_all = exchange(product(keys, values, filters, short_weights, groups), "seq")
    f_all = spread(parts)
    taps, skip = coefficients(short_weights, skip_gain, slab)
    y, q_edge = long_conv(u_all, f_all, queries, taps, skip)
    y_home = exchange(y, "seq")
    q_edge = lax.ppermute(q_edge, "seq", [(i, i + 1) for i in range(groups - 1)])
    qf = gate(queries, q_edge, short_weights)
    low, summed, squares = join(y_home, qf, stream, norm_gain)
    squares = squares + across(squares, fan, Y_SIZE, 0)
    squares = [squares] + [across(squares, fan, 0, k) for k in range(1, Y_SIZE)]
    return norm(low, summed, squares, width * fan)


def solution(mesh):
    wide = P("seq", "ch")
    in_specs = (wide, wide, wide, wide, P(None, None, "ch"), P("ch"), wide, P("ch"))
    return jax.shard_map(shards, mesh=mesh, in_specs=in_specs, out_specs=(wide, wide), check_vma=False)
```

```python
import jax
import jax.numpy as jnp
import numpy as np
from jax import lax
from jax.experimental import pallas as pl
from jax.experimental.pallas import tpu as pltpu
from jax.sharding import PartitionSpec as P

LANE = 128
EDGE = 16
GROUP = 8
Z_SIZE = 4
X_SIZE = 4
AHEAD = 4
Y_SIZE = 4
MIB = 1024 * 1024


def params(mebibytes):
    return pltpu.CompilerParams(vmem_limit_bytes=mebibytes * MIB)


def cost(micros):
    return pl.CostEstimate(flops=int(micros * 1e9), bytes_accessed=0, transcendentals=0)


def tables():
    n = LANE * LANE
    a = np.arange(LANE, dtype=np.float64)
    first = -2.0 * np.pi * np.outer(a + 0.25, a) / LANE
    twist = -2.0 * np.pi * np.outer(a + 0.25, a) / n
    second = -2.0 * np.pi * np.outer(a, a) / LANE
    t1 = np.concatenate([np.cos(first), np.sin(first)], 0)
    cos2, sin2 = np.cos(second), np.sin(second)
    t2 = np.block([[cos2, sin2], [-sin2, cos2]])
    t2_inv = np.block([[cos2, -sin2], [sin2, cos2]])
    t1_inv = np.concatenate([np.cos(first).T, np.sin(first).T], 1) / n
    low = [jnp.asarray(t, jnp.bfloat16) for t in (t1, t2, t2_inv, t1_inv)]
    return (*low, jnp.asarray(np.cos(twist), jnp.float32), jnp.asarray(np.sin(twist), jnp.float32))


def place():
    me = lax.axis_index("seq")
    return me // (X_SIZE * 2), me // 2 % X_SIZE, me % 2


HBM = pl.BlockSpec(memory_space=pl.ANY)
VMEM = pl.BlockSpec(memory_space=pltpu.VMEM)


def send(source, target, sem):
    copy = pltpu.make_async_copy(source, target, sem)
    copy.start()
    return copy


def wait_all(copies):
    for copy in copies:
        copy.wait()


def edge_rows(first, last):
    zero = jnp.zeros_like(first[:1])
    own = [first[0:1], first[1:2], zero, first[0:1]]
    passed = [last[EDGE - 1 :], zero, last[EDGE - 2 : EDGE - 1], last[EDGE - 1 :]]
    return own, passed


def lead_kernel(q_ref, k_ref, v_ref, f_ref, *rest):
    outs, (f_buf, e_buf, f_sem, e_sem) = rest[:Z_SIZE], rest[Z_SIZE:]
    rows = f_ref.shape[0]
    head, tail = pl.ds(0, EDGE), pl.ds(rows - EDGE, EDGE)
    pieces = [pl.ds(j * LANE, LANE) for j in range(AHEAD)]
    f_copies = [send(f_ref.at[p, :], f_buf.at[p, :], f_sem.at[j]) for j, p in enumerate(pieces)]
    sources = [k_ref.at[head, :], k_ref.at[tail, :], v_ref.at[head, :], v_ref.at[tail, :]]
    e_copies = [send(x, e_buf.at[i], e_sem.at[i]) for i, x in enumerate(sources + [q_ref.at[tail, :]])]
    z, x, c = place()
    depth = outs[0].shape[1]
    cols = [pl.ds(pl.multiple_of((z + kz) % Z_SIZE * LANE, LANE), LANE) for kz in range(Z_SIZE)]
    for j, p in enumerate(pieces):
        f_copies[j].wait()
        for kz, out_ref in enumerate(outs):
            turned = f_buf[p, cols[kz]].astype(jnp.float32).T.astype(out_ref.dtype)
            for d in range(X_SIZE * 2):
                to = (d // 2 - x + X_SIZE) % X_SIZE * 2 + (d % 2 - c + 2) % 2
                out_ref[to * AHEAD + j] = turned[d * depth : (d + 1) * depth]
    wait_all(e_copies)
    edge_at = X_SIZE * 2 * AHEAD
    q_rows = e_buf[len(sources)].astype(jnp.float32)
    parts = [slice(g * LANE, (g + 1) * LANE) for g in range(q_rows.shape[1] // LANE)]
    q_list = [q_rows[r : r + 1, p] for r in (EDGE - 2, EDGE - 1) for p in parts]
    q_tile = jnp.concatenate(q_list + [jnp.zeros((EDGE - len(q_list), LANE), jnp.float32)], 0)
    for kz, out_ref in enumerate(outs):
        k0, k1, v0, v1 = [e_buf[i, :, cols[kz]].astype(jnp.float32) for i in range(len(sources))]
        own_k, next_k = edge_rows(k0, k1)
        own_v, next_v = edge_rows(v0, v1)
        edge = jnp.concatenate(own_k + own_v + next_k + next_v, 0)
        out_ref[edge_at] = edge.astype(out_ref.dtype)
        if kz < 2:
            out_ref[edge_at + 1] = q_tile.astype(out_ref.dtype)


def lead(q, k, v, f, groups):
    rows, width = f.shape
    tile = (width // groups, LANE)
    edge_at = X_SIZE * 2 * AHEAD
    return pl.pallas_call(
        lead_kernel,
        in_specs=[HBM] * 4,
        out_shape=tuple(
            pltpu.VMEM((edge_at + (2 if kz < 2 else 1), *tile), f.dtype) for kz in range(Z_SIZE)
        ),
        scratch_shapes=[
            pltpu.VMEM((AHEAD * LANE, width), f.dtype),
            pltpu.VMEM((5, EDGE, width), f.dtype),
            pltpu.SemaphoreType.DMA((AHEAD,)),
            pltpu.SemaphoreType.DMA((5,)),
        ],
        cost_estimate=cost(10),
        compiler_params=params(60),
    )(q, k, v, f)


def coef_kernel(taps_ref, skip_ref, taps_out, skip_out, turned):
    depth = skip_out.shape[0]
    me = lax.axis_index("seq")
    per = LANE // depth
    cols = pl.ds(pl.multiple_of(me // per * LANE, LANE), LANE)
    k, v = taps_ref[1, :, cols], taps_ref[2, :, cols]

    def pairs(w, order):
        return [w[i : i + 1] for i in order for _ in range(2)]

    rows = pairs(k, (0, 1)) + pairs(v, (0, 1)) + pairs(k, (1, 2)) + pairs(v, (1, 2))
    zeros = jnp.zeros((LANE - len(rows), LANE), jnp.float32)
    mine = pl.ds(pl.multiple_of(me % per * depth, depth), depth)
    turned[...] = jnp.concatenate(rows + [zeros], 0).T
    taps_out[...] = turned[mine, :]
    turned[...] = jnp.broadcast_to(skip_ref[:, cols], (LANE, LANE)).T
    skip_out[...] = turned[mine, :]


def coefficients(taps, skip, depth):
    shape = jax.ShapeDtypeStruct((depth, LANE), jnp.float32)
    return pl.pallas_call(
        coef_kernel,
        out_shape=(shape, shape),
        scratch_shapes=[pltpu.VMEM((LANE, LANE), jnp.float32)],
        compiler_params=params(4),
    )(taps, skip[None, :])


def put_turned(out_ref, j, block):
    depth = out_ref.shape[2]
    per = LANE // depth
    for g in range(block.shape[1] // LANE):
        turned = block[:, g * LANE : (g + 1) * LANE].T
        out_ref[g * per : (g + 1) * per, j] = turned.reshape(per, depth, LANE).astype(out_ref.dtype)


def query_tiles(d):
    return {1: 1, 3: 2}.get(d, 0)


def pack_kernel(*refs):
    ins, outs, turned = refs[:Z_SIZE], refs[Z_SIZE:-1], refs[-1]
    last = X_SIZE * 2 * AHEAD
    depth = ins[0].shape[1]
    edges = [in_ref[last].astype(jnp.float32) for in_ref in ins]
    zeros = jnp.zeros((LANE - Z_SIZE * depth, LANE), jnp.float32)
    turned[...] = jnp.concatenate(edges + [zeros], 0).T
    _, x, c = place()
    for d, out_ref in enumerate(outs):
        for kz, in_ref in enumerate(ins):
            out_ref[kz * AHEAD : (kz + 1) * AHEAD] = in_ref[d * AHEAD : (d + 1) * AHEAD]
        at = ((x + d // 2) % X_SIZE * 2 + (c + d) % 2) * depth
        out_ref[Z_SIZE * AHEAD] = turned[pl.ds(pl.multiple_of(at, depth), depth), :].astype(out_ref.dtype)
        for i in range(query_tiles(d)):
            out_ref[Z_SIZE * AHEAD + 1 + i] = ins[i][last + 1]


def pack(parts):
    tile, dtype = parts[0].shape[1:], parts[0].dtype
    return pl.pallas_call(
        pack_kernel,
        out_shape=tuple(
            jax.ShapeDtypeStruct((Z_SIZE * AHEAD + 1 + query_tiles(d), *tile), dtype) for d in range(X_SIZE * 2)
        ),
        scratch_shapes=[pltpu.VMEM((LANE, LANE), jnp.float32)],
        cost_estimate=cost(20),
        compiler_params=params(6),
    )(*parts)


def shift(block, dz, dx, dc):
    route = []
    for z in range(Z_SIZE):
        for x in range(X_SIZE):
            for c in range(2):
                to = ((z + dz) % Z_SIZE * X_SIZE + (x + dx) % X_SIZE) * 2 + (c + dc) % 2
                route.append(((z * X_SIZE + x) * 2 + c, to))
    return lax.ppermute(block, "seq", route)


def spread(parts):
    parts = [parts[0]] + [shift(parts[k], k, 0, 0) for k in range(1, Z_SIZE)]
    parts = pack(parts)
    return [parts[0]] + [shift(parts[d], 0, d // 2, d % 2) for d in range(1, X_SIZE * 2)]


def taps_of(ext_ref, taps, start, size):
    return (
        taps[0:1, :] * ext_ref[start + 8 : start + 8 + size, :]
        + taps[1:2, :] * ext_ref[start + 7 : start + 7 + size, :]
        + taps[2:3, :] * ext_ref[start + 6 : start + 6 + size, :]
    )


def product_kernel(k_ref, v_ref, f_ref, taps_ref, out_ref, k_ext, v_ext, out_buf, sem):
    slabs = k_ref.shape[0] // LANE
    copies = []

    def put(j, block):
        put_turned(out_buf, j, block)
        copies.append(send(out_buf.at[:, j], out_ref.at[:, j], sem.at[j]))

    for j in range(AHEAD, slabs):
        put(slabs + j - AHEAD, f_ref[j * LANE : (j + 1) * LANE, :].astype(jnp.float32))
    zero = jnp.zeros((8, k_ref.shape[1]), jnp.float32)
    k_ext[0:8, :] = zero
    v_ext[0:8, :] = zero
    for j in range(slabs):
        rows, ext = slice(j * LANE, (j + 1) * LANE), slice(8 + j * LANE, 8 + (j + 1) * LANE)
        k_ext[ext, :] = k_ref[rows, :].astype(jnp.float32)
        v_ext[ext, :] = v_ref[rows, :].astype(jnp.float32)
        kf = taps_of(k_ext, taps_ref[1], j * LANE, LANE)
        vf = taps_of(v_ext, taps_ref[2], j * LANE, LANE)
        put(j, kf * vf)
    wait_all(copies)


def product(k, v, f, taps, groups):
    rows, width = k.shape
    ext = pltpu.VMEM((rows + 8, width), jnp.float32)
    slabs = rows // LANE * 2 - AHEAD
    shape = jax.ShapeDtypeStruct((groups, slabs, width // groups, LANE), k.dtype)
    return pl.pallas_call(
        product_kernel,
        in_specs=[VMEM] * 4,
        out_specs=HBM,
        out_shape=shape,
        scratch_shapes=[ext, ext, pltpu.VMEM(shape.shape, shape.dtype), pltpu.SemaphoreType.DMA((slabs,))],
        cost_estimate=cost(20),
        compiler_params=params(12),
    )(k, v, f, taps)


def gate_kernel(q_ref, core_ref, step_ref, taps_ref, out_ref, q_ext):
    rows, width = q_ref.shape
    z, x, c = place()
    at = Z_SIZE * AHEAD + 1
    tiles = [core_ref[at], step_ref[at], step_ref[at + 1]]
    core, step, round_z = [t.astype(jnp.float32) for t in tiles]
    halo = jnp.where(c == 1, core, jnp.where(x > 0, step, jnp.where(z > 0, round_z, 0.0)))
    parts = width // LANE
    for r in range(2):
        for g in range(parts):
            i = r * parts + g
            q_ext[6 + r : 7 + r, g * LANE : (g + 1) * LANE] = halo[i : i + 1]
    q_ext[8 : 8 + rows, :] = q_ref[...].astype(jnp.float32)
    for j in range(rows // LANE):
        qf = taps_of(q_ext, taps_ref[0], j * LANE, LANE)
        out_ref[j * LANE : (j + 1) * LANE, :] = qf.astype(out_ref.dtype)


def gate(q, core, step, taps):
    rows, width = q.shape
    return pl.pallas_call(
        gate_kernel,
        out_shape=jax.ShapeDtypeStruct(q.shape, q.dtype),
        scratch_shapes=[pltpu.VMEM((rows + 8, width), jnp.float32)],
        compiler_params=params(8),
    )(q, core, step, taps)


def mix(table, data):
    return jnp.dot(table, data, preferred_element_type=jnp.float32)


def mend(u_wide, edges, taps):
    depth = taps.shape[0]
    rows = edges.shape[0] - depth
    lane = lax.broadcasted_iota(jnp.int32, (rows, LANE), 1)
    sources = rows // depth
    weights = jnp.broadcast_to(taps[...][None], (sources, depth, LANE)).reshape(rows, LANE)
    terms = jnp.where(lane < 8, edges[depth:, :], edges[:rows, :]) * weights

    def after(x, steps):
        return pltpu.roll(x, LANE - steps, 1)

    terms = terms + after(terms, 2)
    terms = terms + after(terms, 8)
    fixed = (terms * after(terms, 4)).astype(jnp.bfloat16).astype(jnp.float32)
    size = u_wide.shape[0] // sources
    for i in range(sources):
        part, at = slice(i * depth, (i + 1) * depth), slice(i * size, i * size + depth)
        u_wide[at, :] = jnp.where(lane[part] < 2, fixed[part], u_wide[at, :])


def conv_kernel(u_ref, after_ref, taps_ref, skip_ref, t1, t2, t2_inv, t1_inv, tw_c, tw_s, *rest):
    f_refs, (y_ref, u_wide, f_wide, y_wide, edges) = rest[:-5], rest[-5:]
    depth = skip_ref.shape[0]
    edges[:depth, :] = jnp.zeros((depth, LANE), jnp.float32)
    z, x, c = place()
    sources = u_ref.shape[0]
    size = u_wide.shape[0] // sources
    ahead = AHEAD * depth
    for i in range(sources):
        both = u_ref[i].astype(jnp.float32).reshape(-1, LANE)
        u_wide[i * size : (i + 1) * size, :] = both[:size]
        if ahead < size:
            f_wide[i * size + ahead : (i + 1) * size, :] = both[size:]
    for d, f_ref in enumerate(f_refs):
        edge = f_ref[Z_SIZE * AHEAD].astype(jnp.float32)
        for kz in range(Z_SIZE):
            src = ((z - kz + Z_SIZE) % Z_SIZE * X_SIZE + (x - d // 2 + X_SIZE) % X_SIZE) * 2 + (c + d) % 2
            row = pl.multiple_of(src * size, size)
            tiles = f_ref[kz * AHEAD : (kz + 1) * AHEAD].reshape(ahead, LANE)
            f_wide[pl.ds(row, ahead), :] = tiles.astype(jnp.float32)
            row = pl.multiple_of((src + 1) * depth, depth)
            edges[pl.ds(row, depth), :] = pltpu.roll(edge, LANE - kz * depth, 1) if kz else edge
    low = jnp.bfloat16

    def part(x, i):
        return x[:, i * LANE : (i + 1) * LANE]

    def spectra(wide, rows):
        data = [wide[r, :].astype(low) for r in rows]
        first = mix(t1[...], jnp.concatenate(data, 1))
        turned = []
        for i in range(len(rows)):
            re, im = part(first[:LANE], i), part(first[LANE:], i)
            c, s = tw_c[...], tw_s[...]
            turned.append(jnp.concatenate([re * c - im * s, re * s + im * c], 1).astype(low))
        return mix(jnp.concatenate(turned, 0), t2[...])

    for start in range(0, depth, GROUP):
        rows = [pl.ds(ch, LANE, stride=depth) for ch in range(start, start + GROUP)]
        f_spec = spectra(f_wide, rows)
        if start == 0:
            mend(u_wide, edges, taps_ref)
        u_spec = spectra(u_wide, rows)
        prod = []
        for i in range(GROUP):
            a, b = u_spec[i * LANE : (i + 1) * LANE], f_spec[i * LANE : (i + 1) * LANE]
            ar, ai, br, bi = a[:, :LANE], a[:, LANE:], b[:, :LANE], b[:, LANE:]
            prod.append(jnp.concatenate([ar * br - ai * bi, ar * bi + ai * br], 1).astype(low))
        back = mix(jnp.concatenate(prod, 0), t2_inv[...])
        cols = []
        for i in range(GROUP):
            v = back[i * LANE : (i + 1) * LANE]
            re, im = v[:, :LANE], v[:, LANE:]
            c, s = tw_c[...], tw_s[...]
            cols.append(jnp.concatenate([re * c + im * s, im * c - re * s], 0).astype(low))
        conv = mix(t1_inv[...], jnp.concatenate(cols, 1))
        for i, r in enumerate(rows):
            y_wide[r, :] = part(conv, i)
    shape = (LANE, depth, LANE)
    y = y_wide[...].reshape(shape) + skip_ref[...][None] * u_wide[...].reshape(shape)
    y_ref[...] = y.reshape(y_ref.shape).astype(y_ref.dtype)


def long_conv(u, f, after, taps, skip):
    sources, slabs, depth, _ = u.shape
    slabs = (slabs + AHEAD) // 2
    flat = (sources * slabs * depth, LANE)
    wide = pltpu.VMEM(flat, jnp.float32)
    edges = pltpu.VMEM(((sources + 1) * depth, LANE), jnp.float32)
    operands = (u, after, taps, skip, *tables(), *f)
    y = pl.pallas_call(
        conv_kernel,
        in_specs=[HBM if x is after else VMEM for x in operands],
        out_shape=jax.ShapeDtypeStruct(flat, u.dtype),
        scratch_shapes=[wide] * 3 + [edges],
        compiler_params=params(40),
    )(*operands)
    return y.reshape(sources, slabs, depth, LANE)


def join_kernel(y_ref, qf_ref, stream_ref, gain_ref, out_ref, sum_ref, sq_ref):
    groups, slabs, depth, _ = y_ref.shape
    per = LANE // depth
    sq_ref[...] = jnp.zeros_like(sq_ref)
    for j in range(slabs):
        rows = slice(j * LANE, (j + 1) * LANE)
        squares = jnp.zeros((LANE, LANE), jnp.float32)
        for g in range(groups // per):
            cols = slice(g * LANE, (g + 1) * LANE)
            y = y_ref[g * per : (g + 1) * per, j].reshape(LANE, LANE).astype(jnp.float32).T
            gated = (qf_ref[rows, cols].astype(jnp.float32) * y).astype(jnp.bfloat16)
            summed = stream_ref[rows, cols].astype(jnp.float32) + gated.astype(jnp.float32)
            out_ref[rows, cols] = summed.astype(out_ref.dtype)
            sum_ref[rows, cols] = summed * gain_ref[:, cols]
            squares = squares + summed * summed
        total = jnp.sum(squares.T, axis=0, keepdims=True)
        sq_ref[j : j + 1, :] = total


def join(y, qf, stream, gain):
    return pl.pallas_call(
        join_kernel,
        in_specs=[VMEM] * 4,
        out_shape=(
            jax.ShapeDtypeStruct(stream.shape, stream.dtype),
            jax.ShapeDtypeStruct(stream.shape, jnp.float32),
            jax.ShapeDtypeStruct((8, LANE), jnp.float32),
        ),
        compiler_params=params(12),
    )(y, qf, stream, gain[None, :])


def norm_kernel(channels, low_ref, sum_ref, *rest):
    sq_refs, (low_out, out_ref, out_buf, low_sem, sem) = rest[:-5], rest[-5:]
    copies = [send(low_ref, low_out, low_sem)]
    squares = sum(ref[...] for ref in sq_refs)
    scale = 1.0 / jnp.sqrt(squares / channels + 1e-05)
    for j in range(out_ref.shape[0] // LANE):
        rows = slice(j * LANE, (j + 1) * LANE)
        column = jnp.broadcast_to(scale[j : j + 1, :], (LANE, LANE)).T
        for g in range(out_ref.shape[1] // LANE):
            cols = slice(g * LANE, (g + 1) * LANE)
            out_buf[rows, cols] = (sum_ref[rows, cols] * column).astype(out_buf.dtype)
        copies.append(send(out_buf.at[rows, :], out_ref.at[rows, :], sem.at[j]))
    wait_all(copies)


def norm(low, summed, squares, channels):

    def kernel(*refs):
        norm_kernel(channels, *refs)

    return pl.pallas_call(
        kernel,
        in_specs=[VMEM] * (2 + len(squares)),
        out_specs=(HBM,) * 2,
        out_shape=(jax.ShapeDtypeStruct(summed.shape, low.dtype),) * 2,
        scratch_shapes=[
            pltpu.VMEM(summed.shape, low.dtype),
            pltpu.SemaphoreType.DMA,
            pltpu.SemaphoreType.DMA((summed.shape[0] // LANE,)),
        ],
        compiler_params=params(8),
    )(low, summed, *squares)


def exchange(x, axis):
    return lax.all_to_all(x, axis, split_axis=0, concat_axis=0, tiled=True)


def across(block, fan, dz, dy):
    route = [(i, (i + dz) % fan // Y_SIZE * Y_SIZE + (i + dy) % Y_SIZE) for i in range(fan)]
    return lax.ppermute(block, "ch", route)


def shards(queries, keys, values, filters, short_weights, skip_gain, stream, norm_gain):
    groups = lax.axis_size("seq")
    fan = lax.axis_size("ch")
    rows, width = queries.shape
    slab = width // groups
    parts = lead(queries, keys, values, filters, groups)
    u_all = exchange(product(keys, values, filters, short_weights, groups), "seq")
    f_all = spread(parts)
    taps, skip = coefficients(short_weights, skip_gain, slab)
    qf = gate(queries, f_all[1], f_all[3], short_weights)
    y_home = exchange(long_conv(u_all, f_all, qf, taps, skip), "seq")
    low, summed, squares = join(y_home, qf, stream, norm_gain)
    squares = squares + across(squares, fan, Y_SIZE, 0)
    squares = [squares] + [across(squares, fan, 0, k) for k in range(1, Y_SIZE)]
    return norm(low, summed, squares, width * fan)


def solution(mesh):
    wide = P("seq", "ch")
    in_specs = (wide, wide, wide, wide, P(None, None, "ch"), P("ch"), wide, P("ch"))
    return jax.shard_map(shards, mesh=mesh, in_specs=in_specs, out_specs=(wide, wide), check_vma=False)
```

```python
import jax
import jax.numpy as jnp
import numpy as np
from jax import lax
from jax.experimental import pallas as pl
from jax.experimental.pallas import tpu as pltpu
from jax.sharding import PartitionSpec as P

LANE = 128
EDGE = 16
GROUP = 16
Z_SIZE = 4
X_SIZE = 4
AHEAD = 4
Y_SIZE = 4
MIB = 1024 * 1024


def params(mebibytes):
    return pltpu.CompilerParams(vmem_limit_bytes=mebibytes * MIB)


def cost(micros):
    return pl.CostEstimate(flops=int(micros * 1e9), bytes_accessed=0, transcendentals=0)


def tables():
    n = LANE * LANE
    a = np.arange(LANE, dtype=np.float64)
    first = -2.0 * np.pi * np.outer(a + 0.25, a) / LANE
    twist = -2.0 * np.pi * np.outer(a + 0.25, a) / n
    second = -2.0 * np.pi * np.outer(a, a) / LANE
    t1 = np.concatenate([np.cos(first), np.sin(first)], 0)
    cos2, sin2 = np.cos(second), np.sin(second)
    t2 = np.block([[cos2, sin2], [-sin2, cos2]])
    t2_inv = np.block([[cos2, -sin2], [sin2, cos2]])
    t1_inv = np.concatenate([np.cos(first).T, np.sin(first).T], 1) / n
    return [jnp.asarray(t, jnp.bfloat16) for t in (t1, t2, t2_inv, t1_inv, np.cos(twist), np.sin(twist))]


def place():
    me = lax.axis_index("seq")
    return me // (X_SIZE * 2), me // 2 % X_SIZE, me % 2


HBM = pl.BlockSpec(memory_space=pl.ANY)
VMEM = pl.BlockSpec(memory_space=pltpu.VMEM)


def send(source, target, sem):
    copy = pltpu.make_async_copy(source, target, sem)
    copy.start()
    return copy


def wait_all(copies):
    for copy in copies:
        copy.wait()


def edge_rows(first, last):
    zero = jnp.zeros_like(first[:1])
    own = [first[0:1], first[1:2], zero, first[0:1]]
    passed = [last[EDGE - 1 :], zero, last[EDGE - 2 : EDGE - 1], last[EDGE - 1 :]]
    return own, passed


def lead_kernel(q_ref, k_ref, v_ref, f_ref, *rest):
    outs, (f_buf, e_buf, f_sem, e_sem) = rest[:Z_SIZE], rest[Z_SIZE:]
    rows = f_ref.shape[0]
    head, tail = pl.ds(0, EDGE), pl.ds(rows - EDGE, EDGE)
    pieces = [pl.ds(j * LANE, LANE) for j in range(AHEAD)]
    f_copies = [send(f_ref.at[p, :], f_buf.at[p, :], f_sem.at[j]) for j, p in enumerate(pieces)]
    sources = [k_ref.at[head, :], k_ref.at[tail, :], v_ref.at[head, :], v_ref.at[tail, :]]
    e_copies = [send(x, e_buf.at[i], e_sem.at[i]) for i, x in enumerate(sources + [q_ref.at[tail, :]])]
    z, x, c = place()
    depth = outs[0].shape[1]
    cols = [pl.ds(pl.multiple_of((z + kz) % Z_SIZE * LANE, LANE), LANE) for kz in range(Z_SIZE)]
    for j, p in enumerate(pieces):
        f_copies[j].wait()
        for kz, out_ref in enumerate(outs):
            turned = f_buf[p, cols[kz]].astype(jnp.float32).T.astype(out_ref.dtype)
            for d in range(X_SIZE * 2):
                to = (d // 2 - x + X_SIZE) % X_SIZE * 2 + (d % 2 - c + 2) % 2
                out_ref[to * AHEAD + j] = turned[d * depth : (d + 1) * depth]
    wait_all(e_copies)
    edge_at = X_SIZE * 2 * AHEAD
    q_rows = e_buf[len(sources)].astype(jnp.float32)
    parts = [slice(g * LANE, (g + 1) * LANE) for g in range(q_rows.shape[1] // LANE)]
    q_list = [q_rows[r : r + 1, p] for r in (EDGE - 2, EDGE - 1) for p in parts]
    q_tile = jnp.concatenate(q_list + [jnp.zeros((EDGE - len(q_list), LANE), jnp.float32)], 0)
    for kz, out_ref in enumerate(outs):
        k0, k1, v0, v1 = [e_buf[i, :, cols[kz]].astype(jnp.float32) for i in range(len(sources))]
        own_k, next_k = edge_rows(k0, k1)
        own_v, next_v = edge_rows(v0, v1)
        edge = jnp.concatenate(own_k + own_v + next_k + next_v, 0)
        out_ref[edge_at] = edge.astype(out_ref.dtype)
        if kz < 2:
            out_ref[edge_at + 1] = q_tile.astype(out_ref.dtype)


def lead(q, k, v, f, groups):
    rows, width = f.shape
    tile = (width // groups, LANE)
    edge_at = X_SIZE * 2 * AHEAD
    return pl.pallas_call(
        lead_kernel,
        in_specs=[HBM] * 4,
        out_shape=tuple(
            pltpu.VMEM((edge_at + (2 if kz < 2 else 1), *tile), f.dtype) for kz in range(Z_SIZE)
        ),
        scratch_shapes=[
            pltpu.VMEM((AHEAD * LANE, width), f.dtype),
            pltpu.VMEM((5, EDGE, width), f.dtype),
            pltpu.SemaphoreType.DMA((AHEAD,)),
            pltpu.SemaphoreType.DMA((5,)),
        ],
        cost_estimate=cost(10),
        compiler_params=params(60),
    )(q, k, v, f)


def coef_kernel(taps_ref, skip_ref, taps_out, skip_out, turned):
    depth = skip_out.shape[0]
    me = lax.axis_index("seq")
    per = LANE // depth
    cols = pl.ds(pl.multiple_of(me // per * LANE, LANE), LANE)
    k, v = taps_ref[1, :, cols], taps_ref[2, :, cols]

    def pairs(w, order):
        return [w[i : i + 1] for i in order for _ in range(2)]

    rows = pairs(k, (0, 1)) + pairs(v, (0, 1)) + pairs(k, (1, 2)) + pairs(v, (1, 2))
    zeros = jnp.zeros((LANE - len(rows), LANE), jnp.float32)
    mine = pl.ds(pl.multiple_of(me % per * depth, depth), depth)
    turned[...] = jnp.concatenate(rows + [zeros], 0).T
    taps_out[...] = turned[mine, :]
    turned[...] = jnp.broadcast_to(skip_ref[:, cols], (LANE, LANE)).T
    skip_out[...] = turned[mine, :]


def coefficients(taps, skip, depth):
    shape = jax.ShapeDtypeStruct((depth, LANE), jnp.float32)
    return pl.pallas_call(
        coef_kernel,
        out_shape=(shape, shape),
        scratch_shapes=[pltpu.VMEM((LANE, LANE), jnp.float32)],
        compiler_params=params(4),
    )(taps, skip[None, :])


def put_turned(out_ref, j, block):
    depth = out_ref.shape[2]
    per = LANE // depth
    for g in range(block.shape[1] // LANE):
        turned = block[:, g * LANE : (g + 1) * LANE].T
        out_ref[g * per : (g + 1) * per, j] = turned.reshape(per, depth, LANE).astype(out_ref.dtype)


def step_x(step, core):
    return jnp.where(core == 0, step, (X_SIZE - step) % X_SIZE)


def query_tiles(d):
    return {1: 1, 7: 2}.get(d, 0)


def pack_kernel(*refs):
    ins, outs, turned = refs[:Z_SIZE], refs[Z_SIZE:-1], refs[-1]
    last = X_SIZE * 2 * AHEAD
    depth = ins[0].shape[1]
    edges = [in_ref[last].astype(jnp.float32) for in_ref in ins]
    zeros = jnp.zeros((LANE - Z_SIZE * depth, LANE), jnp.float32)
    turned[...] = jnp.concatenate(edges + [zeros], 0).T
    _, x, c = place()
    for d, out_ref in enumerate(outs):
        kx = step_x(d // 2, c)
        for kz, in_ref in enumerate(ins):
            out_ref[kz * AHEAD : (kz + 1) * AHEAD] = in_ref[pl.ds((kx * 2 + d % 2) * AHEAD, AHEAD)]
        at = ((x + kx) % X_SIZE * 2 + (c + d) % 2) * depth
        out_ref[Z_SIZE * AHEAD] = turned[pl.ds(pl.multiple_of(at, depth), depth), :].astype(out_ref.dtype)
        for i in range(query_tiles(d)):
            out_ref[Z_SIZE * AHEAD + 1 + i] = ins[i][last + 1]


def pack(parts):
    tile, dtype = parts[0].shape[1:], parts[0].dtype
    return pl.pallas_call(
        pack_kernel,
        out_shape=tuple(
            jax.ShapeDtypeStruct((Z_SIZE * AHEAD + 1 + query_tiles(d), *tile), dtype) for d in range(X_SIZE * 2)
        ),
        scratch_shapes=[pltpu.VMEM((LANE, LANE), jnp.float32)],
        cost_estimate=cost(20),
        compiler_params=params(6),
    )(*parts)


def seq_index(z, x, c):
    return (z % Z_SIZE * X_SIZE + x % X_SIZE) * 2 + c % 2


def moved(block, target):
    places = [(z, x, c) for z in range(Z_SIZE) for x in range(X_SIZE) for c in range(2)]
    return lax.ppermute(block, "seq", [(seq_index(*p), seq_index(*target(*p))) for p in places])


def along_z(block, dz):
    return moved(block, lambda z, x, c: (z + dz, x, c))


def cross(block, step, dc):
    return moved(block, lambda z, x, c: (z, x + step * (1 - 2 * c), c + dc))


def spread(parts):
    parts = [parts[0]] + [along_z(parts[k], k) for k in range(1, Z_SIZE)]
    parts = pack(parts)
    return [parts[0]] + [cross(parts[d], d // 2, d % 2) for d in range(1, X_SIZE * 2)]


def taps_of(ext_ref, taps, start, size):
    return (
        taps[0:1, :] * ext_ref[start + 8 : start + 8 + size, :]
        + taps[1:2, :] * ext_ref[start + 7 : start + 7 + size, :]
        + taps[2:3, :] * ext_ref[start + 6 : start + 6 + size, :]
    )


def product_kernel(k_ref, v_ref, f_ref, taps_ref, out_ref, k_ext, v_ext, out_buf, sem):
    slabs = k_ref.shape[0] // LANE
    copies = []

    def put(j, block):
        put_turned(out_buf, j, block)
        copies.append(send(out_buf.at[:, j], out_ref.at[:, j], sem.at[j]))

    for j in range(AHEAD, slabs):
        put(slabs + j - AHEAD, f_ref[j * LANE : (j + 1) * LANE, :].astype(jnp.float32))
    zero = jnp.zeros((8, k_ref.shape[1]), jnp.float32)
    k_ext[0:8, :] = zero
    v_ext[0:8, :] = zero
    for j in range(slabs):
        rows, ext = slice(j * LANE, (j + 1) * LANE), slice(8 + j * LANE, 8 + (j + 1) * LANE)
        k_ext[ext, :] = k_ref[rows, :].astype(jnp.float32)
        v_ext[ext, :] = v_ref[rows, :].astype(jnp.float32)
        kf = taps_of(k_ext, taps_ref[1], j * LANE, LANE)
        vf = taps_of(v_ext, taps_ref[2], j * LANE, LANE)
        put(j, kf * vf)
    wait_all(copies)


def product(k, v, f, taps, groups):
    rows, width = k.shape
    ext = pltpu.VMEM((rows + 8, width), jnp.float32)
    slabs = rows // LANE * 2 - AHEAD
    shape = jax.ShapeDtypeStruct((groups, slabs, width // groups, LANE), k.dtype)
    return pl.pallas_call(
        product_kernel,
        in_specs=[VMEM] * 4,
        out_specs=HBM,
        out_shape=shape,
        scratch_shapes=[ext, ext, pltpu.VMEM(shape.shape, shape.dtype), pltpu.SemaphoreType.DMA((slabs,))],
        cost_estimate=cost(20),
        compiler_params=params(12),
    )(k, v, f, taps)


def gate_kernel(q_ref, core_ref, step_ref, taps_ref, out_ref, q_ext):
    rows, width = q_ref.shape
    z, x, c = place()
    at = Z_SIZE * AHEAD + 1
    tiles = [core_ref[at], step_ref[at], step_ref[at + 1]]
    core, step, round_z = [t.astype(jnp.float32) for t in tiles]
    halo = jnp.where(c == 1, core, jnp.where(x > 0, step, jnp.where(z > 0, round_z, 0.0)))
    parts = width // LANE
    for r in range(2):
        for g in range(parts):
            i = r * parts + g
            q_ext[6 + r : 7 + r, g * LANE : (g + 1) * LANE] = halo[i : i + 1]
    q_ext[8 : 8 + rows, :] = q_ref[...].astype(jnp.float32)
    for j in range(rows // LANE):
        qf = taps_of(q_ext, taps_ref[0], j * LANE, LANE)
        out_ref[j * LANE : (j + 1) * LANE, :] = qf.astype(out_ref.dtype)


def gate(q, core, step, taps):
    rows, width = q.shape
    return pl.pallas_call(
        gate_kernel,
        out_shape=jax.ShapeDtypeStruct(q.shape, q.dtype),
        scratch_shapes=[pltpu.VMEM((rows + 8, width), jnp.float32)],
        compiler_params=params(8),
    )(q, core, step, taps)


def mix(table, data):
    return jnp.dot(table, data, preferred_element_type=jnp.float32)


def mend(u_wide, edges, taps):
    depth = taps.shape[0]
    rows = edges.shape[0] - depth
    lane = lax.broadcasted_iota(jnp.int32, (rows, LANE), 1)
    sources = rows // depth
    weights = jnp.broadcast_to(taps[...][None], (sources, depth, LANE)).reshape(rows, LANE)
    terms = jnp.where(lane < 8, edges[depth:, :], edges[:rows, :]) * weights

    def after(x, steps):
        return pltpu.roll(x, LANE - steps, 1)

    terms = terms + after(terms, 2)
    terms = terms + after(terms, 8)
    fixed = (terms * after(terms, 4)).astype(jnp.bfloat16).astype(jnp.float32)
    size = u_wide.shape[0] // sources
    for i in range(sources):
        part, at = slice(i * depth, (i + 1) * depth), slice(i * size, i * size + depth)
        u_wide[at, :] = jnp.where(lane[part] < 2, fixed[part], u_wide[at, :])


def conv_kernel(u_ref, after_ref, taps_ref, skip_ref, t1, t2, t2_inv, t1_inv, tw_c, tw_s, *rest):
    f_refs, (y_ref, u_wide, f_wide, y_wide, edges) = rest[:-5], rest[-5:]
    depth = skip_ref.shape[0]
    edges[:depth, :] = jnp.zeros((depth, LANE), jnp.float32)
    z, x, c = place()
    sources = u_ref.shape[0]
    size = u_wide.shape[0] // sources
    ahead = AHEAD * depth
    for i in range(sources):
        both = u_ref[i].astype(jnp.float32).reshape(-1, LANE)
        u_wide[i * size : (i + 1) * size, :] = both[:size]
        if ahead < size:
            f_wide[i * size + ahead : (i + 1) * size, :] = both[size:]
    for d, f_ref in enumerate(f_refs):
        core = (c + d) % 2
        kx = step_x(d // 2, core)
        edge = f_ref[Z_SIZE * AHEAD].astype(jnp.float32)
        for kz in range(Z_SIZE):
            src = ((z - kz + Z_SIZE) % Z_SIZE * X_SIZE + (x - kx + X_SIZE) % X_SIZE) * 2 + core
            row = pl.multiple_of(src * size, size)
            tiles = f_ref[kz * AHEAD : (kz + 1) * AHEAD].reshape(ahead, LANE)
            f_wide[pl.ds(row, ahead), :] = tiles.astype(jnp.float32)
            row = pl.multiple_of((src + 1) * depth, depth)
            edges[pl.ds(row, depth), :] = pltpu.roll(edge, LANE - kz * depth, 1) if kz else edge
    low = jnp.bfloat16

    def part(x, i):
        return x[:, i * LANE : (i + 1) * LANE]

    def spectra(wide, rows):
        data = [wide[r, :].astype(low) for r in rows]
        first = mix(t1[...], jnp.concatenate(data, 1))
        turned = []
        for i in range(len(rows)):
            re, im = part(first[:LANE], i).astype(low), part(first[LANE:], i).astype(low)
            c, s = tw_c[...], tw_s[...]
            turned.append(jnp.concatenate([re * c - im * s, re * s + im * c], 1))
        return mix(jnp.concatenate(turned, 0), t2[...])

    for start in range(0, depth, GROUP):
        rows = [pl.ds(ch, LANE, stride=depth) for ch in range(start, start + GROUP)]
        f_spec = spectra(f_wide, rows)
        if start == 0:
            mend(u_wide, edges, taps_ref)
        u_spec = spectra(u_wide, rows)
        prod = []
        for i in range(GROUP):
            a, b = u_spec[i * LANE : (i + 1) * LANE], f_spec[i * LANE : (i + 1) * LANE]
            ar, ai, br, bi = a[:, :LANE], a[:, LANE:], b[:, :LANE], b[:, LANE:]
            prod.append(jnp.concatenate([ar * br - ai * bi, ar * bi + ai * br], 1).astype(low))
        back = mix(jnp.concatenate(prod, 0), t2_inv[...])
        cols = []
        for i in range(GROUP):
            v = back[i * LANE : (i + 1) * LANE]
            re, im = v[:, :LANE].astype(low), v[:, LANE:].astype(low)
            c, s = tw_c[...], tw_s[...]
            cols.append(jnp.concatenate([re * c + im * s, im * c - re * s], 0))
        conv = mix(t1_inv[...], jnp.concatenate(cols, 1))
        for i, r in enumerate(rows):
            y_wide[r, :] = part(conv, i)
    shape = (LANE, depth, LANE)
    y = y_wide[...].reshape(shape) + skip_ref[...][None] * u_wide[...].reshape(shape)
    y_ref[...] = y.reshape(y_ref.shape).astype(y_ref.dtype)


def long_conv(u, f, after, taps, skip):
    sources, slabs, depth, _ = u.shape
    slabs = (slabs + AHEAD) // 2
    flat = (sources * slabs * depth, LANE)
    wide = pltpu.VMEM(flat, jnp.float32)
    edges = pltpu.VMEM(((sources + 1) * depth, LANE), jnp.float32)
    operands = (u, after, taps, skip, *tables(), *f)
    y = pl.pallas_call(
        conv_kernel,
        in_specs=[HBM if x is after else VMEM for x in operands],
        out_shape=jax.ShapeDtypeStruct(flat, u.dtype),
        scratch_shapes=[wide] * 3 + [edges],
        compiler_params=params(40),
    )(*operands)
    return y.reshape(sources, slabs, depth, LANE)


def join_kernel(y_ref, qf_ref, stream_ref, gain_ref, out_ref, sum_ref, sq_ref):
    groups, slabs, depth, _ = y_ref.shape
    per = LANE // depth
    sq_ref[...] = jnp.zeros_like(sq_ref)
    for j in range(slabs):
        rows = slice(j * LANE, (j + 1) * LANE)
        squares = jnp.zeros((LANE, LANE), jnp.float32)
        for g in range(groups // per):
            cols = slice(g * LANE, (g + 1) * LANE)
            y = y_ref[g * per : (g + 1) * per, j].reshape(LANE, LANE).astype(jnp.float32).T
            gated = (qf_ref[rows, cols].astype(jnp.float32) * y).astype(jnp.bfloat16)
            summed = stream_ref[rows, cols].astype(jnp.float32) + gated.astype(jnp.float32)
            out_ref[rows, cols] = summed.astype(out_ref.dtype)
            sum_ref[rows, cols] = summed * gain_ref[:, cols]
            squares = squares + summed * summed
        total = jnp.sum(squares.T, axis=0, keepdims=True)
        sq_ref[j : j + 1, :] = total


def join(y, qf, stream, gain):
    return pl.pallas_call(
        join_kernel,
        in_specs=[VMEM] * 4,
        out_shape=(
            jax.ShapeDtypeStruct(stream.shape, stream.dtype),
            jax.ShapeDtypeStruct(stream.shape, jnp.float32),
            jax.ShapeDtypeStruct((8, LANE), jnp.float32),
        ),
        compiler_params=params(12),
    )(y, qf, stream, gain[None, :])


def norm_kernel(channels, low_ref, sum_ref, *rest):
    sq_refs, (low_out, out_ref, out_buf, low_sem, sem) = rest[:-5], rest[-5:]
    copies = [send(low_ref, low_out, low_sem)]
    squares = sum(ref[...] for ref in sq_refs)
    scale = 1.0 / jnp.sqrt(squares / channels + 1e-05)
    for j in range(out_ref.shape[0] // LANE):
        rows = slice(j * LANE, (j + 1) * LANE)
        column = jnp.broadcast_to(scale[j : j + 1, :], (LANE, LANE)).T
        for g in range(out_ref.shape[1] // LANE):
            cols = slice(g * LANE, (g + 1) * LANE)
            out_buf[rows, cols] = (sum_ref[rows, cols] * column).astype(out_buf.dtype)
        copies.append(send(out_buf.at[rows, :], out_ref.at[rows, :], sem.at[j]))
    wait_all(copies)


def norm(low, summed, squares, channels):

    def kernel(*refs):
        norm_kernel(channels, *refs)

    return pl.pallas_call(
        kernel,
        in_specs=[VMEM] * (2 + len(squares)),
        out_specs=(HBM,) * 2,
        out_shape=(jax.ShapeDtypeStruct(summed.shape, low.dtype),) * 2,
        scratch_shapes=[
            pltpu.VMEM(summed.shape, low.dtype),
            pltpu.SemaphoreType.DMA,
            pltpu.SemaphoreType.DMA((summed.shape[0] // LANE,)),
        ],
        compiler_params=params(8),
    )(low, summed, *squares)


def exchange(x, axis):
    return lax.all_to_all(x, axis, split_axis=0, concat_axis=0, tiled=True)


def across(block, fan, dz, dy):
    route = [(i, (i + dz) % fan // Y_SIZE * Y_SIZE + (i + dy) % Y_SIZE) for i in range(fan)]
    return lax.ppermute(block, "ch", route)


def shards(queries, keys, values, filters, short_weights, skip_gain, stream, norm_gain):
    groups = lax.axis_size("seq")
    fan = lax.axis_size("ch")
    rows, width = queries.shape
    slab = width // groups
    parts = lead(queries, keys, values, filters, groups)
    u_all = exchange(product(keys, values, filters, short_weights, groups), "seq")
    f_all = spread(parts)
    taps, skip = coefficients(short_weights, skip_gain, slab)
    qf = gate(queries, f_all[1], f_all[7], short_weights)
    y_home = exchange(long_conv(u_all, f_all, qf, taps, skip), "seq")
    low, summed, squares = join(y_home, qf, stream, norm_gain)
    squares = squares + across(squares, fan, Y_SIZE, 0)
    squares = [squares] + [across(squares, fan, 0, k) for k in range(1, Y_SIZE)]
    return norm(low, summed, squares, width * fan)


def solution(mesh):
    wide = P("seq", "ch")
    in_specs = (wide, wide, wide, wide, P(None, None, "ch"), P("ch"), wide, P("ch"))
    return jax.shard_map(shards, mesh=mesh, in_specs=in_specs, out_specs=(wide, wide), check_vma=False)
```

```python
import jax
import jax.numpy as jnp
import numpy as np
from jax import lax
from jax.experimental import pallas as pl
from jax.experimental.pallas import tpu as pltpu
from jax.sharding import PartitionSpec as P

LANE = 128
EDGE = 16
GROUP = 16
Z_SIZE = 4
X_SIZE = 4
SLABS = 4
Y_SIZE = 4
MIB = 1024 * 1024


def params(mebibytes):
    return pltpu.CompilerParams(vmem_limit_bytes=mebibytes * MIB)


def cost(micros):
    return pl.CostEstimate(flops=int(micros * 1e9), bytes_accessed=0, transcendentals=0)


def tables():
    n = LANE * LANE
    a = np.arange(LANE, dtype=np.float64)
    first = -2.0 * np.pi * np.outer(a + 0.25, a) / LANE
    twist = -2.0 * np.pi * np.outer(a + 0.25, a) / n
    second = -2.0 * np.pi * np.outer(a, a) / LANE
    t1 = np.concatenate([np.cos(first), np.sin(first)], 0)
    cos2, sin2 = np.cos(second), np.sin(second)
    t2 = np.block([[cos2, sin2], [-sin2, cos2]])
    t2_inv = np.block([[cos2, -sin2], [sin2, cos2]])
    t1_inv = np.concatenate([np.cos(first).T, np.sin(first).T], 1) / n
    low = [jnp.asarray(t, jnp.bfloat16) for t in (t1, t2, t2_inv, t1_inv)]
    return (*low, jnp.asarray(np.cos(twist), jnp.float32), jnp.asarray(np.sin(twist), jnp.float32))


def place():
    me = lax.axis_index("seq")
    return me // (X_SIZE * 2), me // 2 % X_SIZE, me % 2


HBM = pl.BlockSpec(memory_space=pl.ANY)
VMEM = pl.BlockSpec(memory_space=pltpu.VMEM)


def send(source, target, sem):
    copy = pltpu.make_async_copy(source, target, sem)
    copy.start()
    return copy


def wait_all(copies):
    for copy in copies:
        copy.wait()


def edge_rows(first, last):
    zero = jnp.zeros_like(first[:1])
    own = [first[0:1], first[1:2], zero, first[0:1]]
    passed = [last[EDGE - 1 :], zero, last[EDGE - 2 : EDGE - 1], last[EDGE - 1 :]]
    return own, passed


def lead_kernel(q_ref, k_ref, v_ref, f_ref, *rest):
    outs, (f_buf, e_buf, f_sem, e_sem) = rest[:Z_SIZE], rest[Z_SIZE:]
    rows = f_ref.shape[0]
    head, tail = pl.ds(0, EDGE), pl.ds(rows - EDGE, EDGE)
    pieces = [pl.ds(j * LANE, LANE) for j in range(SLABS)]
    f_copies = [send(f_ref.at[p, :], f_buf.at[p, :], f_sem.at[j]) for j, p in enumerate(pieces)]
    sources = [k_ref.at[head, :], k_ref.at[tail, :], v_ref.at[head, :], v_ref.at[tail, :]]
    e_copies = [send(x, e_buf.at[i], e_sem.at[i]) for i, x in enumerate(sources + [q_ref.at[tail, :]])]
    z, x, c = place()
    depth = outs[0].shape[1]
    cols = [pl.ds(pl.multiple_of((z + kz) % Z_SIZE * LANE, LANE), LANE) for kz in range(Z_SIZE)]
    for j, p in enumerate(pieces):
        f_copies[j].wait()
        for kz, out_ref in enumerate(outs):
            turned = f_buf[p, cols[kz]].T
            for d in range(X_SIZE * 2):
                to = (d // 2 - x + X_SIZE) % X_SIZE * 2 + (d % 2 - c + 2) % 2
                out_ref[to * SLABS + j] = turned[d * depth : (d + 1) * depth]
    wait_all(e_copies)
    edge_at = X_SIZE * 2 * SLABS
    q_rows = e_buf[len(sources)].astype(jnp.float32)
    parts = [slice(g * LANE, (g + 1) * LANE) for g in range(q_rows.shape[1] // LANE)]
    q_list = [q_rows[r : r + 1, p] for r in (EDGE - 2, EDGE - 1) for p in parts]
    q_tile = jnp.concatenate(q_list + [jnp.zeros((EDGE - len(q_list), LANE), jnp.float32)], 0)
    for kz, out_ref in enumerate(outs):
        k0, k1, v0, v1 = [e_buf[i, :, cols[kz]].astype(jnp.float32) for i in range(len(sources))]
        own_k, next_k = edge_rows(k0, k1)
        own_v, next_v = edge_rows(v0, v1)
        edge = jnp.concatenate(own_k + own_v + next_k + next_v, 0)
        out_ref[edge_at] = edge.astype(out_ref.dtype)
        if kz < 2:
            out_ref[edge_at + 1] = q_tile.astype(out_ref.dtype)


def lead(q, k, v, f, groups):
    rows, width = f.shape
    tile = (width // groups, LANE)
    edge_at = X_SIZE * 2 * SLABS
    return pl.pallas_call(
        lead_kernel,
        in_specs=[HBM] * 4,
        out_shape=tuple(
            pltpu.VMEM((edge_at + (2 if kz < 2 else 1), *tile), f.dtype) for kz in range(Z_SIZE)
        ),
        scratch_shapes=[
            pltpu.VMEM((SLABS * LANE, width), f.dtype),
            pltpu.VMEM((5, EDGE, width), f.dtype),
            pltpu.SemaphoreType.DMA((SLABS,)),
            pltpu.SemaphoreType.DMA((5,)),
        ],
        cost_estimate=cost(10),
        compiler_params=params(60),
    )(q, k, v, f)


def coef_kernel(taps_ref, skip_ref, taps_out, skip_out, turned):
    depth = skip_out.shape[0]
    me = lax.axis_index("seq")
    per = LANE // depth
    cols = pl.ds(pl.multiple_of(me // per * LANE, LANE), LANE)
    k, v = taps_ref[1, :, cols], taps_ref[2, :, cols]

    def pairs(w, order):
        return [w[i : i + 1] for i in order for _ in range(2)]

    rows = pairs(k, (0, 1)) + pairs(v, (0, 1)) + pairs(k, (1, 2)) + pairs(v, (1, 2))
    zeros = jnp.zeros((LANE - len(rows), LANE), jnp.float32)
    mine = pl.ds(pl.multiple_of(me % per * depth, depth), depth)
    turned[...] = jnp.concatenate(rows + [zeros], 0).T
    taps_out[...] = turned[mine, :]
    turned[...] = jnp.broadcast_to(skip_ref[:, cols], (LANE, LANE)).T
    skip_out[...] = turned[mine, :]


def coefficients(taps, skip, depth):
    shape = jax.ShapeDtypeStruct((depth, LANE), jnp.float32)
    return pl.pallas_call(
        coef_kernel,
        out_shape=(shape, shape),
        scratch_shapes=[pltpu.VMEM((LANE, LANE), jnp.float32)],
        compiler_params=params(4),
    )(taps, skip[None, :])


def put_turned(out_ref, j, block):
    depth = out_ref.shape[2]
    per = LANE // depth
    for g in range(block.shape[1] // LANE):
        turned = block[:, g * LANE : (g + 1) * LANE].astype(out_ref.dtype).T
        out_ref[g * per : (g + 1) * per, j] = turned.reshape(per, depth, LANE)


def step_x(step, core):
    return jnp.where(core == 0, step, (X_SIZE - step) % X_SIZE)


def query_tiles(d):
    return {1: 1, 7: 2}.get(d, 0)


def pack_kernel(*refs):
    ins, outs, turned = refs[:Z_SIZE], refs[Z_SIZE:-1], refs[-1]
    last = X_SIZE * 2 * SLABS
    depth = ins[0].shape[1]
    edges = [in_ref[last].astype(jnp.float32) for in_ref in ins]
    zeros = jnp.zeros((LANE - Z_SIZE * depth, LANE), jnp.float32)
    turned[...] = jnp.concatenate(edges + [zeros], 0).T
    _, x, c = place()
    for d, out_ref in enumerate(outs):
        kx = step_x(d // 2, c)
        for kz, in_ref in enumerate(ins):
            out_ref[kz * SLABS : (kz + 1) * SLABS] = in_ref[pl.ds((kx * 2 + d % 2) * SLABS, SLABS)]
        at = ((x + kx) % X_SIZE * 2 + (c + d) % 2) * depth
        out_ref[Z_SIZE * SLABS] = turned[pl.ds(pl.multiple_of(at, depth), depth), :].astype(out_ref.dtype)
        for i in range(query_tiles(d)):
            out_ref[Z_SIZE * SLABS + 1 + i] = ins[i][last + 1]


def pack(parts):
    tile, dtype = parts[0].shape[1:], parts[0].dtype
    return pl.pallas_call(
        pack_kernel,
        out_shape=tuple(
            jax.ShapeDtypeStruct((Z_SIZE * SLABS + 1 + query_tiles(d), *tile), dtype) for d in range(X_SIZE * 2)
        ),
        scratch_shapes=[pltpu.VMEM((LANE, LANE), jnp.float32)],
        cost_estimate=cost(20),
        compiler_params=params(6),
    )(*parts)


def seq_index(z, x, c):
    return (z % Z_SIZE * X_SIZE + x % X_SIZE) * 2 + c % 2


def moved(block, target):
    places = [(z, x, c) for z in range(Z_SIZE) for x in range(X_SIZE) for c in range(2)]
    return lax.ppermute(block, "seq", [(seq_index(*p), seq_index(*target(*p))) for p in places])


def along_z(block, dz):
    return moved(block, lambda z, x, c: (z + dz, x, c))


def cross(block, step, dc):
    return moved(block, lambda z, x, c: (z, x + step * (1 - 2 * c), c + dc))


def spread(parts):
    parts = [parts[0]] + [along_z(parts[k], k) for k in range(1, Z_SIZE)]
    parts = pack(parts)
    return [parts[0]] + [cross(parts[d], d // 2, d % 2) for d in range(1, X_SIZE * 2)]


def taps_of(ext_ref, taps, start, size):
    return (
        taps[0:1, :] * ext_ref[start + 8 : start + 8 + size, :]
        + taps[1:2, :] * ext_ref[start + 7 : start + 7 + size, :]
        + taps[2:3, :] * ext_ref[start + 6 : start + 6 + size, :]
    )


def product_kernel(k_ref, v_ref, taps_ref, out_ref, k_ext, v_ext, out_buf, sem):
    slabs = k_ref.shape[0] // LANE
    copies = []

    def put(j, block):
        put_turned(out_buf, j, block)
        copies.append(send(out_buf.at[:, j], out_ref.at[:, j], sem.at[j]))

    zero = jnp.zeros((8, k_ref.shape[1]), jnp.float32)
    k_ext[0:8, :] = zero
    v_ext[0:8, :] = zero
    for j in range(slabs):
        rows, ext = slice(j * LANE, (j + 1) * LANE), slice(8 + j * LANE, 8 + (j + 1) * LANE)
        k_ext[ext, :] = k_ref[rows, :].astype(jnp.float32)
        v_ext[ext, :] = v_ref[rows, :].astype(jnp.float32)
        kf = taps_of(k_ext, taps_ref[1], j * LANE, LANE)
        vf = taps_of(v_ext, taps_ref[2], j * LANE, LANE)
        put(j, kf * vf)
    wait_all(copies)


def product(k, v, taps, groups):
    rows, width = k.shape
    ext = pltpu.VMEM((rows + 8, width), jnp.float32)
    slabs = rows // LANE
    shape = jax.ShapeDtypeStruct((groups, slabs, width // groups, LANE), k.dtype)
    return pl.pallas_call(
        product_kernel,
        in_specs=[VMEM] * 3,
        out_specs=HBM,
        out_shape=shape,
        scratch_shapes=[ext, ext, pltpu.VMEM(shape.shape, shape.dtype), pltpu.SemaphoreType.DMA((slabs,))],
        cost_estimate=cost(20),
        compiler_params=params(12),
    )(k, v, taps)


def gate_kernel(q_ref, core_ref, step_ref, taps_ref, out_ref, q_ext):
    rows, width = q_ref.shape
    z, x, c = place()
    at = Z_SIZE * SLABS + 1
    tiles = [core_ref[at], step_ref[at], step_ref[at + 1]]
    core, step, round_z = [t.astype(jnp.float32) for t in tiles]
    halo = jnp.where(c == 1, core, jnp.where(x > 0, step, jnp.where(z > 0, round_z, 0.0)))
    parts = width // LANE
    for r in range(2):
        for g in range(parts):
            i = r * parts + g
            q_ext[6 + r : 7 + r, g * LANE : (g + 1) * LANE] = halo[i : i + 1]
    q_ext[8 : 8 + rows, :] = q_ref[...].astype(jnp.float32)
    for j in range(rows // LANE):
        qf = taps_of(q_ext, taps_ref[0], j * LANE, LANE)
        out_ref[j * LANE : (j + 1) * LANE, :] = qf.astype(out_ref.dtype)


def gate(q, core, step, taps):
    rows, width = q.shape
    return pl.pallas_call(
        gate_kernel,
        out_shape=jax.ShapeDtypeStruct(q.shape, q.dtype),
        scratch_shapes=[pltpu.VMEM((rows + 8, width), jnp.float32)],
        compiler_params=params(8),
    )(q, core, step, taps)


def mix(table, data):
    return jnp.dot(table, data, preferred_element_type=jnp.float32)


def mend(u_wide, edges, taps):
    depth = taps.shape[0]
    rows = edges.shape[0] - depth
    lane = lax.broadcasted_iota(jnp.int32, (rows, LANE), 1)
    sources = rows // depth
    weights = jnp.broadcast_to(taps[...][None], (sources, depth, LANE)).reshape(rows, LANE)
    terms = jnp.where(lane < 8, edges[depth:, :], edges[:rows, :]) * weights

    def after(x, steps):
        return pltpu.roll(x, LANE - steps, 1)

    terms = terms + after(terms, 2)
    terms = terms + after(terms, 8)
    fixed = (terms * after(terms, 4)).astype(jnp.bfloat16).astype(jnp.float32)
    size = u_wide.shape[0] // sources
    for i in range(sources):
        part, at = slice(i * depth, (i + 1) * depth), slice(i * size, i * size + depth)
        u_wide[at, :] = jnp.where(lane[part] < 2, fixed[part], u_wide[at, :])


def conv_kernel(u_ref, after_ref, taps_ref, skip_ref, t1, t2, t2_inv, t1_inv, tw_c, tw_s, *rest):
    f_refs, (y_ref, u_wide, f_wide, y_wide, edges) = rest[:-5], rest[-5:]
    depth = skip_ref.shape[0]
    edges[:depth, :] = jnp.zeros((depth, LANE), jnp.float32)
    z, x, c = place()
    sources = u_ref.shape[0]
    size = u_wide.shape[0] // sources
    for i in range(sources):
        u_wide[i * size : (i + 1) * size, :] = u_ref[i].astype(jnp.float32).reshape(size, LANE)
    for d, f_ref in enumerate(f_refs):
        core = (c + d) % 2
        kx = step_x(d // 2, core)
        edge = f_ref[Z_SIZE * SLABS].astype(jnp.float32)
        for kz in range(Z_SIZE):
            src = ((z - kz + Z_SIZE) % Z_SIZE * X_SIZE + (x - kx + X_SIZE) % X_SIZE) * 2 + core
            row = pl.multiple_of(src * size, size)
            tiles = f_ref[kz * SLABS : (kz + 1) * SLABS].reshape(size, LANE)
            f_wide[pl.ds(row, size), :] = tiles.astype(jnp.float32)
            row = pl.multiple_of((src + 1) * depth, depth)
            edges[pl.ds(row, depth), :] = pltpu.roll(edge, LANE - kz * depth, 1) if kz else edge
    low = jnp.bfloat16

    def part(x, i):
        return x[:, i * LANE : (i + 1) * LANE]

    def spectra(wide, rows):
        data = [wide[r, :].astype(low) for r in rows]
        first = mix(t1[...], jnp.concatenate(data, 1))
        turned = []
        for i in range(len(rows)):
            re, im = part(first[:LANE], i), part(first[LANE:], i)
            c, s = tw_c[...], tw_s[...]
            turned.append(jnp.concatenate([re * c - im * s, re * s + im * c], 1).astype(low))
        return mix(jnp.concatenate(turned, 0), t2[...])

    for start in range(0, depth, GROUP):
        rows = [pl.ds(ch, LANE, stride=depth) for ch in range(start, start + GROUP)]
        f_spec = spectra(f_wide, rows)
        if start == 0:
            mend(u_wide, edges, taps_ref)
        u_spec = spectra(u_wide, rows)
        prod = []
        for i in range(GROUP):
            a, b = u_spec[i * LANE : (i + 1) * LANE], f_spec[i * LANE : (i + 1) * LANE]
            ar, ai, br, bi = a[:, :LANE], a[:, LANE:], b[:, :LANE], b[:, LANE:]
            prod.append(jnp.concatenate([ar * br - ai * bi, ar * bi + ai * br], 1).astype(low))
        back = mix(jnp.concatenate(prod, 0), t2_inv[...])
        cols = []
        for i in range(GROUP):
            v = back[i * LANE : (i + 1) * LANE]
            re, im = v[:, :LANE], v[:, LANE:]
            c, s = tw_c[...], tw_s[...]
            cols.append(jnp.concatenate([re * c + im * s, im * c - re * s], 0).astype(low))
        conv = mix(t1_inv[...], jnp.concatenate(cols, 1))
        for i, r in enumerate(rows):
            y_wide[r, :] = part(conv, i)
    shape = (LANE, depth, LANE)
    y = y_wide[...].reshape(shape) + skip_ref[...][None] * u_wide[...].reshape(shape)
    y_ref[...] = y.reshape(y_ref.shape).astype(y_ref.dtype)


def long_conv(u, f, after, taps, skip):
    sources, slabs, depth, _ = u.shape
    flat = (sources * slabs * depth, LANE)
    wide = pltpu.VMEM(flat, jnp.float32)
    edges = pltpu.VMEM(((sources + 1) * depth, LANE), jnp.float32)
    operands = (u, after, taps, skip, *tables(), *f)
    y = pl.pallas_call(
        conv_kernel,
        in_specs=[HBM if x is after else VMEM for x in operands],
        out_shape=jax.ShapeDtypeStruct(flat, u.dtype),
        scratch_shapes=[wide] * 3 + [edges],
        compiler_params=params(40),
    )(*operands)
    return y.reshape(sources, slabs, depth, LANE)


def join_kernel(y_ref, qf_ref, stream_ref, gain_ref, out_ref, sum_ref, sq_ref):
    groups, slabs, depth, _ = y_ref.shape
    per = LANE // depth
    sq_ref[...] = jnp.zeros_like(sq_ref)
    for j in range(slabs):
        rows = slice(j * LANE, (j + 1) * LANE)
        squares = jnp.zeros((LANE, LANE), jnp.float32)
        for g in range(groups // per):
            cols = slice(g * LANE, (g + 1) * LANE)
            y = y_ref[g * per : (g + 1) * per, j].reshape(LANE, LANE).T.astype(jnp.float32)
            gated = (qf_ref[rows, cols].astype(jnp.float32) * y).astype(jnp.bfloat16)
            summed = stream_ref[rows, cols].astype(jnp.float32) + gated.astype(jnp.float32)
            out_ref[rows, cols] = summed.astype(out_ref.dtype)
            sum_ref[rows, cols] = summed * gain_ref[:, cols]
            squares = squares + summed * summed
        total = jnp.sum(squares.T, axis=0, keepdims=True)
        sq_ref[j : j + 1, :] = total


def join(y, qf, stream, gain):
    return pl.pallas_call(
        join_kernel,
        in_specs=[VMEM] * 4,
        out_shape=(
            jax.ShapeDtypeStruct(stream.shape, stream.dtype),
            jax.ShapeDtypeStruct(stream.shape, jnp.float32),
            jax.ShapeDtypeStruct((8, LANE), jnp.float32),
        ),
        compiler_params=params(12),
    )(y, qf, stream, gain[None, :])


def norm_kernel(channels, low_ref, sum_ref, *rest):
    sq_refs, (low_out, out_ref, out_buf, low_sem, sem) = rest[:-5], rest[-5:]
    copies = [send(low_ref, low_out, low_sem)]
    squares = sum(ref[...] for ref in sq_refs)
    scale = 1.0 / jnp.sqrt(squares / channels + 1e-05)
    for j in range(out_ref.shape[0] // LANE):
        rows = slice(j * LANE, (j + 1) * LANE)
        column = jnp.broadcast_to(scale[j : j + 1, :], (LANE, LANE)).T
        for g in range(out_ref.shape[1] // LANE):
            cols = slice(g * LANE, (g + 1) * LANE)
            out_buf[rows, cols] = (sum_ref[rows, cols] * column).astype(out_buf.dtype)
        copies.append(send(out_buf.at[rows, :], out_ref.at[rows, :], sem.at[j]))
    wait_all(copies)


def norm(low, summed, squares, channels):

    def kernel(*refs):
        norm_kernel(channels, *refs)

    return pl.pallas_call(
        kernel,
        in_specs=[VMEM] * (2 + len(squares)),
        out_specs=(HBM,) * 2,
        out_shape=(jax.ShapeDtypeStruct(summed.shape, low.dtype),) * 2,
        scratch_shapes=[
            pltpu.VMEM(summed.shape, low.dtype),
            pltpu.SemaphoreType.DMA,
            pltpu.SemaphoreType.DMA((summed.shape[0] // LANE,)),
        ],
        compiler_params=params(8),
    )(low, summed, *squares)


def exchange(x, axis):
    return lax.all_to_all(x, axis, split_axis=0, concat_axis=0, tiled=True)


def across(block, fan, dz, dy):
    route = [(i, (i + dz) % fan // Y_SIZE * Y_SIZE + (i + dy) % Y_SIZE) for i in range(fan)]
    return lax.ppermute(block, "ch", route)


def shards(queries, keys, values, filters, short_weights, skip_gain, stream, norm_gain):
    groups = lax.axis_size("seq")
    fan = lax.axis_size("ch")
    rows, width = queries.shape
    slab = width // groups
    parts = lead(queries, keys, values, filters, groups)
    u_all = exchange(product(keys, values, short_weights, groups), "seq")
    f_all = spread(parts)
    taps, skip = coefficients(short_weights, skip_gain, slab)
    qf = gate(queries, f_all[1], f_all[7], short_weights)
    y_home = exchange(long_conv(u_all, f_all, qf, taps, skip), "seq")
    low, summed, squares = join(y_home, qf, stream, norm_gain)
    squares = squares + across(squares, fan, Y_SIZE, 0)
    squares = [squares] + [across(squares, fan, 0, k) for k in range(1, Y_SIZE)]
    return norm(low, summed, squares, width * fan)


def solution(mesh):
    wide = P("seq", "ch")
    in_specs = (wide, wide, wide, wide, P(None, None, "ch"), P("ch"), wide, P("ch"))
    return jax.shard_map(shards, mesh=mesh, in_specs=in_specs, out_specs=(wide, wide), check_vma=False)
```

```python
import jax
import jax.numpy as jnp
import numpy as np
from jax import lax
from jax.experimental import pallas as pl
from jax.experimental.pallas import tpu as pltpu
from jax.sharding import PartitionSpec as P

LANE = 128
EDGE = 16
GROUP = 16
Z_SIZE = 4
X_SIZE = 4
SLABS = 4
Y_SIZE = 4
MIB = 1024 * 1024


def params(mebibytes):
    return pltpu.CompilerParams(vmem_limit_bytes=mebibytes * MIB)


def cost(micros):
    return pl.CostEstimate(flops=int(micros * 1e9), bytes_accessed=0, transcendentals=0)


def tables():
    n = LANE * LANE
    a = np.arange(LANE, dtype=np.float64)
    first = -2.0 * np.pi * np.outer(a + 0.25, a) / LANE
    twist = -2.0 * np.pi * np.outer(a + 0.25, a) / n
    second = -2.0 * np.pi * np.outer(a, a) / LANE
    t1 = np.concatenate([np.cos(first), np.sin(first)], 0)
    cos2, sin2 = np.cos(second), np.sin(second)
    t2 = np.block([[cos2, sin2], [-sin2, cos2]])
    t2_inv = np.block([[cos2, -sin2], [sin2, cos2]])
    t1_inv = np.concatenate([np.cos(first).T, np.sin(first).T], 1) / n
    low = [jnp.asarray(t, jnp.bfloat16) for t in (t1, t2, t2_inv, t1_inv)]
    return (*low, jnp.asarray(np.cos(twist), jnp.float32), jnp.asarray(np.sin(twist), jnp.float32))


def place():
    me = lax.axis_index("seq")
    return me // (X_SIZE * 2), me // 2 % X_SIZE, me % 2


HBM = pl.BlockSpec(memory_space=pl.ANY)
VMEM = pl.BlockSpec(memory_space=pltpu.VMEM)


def send(source, target, sem):
    copy = pltpu.make_async_copy(source, target, sem)
    copy.start()
    return copy


def wait_all(copies):
    for copy in copies:
        copy.wait()


def edge_rows(first, last):
    zero = jnp.zeros_like(first[:1])
    own = [first[0:1], first[1:2], zero, first[0:1]]
    passed = [last[EDGE - 1 :], zero, last[EDGE - 2 : EDGE - 1], last[EDGE - 1 :]]
    return own, passed


def lead_kernel(q_ref, k_ref, v_ref, f_ref, *rest):
    outs, (f_buf, e_buf, f_sem, e_sem) = rest[:Z_SIZE], rest[Z_SIZE:]
    rows = f_ref.shape[0]
    head, tail = pl.ds(0, EDGE), pl.ds(rows - EDGE, EDGE)
    pieces = [pl.ds(j * LANE, LANE) for j in range(SLABS)]
    f_copies = [send(f_ref.at[p, :], f_buf.at[p, :], f_sem.at[j]) for j, p in enumerate(pieces)]
    sources = [k_ref.at[head, :], k_ref.at[tail, :], v_ref.at[head, :], v_ref.at[tail, :]]
    e_copies = [send(x, e_buf.at[i], e_sem.at[i]) for i, x in enumerate(sources + [q_ref.at[tail, :]])]
    z, x, c = place()
    depth = outs[0].shape[1]
    cols = [pl.ds(pl.multiple_of((z + kz) % Z_SIZE * LANE, LANE), LANE) for kz in range(Z_SIZE)]
    for j, p in enumerate(pieces):
        f_copies[j].wait()
        for kz, out_ref in enumerate(outs):
            turned = f_buf[p, cols[kz]].T
            for d in range(X_SIZE * 2):
                to = (d // 2 - x + X_SIZE) % X_SIZE * 2 + (d % 2 - c + 2) % 2
                out_ref[to * SLABS + j] = turned[d * depth : (d + 1) * depth]
    wait_all(e_copies)
    edge_at = X_SIZE * 2 * SLABS
    q_rows = e_buf[len(sources)].astype(jnp.float32)
    parts = [slice(g * LANE, (g + 1) * LANE) for g in range(q_rows.shape[1] // LANE)]
    q_list = [q_rows[r : r + 1, p] for r in (EDGE - 2, EDGE - 1) for p in parts]
    q_tile = jnp.concatenate(q_list + [jnp.zeros((EDGE - len(q_list), LANE), jnp.float32)], 0)
    for kz, out_ref in enumerate(outs):
        k0, k1, v0, v1 = [e_buf[i, :, cols[kz]].astype(jnp.float32) for i in range(len(sources))]
        own_k, next_k = edge_rows(k0, k1)
        own_v, next_v = edge_rows(v0, v1)
        edge = jnp.concatenate(own_k + own_v + next_k + next_v, 0)
        out_ref[edge_at] = edge.astype(out_ref.dtype)
        if kz < 2:
            out_ref[edge_at + 1] = q_tile.astype(out_ref.dtype)


def lead(q, k, v, f, groups):
    rows, width = f.shape
    tile = (width // groups, LANE)
    edge_at = X_SIZE * 2 * SLABS
    return pl.pallas_call(
        lead_kernel,
        in_specs=[HBM] * 4,
        out_shape=tuple(
            pltpu.VMEM((edge_at + (2 if kz < 2 else 1), *tile), f.dtype) for kz in range(Z_SIZE)
        ),
        scratch_shapes=[
            pltpu.VMEM((SLABS * LANE, width), f.dtype),
            pltpu.VMEM((5, EDGE, width), f.dtype),
            pltpu.SemaphoreType.DMA((SLABS,)),
            pltpu.SemaphoreType.DMA((5,)),
        ],
        cost_estimate=cost(10),
        compiler_params=params(60),
    )(q, k, v, f)


def coef_kernel(taps_ref, skip_ref, taps_out, skip_out, turned):
    depth = skip_out.shape[0]
    me = lax.axis_index("seq")
    per = LANE // depth
    cols = pl.ds(pl.multiple_of(me // per * LANE, LANE), LANE)
    k, v = taps_ref[1, :, cols], taps_ref[2, :, cols]

    def pairs(w, order):
        return [w[i : i + 1] for i in order for _ in range(2)]

    rows = pairs(k, (0, 1)) + pairs(v, (0, 1)) + pairs(k, (1, 2)) + pairs(v, (1, 2))
    zeros = jnp.zeros((LANE - len(rows), LANE), jnp.float32)
    mine = pl.ds(pl.multiple_of(me % per * depth, depth), depth)
    turned[...] = jnp.concatenate(rows + [zeros], 0).T
    taps_out[...] = turned[mine, :]
    turned[...] = jnp.broadcast_to(skip_ref[:, cols], (LANE, LANE)).T
    skip_out[...] = turned[mine, :]


def coefficients(taps, skip, depth):
    shape = jax.ShapeDtypeStruct((depth, LANE), jnp.float32)
    return pl.pallas_call(
        coef_kernel,
        out_shape=(shape, shape),
        scratch_shapes=[pltpu.VMEM((LANE, LANE), jnp.float32)],
        compiler_params=params(4),
    )(taps, skip[None, :])


def put_turned(out_ref, j, block):
    depth = out_ref.shape[2]
    per = LANE // depth
    for g in range(block.shape[1] // LANE):
        turned = block[:, g * LANE : (g + 1) * LANE].astype(out_ref.dtype).T
        out_ref[g * per : (g + 1) * per, j] = turned.reshape(per, depth, LANE)


def step_x(step, core):
    return jnp.where(core == 0, step, (X_SIZE - step) % X_SIZE)


def query_tiles(d):
    return {1: 1, 7: 2, 4: 0, 5: 0}.get(d, 1)


def pack_kernel(*refs):
    ins, outs, turned = refs[:Z_SIZE], refs[Z_SIZE:-1], refs[-1]
    last = X_SIZE * 2 * SLABS
    depth = ins[0].shape[1]
    edges = [in_ref[last].astype(jnp.float32) for in_ref in ins]
    zeros = jnp.zeros((LANE - Z_SIZE * depth, LANE), jnp.float32)
    turned[...] = jnp.concatenate(edges + [zeros], 0).T
    _, x, c = place()
    for d, out_ref in enumerate(outs):
        kx = step_x(d // 2, c)
        for kz, in_ref in enumerate(ins):
            out_ref[kz * SLABS : (kz + 1) * SLABS] = in_ref[pl.ds((kx * 2 + d % 2) * SLABS, SLABS)]
        at = ((x + kx) % X_SIZE * 2 + (c + d) % 2) * depth
        out_ref[Z_SIZE * SLABS] = turned[pl.ds(pl.multiple_of(at, depth), depth), :].astype(out_ref.dtype)
        for i in range(query_tiles(d)):
            out_ref[Z_SIZE * SLABS + 1 + i] = ins[i][last + 1]


def pack(parts):
    tile, dtype = parts[0].shape[1:], parts[0].dtype
    return pl.pallas_call(
        pack_kernel,
        out_shape=tuple(
            jax.ShapeDtypeStruct((Z_SIZE * SLABS + 1 + query_tiles(d), *tile), dtype) for d in range(X_SIZE * 2)
        ),
        scratch_shapes=[pltpu.VMEM((LANE, LANE), jnp.float32)],
        cost_estimate=cost(20),
        compiler_params=params(6),
    )(*parts)


def seq_index(z, x, c):
    return (z % Z_SIZE * X_SIZE + x % X_SIZE) * 2 + c % 2


def moved(block, target):
    places = [(z, x, c) for z in range(Z_SIZE) for x in range(X_SIZE) for c in range(2)]
    return lax.ppermute(block, "seq", [(seq_index(*p), seq_index(*target(*p))) for p in places])


def along_z(block, dz):
    return moved(block, lambda z, x, c: (z + dz, x, c))


def cross(block, step, dc):
    return moved(block, lambda z, x, c: (z, x + step * (1 - 2 * c), c + dc))


def spread(parts):
    parts = [parts[0]] + [along_z(parts[k], k) for k in range(1, Z_SIZE)]
    parts = pack(parts)
    return [parts[0]] + [cross(parts[d], d // 2, d % 2) for d in range(1, X_SIZE * 2)]


def taps_of(ext_ref, taps, start, size):
    return (
        taps[0:1, :] * ext_ref[start + 8 : start + 8 + size, :]
        + taps[1:2, :] * ext_ref[start + 7 : start + 7 + size, :]
        + taps[2:3, :] * ext_ref[start + 6 : start + 6 + size, :]
    )


def product_kernel(k_ref, v_ref, taps_ref, out_ref, k_ext, v_ext, out_buf, sem):
    slabs = k_ref.shape[0] // LANE
    copies = []

    def put(j, block):
        put_turned(out_buf, j, block)
        copies.append(send(out_buf.at[:, j], out_ref.at[:, j], sem.at[j]))

    zero = jnp.zeros((8, k_ref.shape[1]), jnp.float32)
    k_ext[0:8, :] = zero
    v_ext[0:8, :] = zero
    for j in range(slabs):
        rows, ext = slice(j * LANE, (j + 1) * LANE), slice(8 + j * LANE, 8 + (j + 1) * LANE)
        k_ext[ext, :] = k_ref[rows, :].astype(jnp.float32)
        v_ext[ext, :] = v_ref[rows, :].astype(jnp.float32)
        kf = taps_of(k_ext, taps_ref[1], j * LANE, LANE)
        vf = taps_of(v_ext, taps_ref[2], j * LANE, LANE)
        put(j, kf * vf)
    wait_all(copies)


def product(k, v, taps, groups):
    rows, width = k.shape
    ext = pltpu.VMEM((rows + 8, width), jnp.float32)
    slabs = rows // LANE
    shape = jax.ShapeDtypeStruct((groups, slabs, width // groups, LANE), k.dtype)
    return pl.pallas_call(
        product_kernel,
        in_specs=[VMEM] * 3,
        out_specs=HBM,
        out_shape=shape,
        scratch_shapes=[ext, ext, pltpu.VMEM(shape.shape, shape.dtype), pltpu.SemaphoreType.DMA((slabs,))],
        cost_estimate=cost(20),
        compiler_params=params(12),
    )(k, v, taps)


def gate_kernel(q_ref, core_ref, step_ref, taps_ref, out_ref, q_ext):
    rows, width = q_ref.shape
    z, x, c = place()
    at = Z_SIZE * SLABS + 1
    tiles = [core_ref[at], step_ref[at], step_ref[at + 1]]
    core, step, round_z = [t.astype(jnp.float32) for t in tiles]
    halo = jnp.where(c == 1, core, jnp.where(x > 0, step, jnp.where(z > 0, round_z, 0.0)))
    parts = width // LANE
    for r in range(2):
        for g in range(parts):
            i = r * parts + g
            q_ext[6 + r : 7 + r, g * LANE : (g + 1) * LANE] = halo[i : i + 1]
    q_ext[8 : 8 + rows, :] = q_ref[...].astype(jnp.float32)
    for j in range(rows // LANE):
        qf = taps_of(q_ext, taps_ref[0], j * LANE, LANE)
        out_ref[j * LANE : (j + 1) * LANE, :] = qf.astype(out_ref.dtype)


def gate(q, core, step, taps):
    rows, width = q.shape
    return pl.pallas_call(
        gate_kernel,
        out_shape=jax.ShapeDtypeStruct(q.shape, q.dtype),
        scratch_shapes=[pltpu.VMEM((rows + 8, width), jnp.float32)],
        compiler_params=params(8),
    )(q, core, step, taps)


def mix(table, data):
    return jnp.dot(table, data, preferred_element_type=jnp.float32)


def mend(u_wide, edges, taps):
    depth = taps.shape[0]
    rows = edges.shape[0] - depth
    lane = lax.broadcasted_iota(jnp.int32, (rows, LANE), 1)
    sources = rows // depth
    weights = jnp.broadcast_to(taps[...][None], (sources, depth, LANE)).reshape(rows, LANE)
    terms = jnp.where(lane < 8, edges[depth:, :], edges[:rows, :]) * weights

    def after(x, steps):
        return pltpu.roll(x, LANE - steps, 1)

    terms = terms + after(terms, 2)
    terms = terms + after(terms, 8)
    fixed = (terms * after(terms, 4)).astype(jnp.bfloat16).astype(jnp.float32)
    size = u_wide.shape[0] // sources
    for i in range(sources):
        part, at = slice(i * depth, (i + 1) * depth), slice(i * size, i * size + depth)
        u_wide[at, :] = jnp.where(lane[part] < 2, fixed[part], u_wide[at, :])


def conv_kernel(u_ref, after_ref, taps_ref, skip_ref, t1, t2, t2_inv, t1_inv, tw_c, tw_s, *rest):
    f_refs, (y_ref, u_wide, f_wide, y_wide, edges) = rest[:-5], rest[-5:]
    depth = skip_ref.shape[0]
    edges[:depth, :] = jnp.zeros((depth, LANE), jnp.float32)
    z, x, c = place()
    sources = u_ref.shape[0]
    size = u_wide.shape[0] // sources
    for i in range(sources):
        u_wide[i * size : (i + 1) * size, :] = u_ref[i].astype(jnp.float32).reshape(size, LANE)
    for d, f_ref in enumerate(f_refs):
        core = (c + d) % 2
        kx = step_x(d // 2, core)
        edge = f_ref[Z_SIZE * SLABS].astype(jnp.float32)
        for kz in range(Z_SIZE):
            src = ((z - kz + Z_SIZE) % Z_SIZE * X_SIZE + (x - kx + X_SIZE) % X_SIZE) * 2 + core
            row = pl.multiple_of(src * size, size)
            tiles = f_ref[kz * SLABS : (kz + 1) * SLABS].reshape(size, LANE)
            f_wide[pl.ds(row, size), :] = tiles.astype(jnp.float32)
            row = pl.multiple_of((src + 1) * depth, depth)
            edges[pl.ds(row, depth), :] = pltpu.roll(edge, LANE - kz * depth, 1) if kz else edge
    low = jnp.bfloat16

    def part(x, i):
        return x[:, i * LANE : (i + 1) * LANE]

    def spectra(wide, rows):
        data = [wide[r, :].astype(low) for r in rows]
        first = mix(t1[...], jnp.concatenate(data, 1))
        turned = []
        for i in range(len(rows)):
            re, im = part(first[:LANE], i), part(first[LANE:], i)
            c, s = tw_c[...], tw_s[...]
            turned.append(jnp.concatenate([re * c - im * s, re * s + im * c], 1).astype(low))
        return mix(jnp.concatenate(turned, 0), t2[...])

    for start in range(0, depth, GROUP):
        rows = [pl.ds(ch, LANE, stride=depth) for ch in range(start, start + GROUP)]
        f_spec = spectra(f_wide, rows)
        if start == 0:
            mend(u_wide, edges, taps_ref)
        u_spec = spectra(u_wide, rows)
        prod = []
        for i in range(GROUP):
            a, b = u_spec[i * LANE : (i + 1) * LANE], f_spec[i * LANE : (i + 1) * LANE]
            ar, ai, br, bi = a[:, :LANE], a[:, LANE:], b[:, :LANE], b[:, LANE:]
            prod.append(jnp.concatenate([ar * br - ai * bi, ar * bi + ai * br], 1).astype(low))
        back = mix(jnp.concatenate(prod, 0), t2_inv[...])
        cols = []
        for i in range(GROUP):
            v = back[i * LANE : (i + 1) * LANE]
            re, im = v[:, :LANE], v[:, LANE:]
            c, s = tw_c[...], tw_s[...]
            cols.append(jnp.concatenate([re * c + im * s, im * c - re * s], 0).astype(low))
        conv = mix(t1_inv[...], jnp.concatenate(cols, 1))
        for i, r in enumerate(rows):
            y_wide[r, :] = part(conv, i)
    shape = (LANE, depth, LANE)
    y = y_wide[...].reshape(shape) + skip_ref[...][None] * u_wide[...].reshape(shape)
    y_ref[...] = y.reshape(y_ref.shape).astype(y_ref.dtype)


def long_conv(u, f, after, taps, skip):
    sources, slabs, depth, _ = u.shape
    flat = (sources * slabs * depth, LANE)
    wide = pltpu.VMEM(flat, jnp.float32)
    edges = pltpu.VMEM(((sources + 1) * depth, LANE), jnp.float32)
    operands = (u, after, taps, skip, *tables(), *f)
    y = pl.pallas_call(
        conv_kernel,
        in_specs=[HBM if x is after else VMEM for x in operands],
        out_shape=jax.ShapeDtypeStruct(flat, u.dtype),
        scratch_shapes=[wide] * 3 + [edges],
        compiler_params=params(40),
    )(*operands)
    return y.reshape(sources, slabs, depth, LANE)


def join_kernel(y_ref, qf_ref, stream_ref, gain_ref, out_ref, sum_ref, sq_ref):
    groups, slabs, depth, _ = y_ref.shape
    per = LANE // depth
    sq_ref[...] = jnp.zeros_like(sq_ref)
    for j in range(slabs):
        rows = slice(j * LANE, (j + 1) * LANE)
        squares = jnp.zeros((LANE, LANE), jnp.float32)
        for g in range(groups // per):
            cols = slice(g * LANE, (g + 1) * LANE)
            y = y_ref[g * per : (g + 1) * per, j].reshape(LANE, LANE).T.astype(jnp.float32)
            gated = (qf_ref[rows, cols].astype(jnp.float32) * y).astype(jnp.bfloat16)
            summed = stream_ref[rows, cols].astype(jnp.float32) + gated.astype(jnp.float32)
            out_ref[rows, cols] = summed.astype(out_ref.dtype)
            sum_ref[rows, cols] = summed * gain_ref[:, cols]
            squares = squares + summed * summed
        total = jnp.sum(squares.T, axis=0, keepdims=True)
        sq_ref[j : j + 1, :] = total


def join(y, qf, stream, gain):
    return pl.pallas_call(
        join_kernel,
        in_specs=[VMEM] * 4,
        out_shape=(
            jax.ShapeDtypeStruct(stream.shape, stream.dtype),
            jax.ShapeDtypeStruct(stream.shape, jnp.float32),
            jax.ShapeDtypeStruct((8, LANE), jnp.float32),
        ),
        compiler_params=params(12),
    )(y, qf, stream, gain[None, :])


def norm_kernel(channels, low_ref, sum_ref, *rest):
    sq_refs, (low_out, out_ref, out_buf, low_sem, sem) = rest[:-5], rest[-5:]
    copies = [send(low_ref, low_out, low_sem)]
    squares = sum(ref[...] for ref in sq_refs)
    scale = 1.0 / jnp.sqrt(squares / channels + 1e-05)
    for j in range(out_ref.shape[0] // LANE):
        rows = slice(j * LANE, (j + 1) * LANE)
        column = jnp.broadcast_to(scale[j : j + 1, :], (LANE, LANE)).T
        for g in range(out_ref.shape[1] // LANE):
            cols = slice(g * LANE, (g + 1) * LANE)
            out_buf[rows, cols] = (sum_ref[rows, cols] * column).astype(out_buf.dtype)
        copies.append(send(out_buf.at[rows, :], out_ref.at[rows, :], sem.at[j]))
    wait_all(copies)


def norm(low, summed, squares, channels):

    def kernel(*refs):
        norm_kernel(channels, *refs)

    return pl.pallas_call(
        kernel,
        in_specs=[VMEM] * (2 + len(squares)),
        out_specs=(HBM,) * 2,
        out_shape=(jax.ShapeDtypeStruct(summed.shape, low.dtype),) * 2,
        scratch_shapes=[
            pltpu.VMEM(summed.shape, low.dtype),
            pltpu.SemaphoreType.DMA,
            pltpu.SemaphoreType.DMA((summed.shape[0] // LANE,)),
        ],
        compiler_params=params(8),
    )(low, summed, *squares)


def exchange(x, axis):
    return lax.all_to_all(x, axis, split_axis=0, concat_axis=0, tiled=True)


def across(block, fan, dz, dy):
    route = [(i, (i + dz) % fan // Y_SIZE * Y_SIZE + (i + dy) % Y_SIZE) for i in range(fan)]
    return lax.ppermute(block, "ch", route)


def shards(queries, keys, values, filters, short_weights, skip_gain, stream, norm_gain):
    groups = lax.axis_size("seq")
    fan = lax.axis_size("ch")
    rows, width = queries.shape
    slab = width // groups
    parts = lead(queries, keys, values, filters, groups)
    u_all = exchange(product(keys, values, short_weights, groups), "seq")
    f_all = spread(parts)
    taps, skip = coefficients(short_weights, skip_gain, slab)
    qf = gate(queries, f_all[1], f_all[7], short_weights)
    y_home = exchange(long_conv(u_all, f_all, qf, taps, skip), "seq")
    low, summed, squares = join(y_home, qf, stream, norm_gain)
    squares = squares + across(squares, fan, Y_SIZE, 0)
    squares = [squares] + [across(squares, fan, 0, k) for k in range(1, Y_SIZE)]
    return norm(low, summed, squares, width * fan)


def solution(mesh):
    wide = P("seq", "ch")
    in_specs = (wide, wide, wide, wide, P(None, None, "ch"), P("ch"), wide, P("ch"))
    return jax.shard_map(shards, mesh=mesh, in_specs=in_specs, out_specs=(wide, wide), check_vma=False)
```

```python
import jax
import jax.numpy as jnp
import numpy as np
from jax import lax
from jax.experimental import pallas as pl
from jax.experimental.pallas import tpu as pltpu
from jax.sharding import PartitionSpec as P

LANE = 128
EDGE = 16
GROUP = 16
Z_SIZE = 4
X_SIZE = 4
SLABS = 4
Y_SIZE = 4
MIB = 1024 * 1024


def params(mebibytes):
    return pltpu.CompilerParams(vmem_limit_bytes=mebibytes * MIB)


def cost(micros):
    return pl.CostEstimate(flops=int(micros * 1e9), bytes_accessed=0, transcendentals=0)


def tables():
    n = LANE * LANE
    a = np.arange(LANE, dtype=np.float64)
    first = -2.0 * np.pi * np.outer(a + 0.25, a) / LANE
    twist = -2.0 * np.pi * np.outer(a + 0.25, a) / n
    second = -2.0 * np.pi * np.outer(a, a) / LANE
    t1 = np.concatenate([np.cos(first), np.sin(first)], 0)
    cos2, sin2 = np.cos(second), np.sin(second)
    t2 = np.block([[cos2, sin2], [-sin2, cos2]])
    t2_inv = np.block([[cos2, -sin2], [sin2, cos2]])
    t1_inv = np.concatenate([np.cos(first).T, np.sin(first).T], 1) / n
    return [jnp.asarray(t, jnp.bfloat16) for t in (t1, t2, t2_inv, t1_inv, np.cos(twist), np.sin(twist))]


def place():
    me = lax.axis_index("seq")
    return me // (X_SIZE * 2), me // 2 % X_SIZE, me % 2


HBM = pl.BlockSpec(memory_space=pl.ANY)
VMEM = pl.BlockSpec(memory_space=pltpu.VMEM)


def send(source, target, sem):
    copy = pltpu.make_async_copy(source, target, sem)
    copy.start()
    return copy


def wait_all(copies):
    for copy in copies:
        copy.wait()


def edge_rows(first, last):
    zero = jnp.zeros_like(first[:1])
    own = [first[0:1], first[1:2], zero, first[0:1]]
    passed = [last[EDGE - 1 :], zero, last[EDGE - 2 : EDGE - 1], last[EDGE - 1 :]]
    return own, passed


def lead_kernel(q_ref, k_ref, v_ref, f_ref, *rest):
    outs, (f_buf, e_buf, f_sem, e_sem) = rest[:Z_SIZE], rest[Z_SIZE:]
    rows = f_ref.shape[0]
    head, tail = pl.ds(0, EDGE), pl.ds(rows - EDGE, EDGE)
    pieces = [pl.ds(j * LANE, LANE) for j in range(SLABS)]
    f_copies = [send(f_ref.at[p, :], f_buf.at[p, :], f_sem.at[j]) for j, p in enumerate(pieces)]
    sources = [k_ref.at[head, :], k_ref.at[tail, :], v_ref.at[head, :], v_ref.at[tail, :]]
    e_copies = [send(x, e_buf.at[i], e_sem.at[i]) for i, x in enumerate(sources + [q_ref.at[tail, :]])]
    z, x, c = place()
    depth = outs[0].shape[1]
    cols = [pl.ds(pl.multiple_of((z + kz) % Z_SIZE * LANE, LANE), LANE) for kz in range(Z_SIZE)]
    for j, p in enumerate(pieces):
        f_copies[j].wait()
        for kz, out_ref in enumerate(outs):
            turned = f_buf[p, cols[kz]].T
            for d in range(X_SIZE * 2):
                to = (d // 2 - x + X_SIZE) % X_SIZE * 2 + (d % 2 - c + 2) % 2
                out_ref[to * SLABS + j] = turned[d * depth : (d + 1) * depth]
    wait_all(e_copies)
    edge_at = X_SIZE * 2 * SLABS
    q_rows = e_buf[len(sources)].astype(jnp.float32)
    parts = [slice(g * LANE, (g + 1) * LANE) for g in range(q_rows.shape[1] // LANE)]
    q_list = [q_rows[r : r + 1, p] for r in (EDGE - 2, EDGE - 1) for p in parts]
    q_tile = jnp.concatenate(q_list + [jnp.zeros((EDGE - len(q_list), LANE), jnp.float32)], 0)
    for kz, out_ref in enumerate(outs):
        k0, k1, v0, v1 = [e_buf[i, :, cols[kz]].astype(jnp.float32) for i in range(len(sources))]
        own_k, next_k = edge_rows(k0, k1)
        own_v, next_v = edge_rows(v0, v1)
        edge = jnp.concatenate(own_k + own_v + next_k + next_v, 0)
        out_ref[edge_at] = edge.astype(out_ref.dtype)
        if kz < 2:
            out_ref[edge_at + 1] = q_tile.astype(out_ref.dtype)


def lead(q, k, v, f, groups):
    rows, width = f.shape
    tile = (width // groups, LANE)
    edge_at = X_SIZE * 2 * SLABS
    return pl.pallas_call(
        lead_kernel,
        in_specs=[HBM] * 4,
        out_shape=tuple(
            pltpu.VMEM((edge_at + (2 if kz < 2 else 1), *tile), f.dtype) for kz in range(Z_SIZE)
        ),
        scratch_shapes=[
            pltpu.VMEM((SLABS * LANE, width), f.dtype),
            pltpu.VMEM((5, EDGE, width), f.dtype),
            pltpu.SemaphoreType.DMA((SLABS,)),
            pltpu.SemaphoreType.DMA((5,)),
        ],
        cost_estimate=cost(10),
        compiler_params=params(60),
    )(q, k, v, f)


def coef_kernel(taps_ref, skip_ref, taps_out, skip_out, turned):
    depth = skip_out.shape[0]
    me = lax.axis_index("seq")
    per = LANE // depth
    cols = pl.ds(pl.multiple_of(me // per * LANE, LANE), LANE)
    k, v = taps_ref[1, :, cols], taps_ref[2, :, cols]

    def pairs(w, order):
        return [w[i : i + 1] for i in order for _ in range(2)]

    rows = pairs(k, (0, 1)) + pairs(v, (0, 1)) + pairs(k, (1, 2)) + pairs(v, (1, 2))
    zeros = jnp.zeros((LANE - len(rows), LANE), jnp.float32)
    mine = pl.ds(pl.multiple_of(me % per * depth, depth), depth)
    turned[...] = jnp.concatenate(rows + [zeros], 0).T
    taps_out[...] = turned[mine, :]
    turned[...] = jnp.broadcast_to(skip_ref[:, cols], (LANE, LANE)).T
    skip_out[...] = turned[mine, :]


def coefficients(taps, skip, depth):
    shape = jax.ShapeDtypeStruct((depth, LANE), jnp.float32)
    return pl.pallas_call(
        coef_kernel,
        out_shape=(shape, shape),
        scratch_shapes=[pltpu.VMEM((LANE, LANE), jnp.float32)],
        compiler_params=params(4),
    )(taps, skip[None, :])


def put_turned(out_ref, j, block):
    depth = out_ref.shape[2]
    per = LANE // depth
    for g in range(block.shape[1] // LANE):
        turned = block[:, g * LANE : (g + 1) * LANE].astype(out_ref.dtype).T
        out_ref[g * per : (g + 1) * per, j] = turned.reshape(per, depth, LANE)


def step_x(step, core):
    return jnp.where(core == 0, step, (X_SIZE - step) % X_SIZE)


def query_tiles(d):
    return {1: 1, 7: 2, 4: 0, 5: 0}.get(d, 1)


def pack_kernel(*refs):
    ins, outs, turned = refs[:Z_SIZE], refs[Z_SIZE:-1], refs[-1]
    last = X_SIZE * 2 * SLABS
    depth = ins[0].shape[1]
    edges = [in_ref[last].astype(jnp.float32) for in_ref in ins]
    zeros = jnp.zeros((LANE - Z_SIZE * depth, LANE), jnp.float32)
    turned[...] = jnp.concatenate(edges + [zeros], 0).T
    _, x, c = place()
    for d, out_ref in enumerate(outs):
        kx = step_x(d // 2, c)
        for kz, in_ref in enumerate(ins):
            out_ref[kz * SLABS : (kz + 1) * SLABS] = in_ref[pl.ds((kx * 2 + d % 2) * SLABS, SLABS)]
        at = ((x + kx) % X_SIZE * 2 + (c + d) % 2) * depth
        out_ref[Z_SIZE * SLABS] = turned[pl.ds(pl.multiple_of(at, depth), depth), :].astype(out_ref.dtype)
        for i in range(query_tiles(d)):
            out_ref[Z_SIZE * SLABS + 1 + i] = ins[i][last + 1]


def pack(parts):
    tile, dtype = parts[0].shape[1:], parts[0].dtype
    return pl.pallas_call(
        pack_kernel,
        out_shape=tuple(
            jax.ShapeDtypeStruct((Z_SIZE * SLABS + 1 + query_tiles(d), *tile), dtype) for d in range(X_SIZE * 2)
        ),
        scratch_shapes=[pltpu.VMEM((LANE, LANE), jnp.float32)],
        cost_estimate=cost(20),
        compiler_params=params(6),
    )(*parts)


def seq_index(z, x, c):
    return (z % Z_SIZE * X_SIZE + x % X_SIZE) * 2 + c % 2


def moved(block, target):
    places = [(z, x, c) for z in range(Z_SIZE) for x in range(X_SIZE) for c in range(2)]
    return lax.ppermute(block, "seq", [(seq_index(*p), seq_index(*target(*p))) for p in places])


def along_z(block, dz):
    return moved(block, lambda z, x, c: (z + dz, x, c))


def cross(block, step, dc):
    return moved(block, lambda z, x, c: (z, x + step * (1 - 2 * c), c + dc))


def spread(parts):
    parts = [parts[0]] + [along_z(parts[k], k) for k in range(1, Z_SIZE)]
    parts = pack(parts)
    return [parts[0]] + [cross(parts[d], d // 2, d % 2) for d in range(1, X_SIZE * 2)]


def taps_of(ext_ref, taps, start, size):
    return (
        taps[0:1, :] * ext_ref[start + 8 : start + 8 + size, :]
        + taps[1:2, :] * ext_ref[start + 7 : start + 7 + size, :]
        + taps[2:3, :] * ext_ref[start + 6 : start + 6 + size, :]
    )


def product_kernel(k_ref, v_ref, taps_ref, out_ref, k_ext, v_ext, out_buf, sem):
    slabs = k_ref.shape[0] // LANE
    copies = []

    def put(j, block):
        put_turned(out_buf, j, block)
        copies.append(send(out_buf.at[:, j], out_ref.at[:, j], sem.at[j]))

    zero = jnp.zeros((8, k_ref.shape[1]), jnp.float32)
    k_ext[0:8, :] = zero
    v_ext[0:8, :] = zero
    for j in range(slabs):
        rows, ext = slice(j * LANE, (j + 1) * LANE), slice(8 + j * LANE, 8 + (j + 1) * LANE)
        k_ext[ext, :] = k_ref[rows, :].astype(jnp.float32)
        v_ext[ext, :] = v_ref[rows, :].astype(jnp.float32)
        kf = taps_of(k_ext, taps_ref[1], j * LANE, LANE)
        vf = taps_of(v_ext, taps_ref[2], j * LANE, LANE)
        put(j, kf * vf)
    wait_all(copies)


def product(k, v, taps, groups):
    rows, width = k.shape
    ext = pltpu.VMEM((rows + 8, width), jnp.float32)
    slabs = rows // LANE
    shape = jax.ShapeDtypeStruct((groups, slabs, width // groups, LANE), k.dtype)
    return pl.pallas_call(
        product_kernel,
        in_specs=[VMEM] * 3,
        out_specs=HBM,
        out_shape=shape,
        scratch_shapes=[ext, ext, pltpu.VMEM(shape.shape, shape.dtype), pltpu.SemaphoreType.DMA((slabs,))],
        cost_estimate=cost(20),
        compiler_params=params(12),
    )(k, v, taps)


def gate_kernel(q_ref, core_ref, step_ref, taps_ref, out_ref, q_ext):
    rows, width = q_ref.shape
    z, x, c = place()
    at = Z_SIZE * SLABS + 1
    tiles = [core_ref[at], step_ref[at], step_ref[at + 1]]
    core, step, round_z = [t.astype(jnp.float32) for t in tiles]
    halo = jnp.where(c == 1, core, jnp.where(x > 0, step, jnp.where(z > 0, round_z, 0.0)))
    parts = width // LANE
    for r in range(2):
        for g in range(parts):
            i = r * parts + g
            q_ext[6 + r : 7 + r, g * LANE : (g + 1) * LANE] = halo[i : i + 1]
    q_ext[8 : 8 + rows, :] = q_ref[...].astype(jnp.float32)
    for j in range(rows // LANE):
        qf = taps_of(q_ext, taps_ref[0], j * LANE, LANE)
        out_ref[j * LANE : (j + 1) * LANE, :] = qf.astype(out_ref.dtype)


def gate(q, core, step, taps):
    rows, width = q.shape
    return pl.pallas_call(
        gate_kernel,
        out_shape=jax.ShapeDtypeStruct(q.shape, q.dtype),
        scratch_shapes=[pltpu.VMEM((rows + 8, width), jnp.float32)],
        compiler_params=params(8),
    )(q, core, step, taps)


def mix(table, data):
    return jnp.dot(table, data, preferred_element_type=jnp.float32)


def mend(u_wide, edges, taps):
    depth = taps.shape[0]
    rows = edges.shape[0] - depth
    lane = lax.broadcasted_iota(jnp.int32, (rows, LANE), 1)
    sources = rows // depth
    weights = jnp.broadcast_to(taps[...][None], (sources, depth, LANE)).reshape(rows, LANE)
    terms = jnp.where(lane < 8, edges[depth:, :], edges[:rows, :]) * weights

    def after(x, steps):
        return pltpu.roll(x, LANE - steps, 1)

    terms = terms + after(terms, 2)
    terms = terms + after(terms, 8)
    fixed = (terms * after(terms, 4)).astype(jnp.bfloat16).astype(jnp.float32)
    size = u_wide.shape[0] // sources
    for i in range(sources):
        part, at = slice(i * depth, (i + 1) * depth), slice(i * size, i * size + depth)
        u_wide[at, :] = jnp.where(lane[part] < 2, fixed[part], u_wide[at, :])


def conv_kernel(u_ref, after_ref, taps_ref, skip_ref, t1, t2, t2_inv, t1_inv, tw_c, tw_s, *rest):
    f_refs, (y_ref, u_wide, f_wide, y_wide, edges) = rest[:-5], rest[-5:]
    depth = skip_ref.shape[0]
    edges[:depth, :] = jnp.zeros((depth, LANE), jnp.float32)
    z, x, c = place()
    sources = u_ref.shape[0]
    size = u_wide.shape[0] // sources
    for i in range(sources):
        u_wide[i * size : (i + 1) * size, :] = u_ref[i].astype(jnp.float32).reshape(size, LANE)
    for d, f_ref in enumerate(f_refs):
        core = (c + d) % 2
        kx = step_x(d // 2, core)
        edge = f_ref[Z_SIZE * SLABS].astype(jnp.float32)
        for kz in range(Z_SIZE):
            src = ((z - kz + Z_SIZE) % Z_SIZE * X_SIZE + (x - kx + X_SIZE) % X_SIZE) * 2 + core
            row = pl.multiple_of(src * size, size)
            tiles = f_ref[kz * SLABS : (kz + 1) * SLABS].reshape(size, LANE)
            f_wide[pl.ds(row, size), :] = tiles.astype(jnp.float32)
            row = pl.multiple_of((src + 1) * depth, depth)
            edges[pl.ds(row, depth), :] = pltpu.roll(edge, LANE - kz * depth, 1) if kz else edge
    low = jnp.bfloat16

    def part(x, i):
        return x[:, i * LANE : (i + 1) * LANE]

    def spectra(wide, rows):
        data = [wide[r, :].astype(low) for r in rows]
        first = mix(t1[...], jnp.concatenate(data, 1))
        turned = []
        for i in range(len(rows)):
            re, im = part(first[:LANE], i).astype(low), part(first[LANE:], i).astype(low)
            c, s = tw_c[...], tw_s[...]
            turned.append(jnp.concatenate([re * c - im * s, re * s + im * c], 1))
        return mix(jnp.concatenate(turned, 0), t2[...])

    for start in range(0, depth, GROUP):
        rows = [pl.ds(ch, LANE, stride=depth) for ch in range(start, start + GROUP)]
        f_spec = spectra(f_wide, rows)
        if start == 0:
            mend(u_wide, edges, taps_ref)
        u_spec = spectra(u_wide, rows)
        prod = []
        for i in range(GROUP):
            a, b = u_spec[i * LANE : (i + 1) * LANE], f_spec[i * LANE : (i + 1) * LANE]
            ar, ai, br, bi = a[:, :LANE], a[:, LANE:], b[:, :LANE], b[:, LANE:]
            prod.append(jnp.concatenate([ar * br - ai * bi, ar * bi + ai * br], 1).astype(low))
        back = mix(jnp.concatenate(prod, 0), t2_inv[...])
        cols = []
        for i in range(GROUP):
            v = back[i * LANE : (i + 1) * LANE]
            re, im = v[:, :LANE].astype(low), v[:, LANE:].astype(low)
            c, s = tw_c[...], tw_s[...]
            cols.append(jnp.concatenate([re * c + im * s, im * c - re * s], 0))
        conv = mix(t1_inv[...], jnp.concatenate(cols, 1))
        for i, r in enumerate(rows):
            y_wide[r, :] = part(conv, i)
    shape = (LANE, depth, LANE)
    y = y_wide[...].reshape(shape) + skip_ref[...][None] * u_wide[...].reshape(shape)
    y_ref[...] = y.reshape(y_ref.shape).astype(y_ref.dtype)


def long_conv(u, f, after, taps, skip):
    sources, slabs, depth, _ = u.shape
    flat = (sources * slabs * depth, LANE)
    wide = pltpu.VMEM(flat, jnp.float32)
    edges = pltpu.VMEM(((sources + 1) * depth, LANE), jnp.float32)
    operands = (u, after, taps, skip, *tables(), *f)
    y = pl.pallas_call(
        conv_kernel,
        in_specs=[HBM if x is after else VMEM for x in operands],
        out_shape=jax.ShapeDtypeStruct(flat, u.dtype),
        scratch_shapes=[wide] * 3 + [edges],
        compiler_params=params(40),
    )(*operands)
    return y.reshape(sources, slabs, depth, LANE)


def join_kernel(y_ref, qf_ref, stream_ref, gain_ref, out_ref, sum_ref, sq_ref):
    groups, slabs, depth, _ = y_ref.shape
    per = LANE // depth
    sq_ref[...] = jnp.zeros_like(sq_ref)
    for j in range(slabs):
        rows = slice(j * LANE, (j + 1) * LANE)
        squares = jnp.zeros((LANE, LANE), jnp.float32)
        for g in range(groups // per):
            cols = slice(g * LANE, (g + 1) * LANE)
            y = y_ref[g * per : (g + 1) * per, j].reshape(LANE, LANE).T.astype(jnp.float32)
            gated = (qf_ref[rows, cols].astype(jnp.float32) * y).astype(jnp.bfloat16)
            summed = stream_ref[rows, cols].astype(jnp.float32) + gated.astype(jnp.float32)
            out_ref[rows, cols] = summed.astype(out_ref.dtype)
            sum_ref[rows, cols] = summed * gain_ref[:, cols]
            squares = squares + summed * summed
        total = jnp.sum(squares.T, axis=0, keepdims=True)
        sq_ref[j : j + 1, :] = total


def join(y, qf, stream, gain):
    return pl.pallas_call(
        join_kernel,
        in_specs=[VMEM] * 4,
        out_shape=(
            jax.ShapeDtypeStruct(stream.shape, stream.dtype),
            jax.ShapeDtypeStruct(stream.shape, jnp.float32),
            jax.ShapeDtypeStruct((8, LANE), jnp.float32),
        ),
        compiler_params=params(12),
    )(y, qf, stream, gain[None, :])


def norm_kernel(channels, low_ref, sum_ref, *rest):
    sq_refs, (low_out, out_ref, out_buf, low_sem, sem) = rest[:-5], rest[-5:]
    copies = [send(low_ref, low_out, low_sem)]
    squares = sum(ref[...] for ref in sq_refs)
    scale = 1.0 / jnp.sqrt(squares / channels + 1e-05)
    for j in range(out_ref.shape[0] // LANE):
        rows = slice(j * LANE, (j + 1) * LANE)
        column = jnp.broadcast_to(scale[j : j + 1, :], (LANE, LANE)).T
        for g in range(out_ref.shape[1] // LANE):
            cols = slice(g * LANE, (g + 1) * LANE)
            out_buf[rows, cols] = (sum_ref[rows, cols] * column).astype(out_buf.dtype)
        copies.append(send(out_buf.at[rows, :], out_ref.at[rows, :], sem.at[j]))
    wait_all(copies)


def norm(low, summed, squares, channels):

    def kernel(*refs):
        norm_kernel(channels, *refs)

    return pl.pallas_call(
        kernel,
        in_specs=[VMEM] * (2 + len(squares)),
        out_specs=(HBM,) * 2,
        out_shape=(jax.ShapeDtypeStruct(summed.shape, low.dtype),) * 2,
        scratch_shapes=[
            pltpu.VMEM(summed.shape, low.dtype),
            pltpu.SemaphoreType.DMA,
            pltpu.SemaphoreType.DMA((summed.shape[0] // LANE,)),
        ],
        compiler_params=params(8),
    )(low, summed, *squares)


def exchange(x, axis):
    return lax.all_to_all(x, axis, split_axis=0, concat_axis=0, tiled=True)


def across(block, fan, dz, dy):
    route = [(i, (i + dz) % fan // Y_SIZE * Y_SIZE + (i + dy) % Y_SIZE) for i in range(fan)]
    return lax.ppermute(block, "ch", route)


def shards(queries, keys, values, filters, short_weights, skip_gain, stream, norm_gain):
    groups = lax.axis_size("seq")
    fan = lax.axis_size("ch")
    rows, width = queries.shape
    slab = width // groups
    parts = lead(queries, keys, values, filters, groups)
    u_all = exchange(product(keys, values, short_weights, groups), "seq")
    f_all = spread(parts)
    taps, skip = coefficients(short_weights, skip_gain, slab)
    qf = gate(queries, f_all[1], f_all[7], short_weights)
    y_home = exchange(long_conv(u_all, f_all, qf, taps, skip), "seq")
    low, summed, squares = join(y_home, qf, stream, norm_gain)
    squares = squares + across(squares, fan, Y_SIZE, 0)
    squares = [squares] + [across(squares, fan, 0, k) for k in range(1, Y_SIZE)]
    return norm(low, summed, squares, width * fan)


def solution(mesh):
    wide = P("seq", "ch")
    in_specs = (wide, wide, wide, wide, P(None, None, "ch"), P("ch"), wide, P("ch"))
    return jax.shard_map(shards, mesh=mesh, in_specs=in_specs, out_specs=(wide, wide), check_vma=False)
```

```python
import jax
import jax.numpy as jnp
import numpy as np
from jax import lax
from jax.experimental import pallas as pl
from jax.experimental.pallas import tpu as pltpu
from jax.sharding import PartitionSpec as P

LANE = 128
EDGE = 16
GROUP = 16
Z_SIZE = 4
X_SIZE = 4
SLABS = 4
Y_SIZE = 4
MIB = 1024 * 1024


def params(mebibytes):
    return pltpu.CompilerParams(vmem_limit_bytes=mebibytes * MIB)


def cost(micros):
    return pl.CostEstimate(flops=int(micros * 1e9), bytes_accessed=0, transcendentals=0)


def tables():
    n = LANE * LANE
    a = np.arange(LANE, dtype=np.float64)
    first = -2.0 * np.pi * np.outer(a + 0.25, a) / LANE
    twist = -2.0 * np.pi * np.outer(a + 0.25, a) / n
    second = -2.0 * np.pi * np.outer(a, a) / LANE
    t1 = np.concatenate([np.cos(first), np.sin(first)], 0)
    cos2, sin2 = np.cos(second), np.sin(second)
    t2 = np.block([[cos2, sin2], [-sin2, cos2]])
    t2_inv = np.block([[cos2, -sin2], [sin2, cos2]])
    t1_inv = np.concatenate([np.cos(first).T, np.sin(first).T], 1) / n
    return [jnp.asarray(t, jnp.bfloat16) for t in (t1, t2, t2_inv, t1_inv, np.cos(twist), np.sin(twist))]


def place():
    me = lax.axis_index("seq")
    return me // (X_SIZE * 2), me // 2 % X_SIZE, me % 2


HBM = pl.BlockSpec(memory_space=pl.ANY)
VMEM = pl.BlockSpec(memory_space=pltpu.VMEM)


def send(source, target, sem):
    copy = pltpu.make_async_copy(source, target, sem)
    copy.start()
    return copy


def wait_all(copies):
    for copy in copies:
        copy.wait()


def edge_rows(first, last):
    zero = jnp.zeros_like(first[:1])
    own = [first[0:1], first[1:2], zero, first[0:1]]
    passed = [last[EDGE - 1 :], zero, last[EDGE - 2 : EDGE - 1], last[EDGE - 1 :]]
    return own, passed


def lead_kernel(q_ref, k_ref, v_ref, f_ref, *rest):
    outs, (f_buf, e_buf, f_sem, e_sem) = rest[:Z_SIZE], rest[Z_SIZE:]
    rows = f_ref.shape[0]
    head, tail = pl.ds(0, EDGE), pl.ds(rows - EDGE, EDGE)
    pieces = [pl.ds(j * LANE, LANE) for j in range(SLABS)]
    f_copies = [send(f_ref.at[p, :], f_buf.at[p, :], f_sem.at[j]) for j, p in enumerate(pieces)]
    sources = [k_ref.at[head, :], k_ref.at[tail, :], v_ref.at[head, :], v_ref.at[tail, :]]
    e_copies = [send(x, e_buf.at[i], e_sem.at[i]) for i, x in enumerate(sources + [q_ref.at[tail, :]])]
    z, x, c = place()
    depth = outs[0].shape[1]
    cols = [pl.ds(pl.multiple_of((z + kz) % Z_SIZE * LANE, LANE), LANE) for kz in range(Z_SIZE)]
    for j, p in enumerate(pieces):
        f_copies[j].wait()
        for kz, out_ref in enumerate(outs):
            turned = f_buf[p, cols[kz]].T
            for d in range(X_SIZE * 2):
                to = (d // 2 - x + X_SIZE) % X_SIZE * 2 + (d % 2 - c + 2) % 2
                out_ref[to * SLABS + j] = turned[d * depth : (d + 1) * depth]
    wait_all(e_copies)
    edge_at = X_SIZE * 2 * SLABS
    q_rows = e_buf[len(sources)].astype(jnp.float32)
    parts = [slice(g * LANE, (g + 1) * LANE) for g in range(q_rows.shape[1] // LANE)]
    q_list = [q_rows[r : r + 1, p] for r in (EDGE - 2, EDGE - 1) for p in parts]
    q_tile = jnp.concatenate(q_list + [jnp.zeros((EDGE - len(q_list), LANE), jnp.float32)], 0)
    for kz, out_ref in enumerate(outs):
        k0, k1, v0, v1 = [e_buf[i, :, cols[kz]].astype(jnp.float32) for i in range(len(sources))]
        own_k, next_k = edge_rows(k0, k1)
        own_v, next_v = edge_rows(v0, v1)
        edge = jnp.concatenate(own_k + own_v + next_k + next_v, 0)
        out_ref[edge_at] = edge.astype(out_ref.dtype)
        if kz < 2:
            out_ref[edge_at + 1] = q_tile.astype(out_ref.dtype)


def lead(q, k, v, f, groups):
    rows, width = f.shape
    tile = (width // groups, LANE)
    edge_at = X_SIZE * 2 * SLABS
    return pl.pallas_call(
        lead_kernel,
        in_specs=[HBM] * 4,
        out_shape=tuple(
            pltpu.VMEM((edge_at + (2 if kz < 2 else 1), *tile), f.dtype) for kz in range(Z_SIZE)
        ),
        scratch_shapes=[
            pltpu.VMEM((SLABS * LANE, width), f.dtype),
            pltpu.VMEM((5, EDGE, width), f.dtype),
            pltpu.SemaphoreType.DMA((SLABS,)),
            pltpu.SemaphoreType.DMA((5,)),
        ],
        cost_estimate=cost(10),
        compiler_params=params(60),
    )(q, k, v, f)


def coef_kernel(taps_ref, skip_ref, taps_out, skip_out, turned):
    depth = skip_out.shape[0]
    me = lax.axis_index("seq")
    per = LANE // depth
    cols = pl.ds(pl.multiple_of(me // per * LANE, LANE), LANE)
    k, v = taps_ref[1, :, cols], taps_ref[2, :, cols]

    def pairs(w, order):
        return [w[i : i + 1] for i in order for _ in range(2)]

    rows = pairs(k, (0, 1)) + pairs(v, (0, 1)) + pairs(k, (1, 2)) + pairs(v, (1, 2))
    zeros = jnp.zeros((LANE - len(rows), LANE), jnp.float32)
    mine = pl.ds(pl.multiple_of(me % per * depth, depth), depth)
    turned[...] = jnp.concatenate(rows + [zeros], 0).T
    taps_out[...] = turned[mine, :]
    turned[...] = jnp.broadcast_to(skip_ref[:, cols], (LANE, LANE)).T
    skip_out[...] = turned[mine, :]


def coefficients(taps, skip, depth):
    shape = jax.ShapeDtypeStruct((depth, LANE), jnp.float32)
    return pl.pallas_call(
        coef_kernel,
        out_shape=(shape, shape),
        scratch_shapes=[pltpu.VMEM((LANE, LANE), jnp.float32)],
        compiler_params=params(4),
    )(taps, skip[None, :])


def put_turned(out_ref, j, block):
    depth = out_ref.shape[2]
    per = LANE // depth
    for g in range(block.shape[1] // LANE):
        turned = block[:, g * LANE : (g + 1) * LANE].astype(out_ref.dtype).T
        out_ref[g * per : (g + 1) * per, j] = turned.reshape(per, depth, LANE)


def step_x(step, core):
    return jnp.where(core == 0, step, (X_SIZE - step) % X_SIZE)


def query_tiles(d):
    return {1: 1, 7: 2, 4: 0, 5: 0}.get(d, 1)


def pack_kernel(*refs):
    ins, outs, turned = refs[:Z_SIZE], refs[Z_SIZE:-1], refs[-1]
    last = X_SIZE * 2 * SLABS
    depth = ins[0].shape[1]
    edges = [in_ref[last].astype(jnp.float32) for in_ref in ins]
    zeros = jnp.zeros((LANE - Z_SIZE * depth, LANE), jnp.float32)
    turned[...] = jnp.concatenate(edges + [zeros], 0).T
    _, x, c = place()
    for d, out_ref in enumerate(outs):
        kx = step_x(d // 2, c)
        for kz, in_ref in enumerate(ins):
            out_ref[kz * SLABS : (kz + 1) * SLABS] = in_ref[pl.ds((kx * 2 + d % 2) * SLABS, SLABS)]
        at = ((x + kx) % X_SIZE * 2 + (c + d) % 2) * depth
        out_ref[Z_SIZE * SLABS] = turned[pl.ds(pl.multiple_of(at, depth), depth), :].astype(out_ref.dtype)
        for i in range(query_tiles(d)):
            out_ref[Z_SIZE * SLABS + 1 + i] = ins[i][last + 1]


def pack(parts):
    tile, dtype = parts[0].shape[1:], parts[0].dtype
    return pl.pallas_call(
        pack_kernel,
        out_shape=tuple(
            jax.ShapeDtypeStruct((Z_SIZE * SLABS + 1 + query_tiles(d), *tile), dtype) for d in range(X_SIZE * 2)
        ),
        scratch_shapes=[pltpu.VMEM((LANE, LANE), jnp.float32)],
        cost_estimate=cost(20),
        compiler_params=params(6),
    )(*parts)


def seq_index(z, x, c):
    return (z % Z_SIZE * X_SIZE + x % X_SIZE) * 2 + c % 2


def moved(block, target):
    places = [(z, x, c) for z in range(Z_SIZE) for x in range(X_SIZE) for c in range(2)]
    return lax.ppermute(block, "seq", [(seq_index(*p), seq_index(*target(*p))) for p in places])


def along_z(block, dz):
    return moved(block, lambda z, x, c: (z + dz, x, c))


def cross(block, step, dc):
    return moved(block, lambda z, x, c: (z, x + step * (1 - 2 * c), c + dc))


def spread(parts):
    parts = [parts[0]] + [along_z(parts[k], k) for k in range(1, Z_SIZE)]
    parts = pack(parts)
    return [parts[0]] + [cross(parts[d], d // 2, d % 2) for d in range(1, X_SIZE * 2)]


def taps_of(ext_ref, taps, start, size):
    return (
        taps[0:1, :] * ext_ref[start + 8 : start + 8 + size, :]
        + taps[1:2, :] * ext_ref[start + 7 : start + 7 + size, :]
        + taps[2:3, :] * ext_ref[start + 6 : start + 6 + size, :]
    )


def product_kernel(k_ref, v_ref, taps_ref, out_ref, k_ext, v_ext, out_buf, sem):
    slabs = k_ref.shape[0] // LANE
    copies = []

    def put(j, block):
        put_turned(out_buf, j, block)
        copies.append(send(out_buf.at[:, j], out_ref.at[:, j], sem.at[j]))

    zero = jnp.zeros((8, k_ref.shape[1]), jnp.float32)
    k_ext[0:8, :] = zero
    v_ext[0:8, :] = zero
    for j in range(slabs):
        rows, ext = slice(j * LANE, (j + 1) * LANE), slice(8 + j * LANE, 8 + (j + 1) * LANE)
        k_ext[ext, :] = k_ref[rows, :].astype(jnp.float32)
        v_ext[ext, :] = v_ref[rows, :].astype(jnp.float32)
        kf = taps_of(k_ext, taps_ref[1], j * LANE, LANE)
        vf = taps_of(v_ext, taps_ref[2], j * LANE, LANE)
        put(j, kf * vf)
    wait_all(copies)


def product(k, v, taps, groups):
    rows, width = k.shape
    ext = pltpu.VMEM((rows + 8, width), jnp.float32)
    slabs = rows // LANE
    shape = jax.ShapeDtypeStruct((groups, slabs, width // groups, LANE), k.dtype)
    return pl.pallas_call(
        product_kernel,
        in_specs=[VMEM] * 3,
        out_specs=HBM,
        out_shape=shape,
        scratch_shapes=[ext, ext, pltpu.VMEM(shape.shape, shape.dtype), pltpu.SemaphoreType.DMA((slabs,))],
        cost_estimate=cost(20),
        compiler_params=params(12),
    )(k, v, taps)


def gate_kernel(q_ref, core_ref, step_ref, taps_ref, out_ref, q_ext):
    rows, width = q_ref.shape
    z, x, c = place()
    at = Z_SIZE * SLABS + 1
    tiles = [core_ref[at], step_ref[at], step_ref[at + 1]]
    core, step, round_z = [t.astype(jnp.float32) for t in tiles]
    halo = jnp.where(c == 1, core, jnp.where(x > 0, step, jnp.where(z > 0, round_z, 0.0)))
    parts = width // LANE
    for r in range(2):
        for g in range(parts):
            i = r * parts + g
            q_ext[6 + r : 7 + r, g * LANE : (g + 1) * LANE] = halo[i : i + 1]
    q_ext[8 : 8 + rows, :] = q_ref[...].astype(jnp.float32)
    for j in range(rows // LANE):
        qf = taps_of(q_ext, taps_ref[0], j * LANE, LANE)
        out_ref[j * LANE : (j + 1) * LANE, :] = qf.astype(out_ref.dtype)


def gate(q, core, step, taps):
    rows, width = q.shape
    return pl.pallas_call(
        gate_kernel,
        out_shape=jax.ShapeDtypeStruct(q.shape, q.dtype),
        scratch_shapes=[pltpu.VMEM((rows + 8, width), jnp.float32)],
        compiler_params=params(8),
    )(q, core, step, taps)


def mix(table, data):
    return jnp.dot(table, data, preferred_element_type=jnp.float32)


def mend(u_wide, edges, taps):
    depth = taps.shape[0]
    rows = edges.shape[0] - depth
    lane = lax.broadcasted_iota(jnp.int32, (rows, LANE), 1)
    sources = rows // depth
    weights = jnp.broadcast_to(taps[...][None], (sources, depth, LANE)).reshape(rows, LANE)
    terms = jnp.where(lane < 8, edges[depth:, :], edges[:rows, :]) * weights

    def after(x, steps):
        return pltpu.roll(x, LANE - steps, 1)

    terms = terms + after(terms, 2)
    terms = terms + after(terms, 8)
    fixed = (terms * after(terms, 4)).astype(jnp.bfloat16).astype(jnp.float32)
    size = u_wide.shape[0] // sources
    for i in range(sources):
        part, at = slice(i * depth, (i + 1) * depth), slice(i * size, i * size + depth)
        u_wide[at, :] = jnp.where(lane[part] < 2, fixed[part], u_wide[at, :])


def conv_kernel(u_ref, after_ref, taps_ref, skip_ref, t1, t2, t2_inv, t1_inv, tw_c, tw_s, *rest):
    f_refs, (y_ref, u_wide, f_wide, y_wide, edges) = rest[:-5], rest[-5:]
    depth = skip_ref.shape[0]
    edges[:depth, :] = jnp.zeros((depth, LANE), jnp.float32)
    z, x, c = place()
    sources = u_ref.shape[0]
    size = u_wide.shape[0] // sources
    for i in range(sources):
        u_wide[i * size : (i + 1) * size, :] = u_ref[i].astype(jnp.float32).reshape(size, LANE)
    for d, f_ref in enumerate(f_refs):
        core = (c + d) % 2
        kx = step_x(d // 2, core)
        edge = f_ref[Z_SIZE * SLABS].astype(jnp.float32)
        for kz in range(Z_SIZE):
            src = ((z - kz + Z_SIZE) % Z_SIZE * X_SIZE + (x - kx + X_SIZE) % X_SIZE) * 2 + core
            row = pl.multiple_of(src * size, size)
            tiles = f_ref[kz * SLABS : (kz + 1) * SLABS].reshape(size, LANE)
            f_wide[pl.ds(row, size), :] = tiles.astype(jnp.float32)
            row = pl.multiple_of((src + 1) * depth, depth)
            edges[pl.ds(row, depth), :] = pltpu.roll(edge, LANE - kz * depth, 1) if kz else edge
    low = jnp.bfloat16

    def part(x, i):
        return x[:, i * LANE : (i + 1) * LANE]

    def spectra(wide, rows):
        data = [wide[r, :].astype(low) for r in rows]
        first = mix(t1[...], jnp.concatenate(data, 1))
        turned = []
        for i in range(len(rows)):
            re, im = part(first[:LANE], i).astype(low), part(first[LANE:], i).astype(low)
            c, s = tw_c[...], tw_s[...]
            turned.append(jnp.concatenate([re * c - im * s, re * s + im * c], 1))
        return mix(jnp.concatenate(turned, 0), t2[...])

    for start in range(0, depth, GROUP):
        rows = [pl.ds(ch, LANE, stride=depth) for ch in range(start, start + GROUP)]
        f_spec = spectra(f_wide, rows)
        if start == 0:
            mend(u_wide, edges, taps_ref)
        u_spec = spectra(u_wide, rows)
        prod = []
        for i in range(GROUP):
            a, b = u_spec[i * LANE : (i + 1) * LANE], f_spec[i * LANE : (i + 1) * LANE]
            ar, ai, br, bi = a[:, :LANE], a[:, LANE:], b[:, :LANE], b[:, LANE:]
            prod.append(jnp.concatenate([ar * br - ai * bi, ar * bi + ai * br], 1).astype(low))
        back = mix(jnp.concatenate(prod, 0), t2_inv[...])
        cols = []
        for i in range(GROUP):
            v = back[i * LANE : (i + 1) * LANE]
            re, im = v[:, :LANE].astype(low), v[:, LANE:].astype(low)
            c, s = tw_c[...], tw_s[...]
            cols.append(jnp.concatenate([re * c + im * s, im * c - re * s], 0))
        conv = mix(t1_inv[...], jnp.concatenate(cols, 1))
        for i, r in enumerate(rows):
            y_wide[r, :] = part(conv, i)
    shape = (LANE, depth, LANE)
    y = y_wide[...].reshape(shape) + skip_ref[...][None] * u_wide[...].reshape(shape)
    y_ref[...] = y.reshape(y_ref.shape).astype(y_ref.dtype)


def long_conv(u, f, after, taps, skip):
    sources, slabs, depth, _ = u.shape
    flat = (sources * slabs * depth, LANE)
    wide = pltpu.VMEM(flat, jnp.float32)
    edges = pltpu.VMEM(((sources + 1) * depth, LANE), jnp.float32)
    operands = (u, after, taps, skip, *tables(), *f)
    y = pl.pallas_call(
        conv_kernel,
        in_specs=[HBM if x is after else VMEM for x in operands],
        out_shape=jax.ShapeDtypeStruct(flat, u.dtype),
        scratch_shapes=[wide] * 3 + [edges],
        compiler_params=params(40),
    )(*operands)
    return y.reshape(sources, slabs, depth, LANE)


def join_kernel(y_ref, qf_ref, stream_ref, gain_ref, out_ref, sum_ref, sq_ref):
    groups, slabs, depth, _ = y_ref.shape
    per = LANE // depth
    for j in range(slabs):
        rows = slice(j * LANE, (j + 1) * LANE)
        squares = jnp.zeros((LANE, LANE), jnp.float32)
        for g in range(groups // per):
            cols = slice(g * LANE, (g + 1) * LANE)
            y = y_ref[g * per : (g + 1) * per, j].reshape(LANE, LANE).T.astype(jnp.float32)
            gated = (qf_ref[rows, cols].astype(jnp.float32) * y).astype(jnp.bfloat16)
            summed = stream_ref[rows, cols].astype(jnp.float32) + gated.astype(jnp.float32)
            out_ref[rows, cols] = summed.astype(out_ref.dtype)
            sum_ref[rows, cols] = summed * gain_ref[:, cols]
            squares = squares + summed * summed
        total = jnp.sum(squares.T, axis=0, keepdims=True)
        sq_ref[j : j + 1, :] = total


def join(y, qf, stream, gain):
    return pl.pallas_call(
        join_kernel,
        in_specs=[VMEM] * 4,
        out_shape=(
            jax.ShapeDtypeStruct(stream.shape, stream.dtype),
            jax.ShapeDtypeStruct(stream.shape, jnp.float32),
            jax.ShapeDtypeStruct((stream.shape[0] // LANE, LANE), jnp.float32),
        ),
        compiler_params=params(12),
    )(y, qf, stream, gain[None, :])


def norm_kernel(channels, low_ref, sum_ref, *rest):
    sq_refs, (low_out, out_ref, out_buf, low_sem, sem) = rest[:-5], rest[-5:]
    copies = [send(low_ref, low_out, low_sem)]
    squares = sum(ref[...] for ref in sq_refs)
    scale = 1.0 / jnp.sqrt(squares / channels + 1e-05)
    for j in range(out_ref.shape[0] // LANE):
        rows = slice(j * LANE, (j + 1) * LANE)
        column = jnp.broadcast_to(scale[j : j + 1, :], (LANE, LANE)).T
        for g in range(out_ref.shape[1] // LANE):
            cols = slice(g * LANE, (g + 1) * LANE)
            out_buf[rows, cols] = (sum_ref[rows, cols] * column).astype(out_buf.dtype)
        copies.append(send(out_buf.at[rows, :], out_ref.at[rows, :], sem.at[j]))
    wait_all(copies)


def norm(low, summed, squares, channels):

    def kernel(*refs):
        norm_kernel(channels, *refs)

    return pl.pallas_call(
        kernel,
        in_specs=[VMEM] * (2 + len(squares)),
        out_specs=(HBM,) * 2,
        out_shape=(jax.ShapeDtypeStruct(summed.shape, low.dtype),) * 2,
        scratch_shapes=[
            pltpu.VMEM(summed.shape, low.dtype),
            pltpu.SemaphoreType.DMA,
            pltpu.SemaphoreType.DMA((summed.shape[0] // LANE,)),
        ],
        compiler_params=params(8),
    )(low, summed, *squares)


def exchange(x, axis):
    return lax.all_to_all(x, axis, split_axis=0, concat_axis=0, tiled=True)


def across(block, fan, dz, dy):
    route = [(i, (i + dz) % fan // Y_SIZE * Y_SIZE + (i + dy) % Y_SIZE) for i in range(fan)]
    return lax.ppermute(block, "ch", route)


def shards(queries, keys, values, filters, short_weights, skip_gain, stream, norm_gain):
    groups = lax.axis_size("seq")
    fan = lax.axis_size("ch")
    rows, width = queries.shape
    slab = width // groups
    parts = lead(queries, keys, values, filters, groups)
    u_all = exchange(product(keys, values, short_weights, groups), "seq")
    f_all = spread(parts)
    taps, skip = coefficients(short_weights, skip_gain, slab)
    qf = gate(queries, f_all[1], f_all[7], short_weights)
    y_home = exchange(long_conv(u_all, f_all, qf, taps, skip), "seq")
    low, summed, squares = join(y_home, qf, stream, norm_gain)
    squares = squares + across(squares, fan, Y_SIZE, 0)
    squares = [squares] + [across(squares, fan, 0, k) for k in range(1, Y_SIZE)]
    return norm(low, summed, squares, width * fan)


def solution(mesh):
    wide = P("seq", "ch")
    in_specs = (wide, wide, wide, wide, P(None, None, "ch"), P("ch"), wide, P("ch"))
    return jax.shard_map(shards, mesh=mesh, in_specs=in_specs, out_specs=(wide, wide), check_vma=False)
```
